512 devices in a mesh: gx: 8 (over y_lo, core), gy: 8 (over y_hi, x), gz: 8 (over z).
Axes of the slice: x: 4, y: 8 (y_hi: 2, y_lo: 4; y = y_hi * 4 + y_lo), z: 8, core: 2. Of those that a mesh axis runs over, the one named last changes fastest.
Arguments:
- volume: bfloat16 [16, 32, 64, 1024], P(None, 'gx', 'gy', 'gz'), may hold values from -6 to 6
- enc_weight: bfloat16 [27, 16, 16], replicated, may hold values from -0.3125 to 0.3125
- coarse_weight: bfloat16 [27, 16, 32], replicated, may hold values from -0.3125 to 0.3125
- up_weight: bfloat16 [32, 16], replicated, may hold values from -1 to 1
- dec_weight: bfloat16 [27, 32, 16], replicated, may hold values from -0.21875 to 0.21875
- cotangent: bfloat16 [16, 32, 64, 1024], P(None, 'gx', 'gy', 'gz'), may hold values from -6 to 6
Outputs:
- decoded: bfloat16 [16, 32, 64, 1024], P(None, 'gx', 'gy', 'gz')
- volume_grad: bfloat16 [16, 32, 64, 1024], P(None, 'gx', 'gy', 'gz')
- enc_grad: float32 [27, 16, 16], replicated
- coarse_grad: float32 [27, 16, 32], replicated
- up_grad: float32 [32, 16], replicated
- dec_grad: float32 [27, 32, 16], replicated
The draws below stay inside these ranges and needn't reach their ends.
All inputs are finite; a program needn't handle non-finite values.
Results may differ from the reference program's by a relative error of at most 0.013.
Values may be sent and summed in bfloat16 or wider, within the bound.
A program may use at most 64 MiB of HBM per device.

```python
import jax
import jax.numpy as jnp
from jax import lax

FINE_CH = 16
COARSE_CH = 32
NX = 32
NY = 64
NZ = 1024


def block_scale(stream_key, extent, shards, smallest, top_value):
    level, own = 1.0, jax.random.fold_in(stream_key, 6)
    for dim, shards_of in shards:
        steps = jnp.exp(jax.random.uniform(jax.random.fold_in(own, dim), (shards_of,), jnp.float32, smallest / len(shards), top_value / len(shards)))
        level = level * jnp.repeat(steps, extent[dim] // shards_of).reshape([-1 if axis == dim else 1 for axis in range(len(extent))])
    return level


def centred(key, shape, spread, bound, shards=(), dtype=jnp.bfloat16):
    factor_of = block_scale(key, shape, shards, -0.22, 0.18) if shards else 1.0
    values = jax.random.normal(key, shape, jnp.float32) * spread * factor_of
    return jnp.minimum(jnp.maximum(values, -bound), bound).astype(dtype)


def setup_inputs(seed: int = 0) -> dict:
    splits = jax.random.split(jax.random.key(seed), 7)
    volume = centred(splits[0], (FINE_CH, NX, NY, NZ), 1.0, 6.0, ((1, 8), (2, 8), (3, 8)))
    enc_weight = centred(splits[1], (27, FINE_CH, FINE_CH), (27 * FINE_CH) ** -0.5, 0.3125)
    coarse_weight = centred(splits[2], (27, FINE_CH, COARSE_CH), (27 * FINE_CH) ** -0.5, 0.3125)
    up_weight = centred(splits[3], (COARSE_CH, FINE_CH), COARSE_CH ** -0.5, 1.0)
    dec_weight = centred(splits[4], (27, 2 * FINE_CH, FINE_CH), (54 * FINE_CH) ** -0.5, 0.21875)
    cotangent = centred(splits[5], (FINE_CH, NX, NY, NZ), 1.0, 6.0, ((1, 8), (2, 8), (3, 8)))
    return {"volume": volume, "enc_weight": enc_weight, "coarse_weight": coarse_weight, "up_weight": up_weight, "dec_weight": dec_weight, "cotangent": cotangent}


def conv_float(field, weight):
    inputs = weight.shape[1]
    outputs = weight.shape[2]
    kernel = weight.reshape(3, 3, 3, inputs, outputs).transpose(4, 3, 0, 1, 2)
    result = lax.conv_general_dilated(field[None], kernel, (1, 1, 1), 'SAME', dimension_numbers=('NCDHW', 'OIDHW', 'NCDHW'), precision=lax.Precision.HIGHEST)
    return result[0]

def silu_slope(value):
    sig = jax.nn.sigmoid(value)
    return sig * (1.0 + value * (1.0 - sig))

def block_sum(field):
    chans, depth, height, width = field.shape
    return field.reshape(chans, depth // 2, 2, height // 2, 2, width // 2, 2).sum(axis=(2, 4, 6))

def enlarge(field):
    return jnp.repeat(jnp.repeat(jnp.repeat(field, 2, axis=1), 2, axis=2), 2, axis=3)

def reference(volume, enc_weight, coarse_weight, up_weight, dec_weight, cotangent):
    f32 = jnp.float32
    vol_f = volume.astype(f32)
    enc_f = enc_weight.astype(f32)
    pre_enc, enc_back = jax.vjp(conv_float, vol_f, enc_f)
    skip = jax.nn.silu(pre_enc).astype(jnp.bfloat16)
    pooled = (block_sum(skip.astype(f32)) * 0.125).astype(jnp.bfloat16)
    pre_coarse, coarse_back = jax.vjp(conv_float, pooled.astype(f32), coarse_weight.astype(f32))
    coarse_act = jax.nn.silu(pre_coarse).astype(jnp.bfloat16)
    upper = jnp.einsum('io,ixyz->oxyz', up_weight.astype(f32), coarse_act.astype(f32), precision=lax.Precision.HIGHEST).astype(jnp.bfloat16)
    joined = jnp.concatenate([skip, enlarge(upper)], axis=0)
    decoded_f, dec_back = jax.vjp(conv_float, joined.astype(f32), dec_weight.astype(f32))
    decoded = decoded_f.astype(jnp.bfloat16)
    joined_grad, dec_grad = dec_back(cotangent.astype(f32))
    chans = volume.shape[0]
    upper_grad = block_sum(joined_grad[chans:]).astype(jnp.bfloat16)
    up_grad = jnp.einsum('ixyz,oxyz->io', coarse_act.astype(f32), upper_grad.astype(f32), precision=lax.Precision.HIGHEST)
    act_grad = jnp.einsum('io,oxyz->ixyz', up_weight.astype(f32), upper_grad.astype(f32), precision=lax.Precision.HIGHEST)
    coarse_pre_grad = (act_grad * silu_slope(pre_coarse)).astype(jnp.bfloat16)
    pooled_grad, coarse_grad = coarse_back(coarse_pre_grad.astype(f32))
    skip_grad = joined_grad[:chans] + enlarge(pooled_grad) * 0.125
    enc_pre_grad = (skip_grad * silu_slope(pre_enc)).astype(jnp.bfloat16)
    volume_grad, enc_grad = enc_back(enc_pre_grad.astype(f32))
    return (decoded, volume_grad.astype(jnp.bfloat16), enc_grad, coarse_grad, up_grad, dec_grad)
```

```python
import functools

import jax
import jax.numpy as jnp
from jax import lax
from jax.experimental import pallas as pl
from jax.experimental.pallas import tpu as pltpu
from jax.sharding import PartitionSpec as P

AXES = ("gx", "gy", "gz")
BF = jnp.bfloat16
F32 = jnp.float32
MESH = pl.DeviceIdType.MESH
DIRS = tuple((dx, dy) for dx in (-1, 0, 1) for dy in (-1, 0, 1) if (dx, dy) != (0, 0))


def dot(a, b):
    return jnp.dot(a, b, preferred_element_type=F32)


def dot_nt(a, b):
    return lax.dot_general(a, b, (((1,), (1,)), ((), ())), preferred_element_type=F32)


def all_of(*conds):
    total = None
    for c in conds:
        if c is not None:
            total = c if total is None else jnp.logical_and(total, c)
    return total


def span(step, size, halo):
    if step == 0:
        return (0, size), (halo, size)
    if step > 0:
        return (size - halo, halo), (0, halo)
    return (0, halo), (halo + size, halo)


def kernel(sizes, vol, cot, we, wd, wdb, wc, wcb, web, upt, up, dec_out, vg_out, sum_out,
           vt, ct, pk, lr, vs, cs, skip, slope, jg, ughi, uglo, ug, ps, act, uc, gs, js, eh, es,
           gr, rx, ry, rz, ag,
           vsend, vrecv, csend, crecv, zsend, zrecv, lsend, lrecv, usend, urecv, esend, erecv,
           asend, arecv):
    nx, ny, nz = sizes
    ix, iy, iz = (lax.axis_index(a) for a in AXES)
    depth, height, chans, width = vol.shape
    cd, ch = depth // 2, height // 2

    def exists(step, index, count):
        return None if step == 0 else (index + step < count if step > 0 else index + step >= 0)

    def at(dx, dy, dz=0):
        return (ix + dx, iy + dy, iz + dz)

    def guarded(cond, f):
        if cond is None:
            f()
        else:
            pl.when(cond)(f)

    sends = [all_of(exists(dx, ix, nx), exists(dy, iy, ny)) for dx, dy in DIRS]
    recvs = [all_of(exists(-dx, ix, nx), exists(-dy, iy, ny)) for dx, dy in DIRS]
    zsteps = (-1, 1)
    zsends = [exists(s, iz, nz) for s in zsteps]
    zrecvs = [exists(-s, iz, nz) for s in zsteps]

    for ref in (vt, ct, lr, uc, eh):
        ref[...] = jnp.zeros(ref.shape, ref.dtype)
    barrier = pltpu.get_barrier_semaphore()

    def greet(device):
        pl.semaphore_signal(barrier, inc=1, device_id=device, device_id_type=MESH)

    for k in range(1, nx):
        greet((lax.rem(ix + k, nx), iy, iz))
    for k in range(1, ny):
        greet((ix, lax.rem(iy + k, ny), iz))
    for k in range(1, nz):
        greet((ix, iy, lax.rem(iz + k, nz)))
    for (dx, dy), s in zip(DIRS, sends):
        if dx != 0 and dy != 0:
            guarded(s, lambda dx=dx, dy=dy: greet(at(dx, dy)))
    def both(index, count):
        return (jnp.where(index > 0, 1, 0) + jnp.where(index < count - 1, 1, 0)).astype(jnp.int32)

    pl.semaphore_wait(barrier, nx + ny + nz - 3 + both(ix, nx) * both(iy, ny))

    def exchange(src, src_at, dst, dst_at, send_sem, recv_sem):
        copies = []
        for d, (dx, dy) in enumerate(DIRS):
            copies.append(pltpu.make_async_remote_copy(
                src_ref=src.at[src_at(dx, dy)], dst_ref=dst.at[dst_at(dx, dy)],
                send_sem=send_sem.at[d], recv_sem=recv_sem.at[d],
                device_id=at(dx, dy), device_id_type=MESH))
        return copies

    def begin(copies, conds):
        for c, s in zip(copies, conds):
            guarded(s, c.start)

    def landed(copies, conds):
        for c, r in zip(copies, conds):
            guarded(r, c.wait_recv)

    def left(copies, conds):
        for c, s in zip(copies, conds):
            guarded(s, c.wait_send)

    def rim_src(halo, d0, h0, off):
        def f(dx, dy):
            (a, n), _ = span(dx, d0, halo)
            (b, m), _ = span(dy, h0, halo)
            return (pl.ds(a + off, n), pl.ds(b + off, m))
        return f

    def rim_dst(halo, d0, h0):
        def f(dx, dy):
            _, (a, n) = span(dx, d0, halo)
            _, (b, m) = span(dy, h0, halo)
            return (pl.ds(a, n), pl.ds(b, m))
        return f

    vcopies = exchange(vol, rim_src(3, depth, height, 0), vt, rim_dst(3, depth, height), vsend, vrecv)
    ccopies = exchange(cot, rim_src(1, depth, height, 0), ct, rim_dst(1, depth, height), csend, crecv)

    rows = lax.broadcasted_iota(jnp.int32, (width, width), 0)
    lanes = lax.broadcasted_iota(jnp.int32, (width, width), 1)
    for n, ref in enumerate((vol, cot)):
        total = jnp.zeros((depth * chans, width), F32)
        for y in range(height):
            pick = ((lanes == 8 * y + rows) & (rows < 8)) | ((lanes == 8 * y + rows - 56) & (rows >= 120))
            total = total + dot(ref[:, y].reshape(depth * chans, width), pick.astype(BF))
        pk[:, n] = total.astype(BF).reshape(depth, chans, width)
    zcopies = []
    for d, s in enumerate(zsteps):
        side = 0 if s > 0 else 1
        zcopies.append(pltpu.make_async_remote_copy(
            src_ref=pk, dst_ref=lr.at[1, pl.ds(3, depth), side],
            send_sem=zsend.at[d], recv_sem=zrecv.at[d],
            device_id=at(0, 0, s), device_id_type=MESH))
    begin(zcopies, zsends)
    begin(vcopies, sends)
    begin(ccopies, sends)
    vt[pl.ds(3, depth), pl.ds(3, height)] = vol[...]
    ct[pl.ds(1, depth), pl.ds(1, height)] = cot[...]
    landed(zcopies, zrecvs)

    def lr_src(dx, dy):
        (a, n), _ = span(dx, depth, 3)
        return (1, pl.ds(a + 3, n))

    def lr_dst(dx, dy):
        _, (a, n) = span(dx, depth, 3)
        return (1 - dy, pl.ds(a, n))

    lcopies = exchange(lr, lr_src, lr, lr_dst, lsend, lrecv)
    begin(lcopies, sends)
    landed(vcopies, recvs)
    landed(ccopies, recvs)
    landed(lcopies, recvs)

    def unpacked(tiles, dyi, yy, first, count, which):
        lo = (rows == 8 * yy + lanes - 56) & (lanes >= 120)
        hi = (rows == 8 * yy + lanes) & (lanes < 8)
        got = dot(lr[dyi, pl.ds(first, count), 0, which].reshape(count * chans, width), lo.astype(BF))
        got = got + dot(lr[dyi, pl.ds(first, count), 1, which].reshape(count * chans, width), hi.astype(BF))
        return jnp.concatenate([tiles.reshape(count * chans, width).astype(F32), got], axis=1)

    def shifted(wide, c):
        if c == 1:
            return wide
        return pltpu.roll(wide, 1 if c == 0 else wide.shape[1] - 1, 1)

    def fill_vol(y, _):
        wide = unpacked(vt[:, y], (y + 5) // 8, lax.rem(y + 5, 8), 0, depth + 6, 0)
        for c in range(3):
            vs[:, y, c] = shifted(wide, c).astype(BF).reshape(depth + 6, chans, 2 * width)

    lax.fori_loop(0, height + 6, fill_vol, None)

    def fill_cot(y, _):
        wide = unpacked(ct[:, y], (y + 7) // 8, lax.rem(y + 7, 8), 2, depth + 2, 1)
        for c in range(3):
            cs[:, y, c] = shifted(wide, c).astype(BF).reshape(depth + 2, chans, 2 * width)

    lax.fori_loop(0, height + 2, fill_cot, None)

    fine = lax.broadcasted_iota(jnp.int32, (1, 2 * width), 1)
    coarse = lax.broadcasted_iota(jnp.int32, (1, width), 1)
    low_ok = jnp.where(iz > 0, 1.0, 0.0).astype(F32)
    high_ok = jnp.where(iz < nz - 1, 1.0, 0.0).astype(F32)
    fine_mask = jnp.where(fine < width, 1.0, jnp.where(fine < 3 * width // 2, high_ok, low_ok))
    coarse_mask = jnp.where(coarse < width // 2, 1.0, jnp.where(coarse < 3 * width // 4, high_ok, low_ok))
    own_coarse = coarse < width // 2

    def conv_row(weight, planes, outs):
        m = weight.shape[0] // 3
        ys = [dot(weight, x) for x in planes]
        return [ys[p][:m] + ys[p + 1][m:2 * m] + ys[p + 2][2 * m:] for p in range(outs)]

    def enc_row(q, _):
        k = 9 * chans
        pre = conv_row(we[...], [vs[p, pl.ds(q, 3)].reshape(k, 2 * width) for p in range(depth + 6)], depth + 4)
        gq = iy * height + q - 2
        yok = jnp.where((gq >= 0) & (gq < ny * height), 1.0, 0.0).astype(F32)
        for p in range(depth + 4):
            t = pre[p]
            sig = 1.0 / (1.0 + jnp.exp(-t))
            ok = yok
            if p < 2:
                ok = ok * jnp.where(ix > 0, 1.0, 0.0).astype(F32)
            if p >= depth + 2:
                ok = ok * jnp.where(ix < nx - 1, 1.0, 0.0).astype(F32)
            skip[p, q] = (t * sig * (fine_mask * ok)).astype(BF)
            if 2 <= p < depth + 2:
                slope[p - 2, q] = sig * (1.0 + t * (1.0 - sig)) * fine_mask

    lax.fori_loop(0, height + 4, enc_row, None)

    pool = (lax.broadcasted_iota(jnp.int32, (2 * width, width), 0) // 2
            == lax.broadcasted_iota(jnp.int32, (2 * width, width), 1)).astype(BF)

    def pool_row(q, _):
        rows_in = skip[:, pl.ds(2 * q, 2)].reshape((depth + 4) * 2 * chans, 2 * width)
        half = dot(rows_in, pool).reshape(cd + 2, 4, chans, width)
        mean = ((half[:, 0] + half[:, 1] + half[:, 2] + half[:, 3]) * 0.125).astype(BF)
        wide = mean.astype(F32).reshape((cd + 2) * chans, width)
        for c in range(3):
            ps[:, q, c] = shifted(wide, c).astype(BF).reshape(cd + 2, chans, width)

    lax.fori_loop(0, ch + 2, pool_row, None)

    def joined_row(q, _):
        k = 9 * chans
        sums = [jnp.zeros((chans, 2 * width), F32) for _ in range(cd)]
        for e in range(2):
            r = 2 * q + e
            out = conv_row(wdb[...], [cs[p, pl.ds(r, 3)].reshape(k, 2 * width) for p in range(depth + 2)], depth)
            for p in range(depth):
                jg[p, r] = out[p][:chans]
                sums[p // 2] = sums[p // 2] + out[p][chans:]
        for p in range(cd):
            hi = sums[p].astype(BF)
            ughi[p, q] = hi
            uglo[p, q] = (sums[p] - hi.astype(F32)).astype(BF)

    lax.fori_loop(0, ch, joined_row, None)
    flat = (cd * ch * chans, 2 * width)
    grad = dot(ughi[...].reshape(flat), pool) + dot(uglo[...].reshape(flat), pool)
    ug[...] = grad.astype(BF).reshape(ug.shape)

    for q in range(ch):
        k = 9 * chans
        pre = conv_row(wc[...], [ps[p, q:q + 3].reshape(k, width) for p in range(cd + 2)], cd)
        for p in range(cd):
            t = pre[p]
            sig = 1.0 / (1.0 + jnp.exp(-t))
            a = (t * sig * coarse_mask).astype(BF)
            act[p, q] = a
            uc[1 + p, 1 + q, 0:chans] = dot(upt[...], a).astype(BF)
            back = dot(up[...], ug[p, q])
            uc[1 + p, 1 + q, chans:3 * chans] = (back * (sig * (1.0 + t * (1.0 - sig)) * coarse_mask)).astype(BF)

    ucopies = exchange(uc, rim_src(1, cd, ch, 1), uc, rim_dst(1, cd, ch), usend, urecv)
    begin(ucopies, sends)

    group16 = lax.broadcasted_iota(jnp.int32, (1, width), 1) // 16
    group32 = lax.broadcasted_iota(jnp.int32, (1, width), 1) // 32

    def tap_sums(block, step, groups, gid):
        out = []
        for b in range(3):
            total = jnp.zeros((step, width), F32)
            for q in range(groups):
                total = jnp.where(gid == q, block[(q + b) * step:(q + b + 1) * step], total)
            size = width // 2
            while size >= width // groups:
                total = total + pltpu.roll(total, size, 1)
                size //= 2
            out.append(total)
        return out

    def put(first, value):
        gr[pl.ds(first // 8, value.shape[0] // 8)] = value.reshape(value.shape[0] // 8, 8, width)

    tail = jnp.zeros((3 * chans, width), F32)
    step = 3 * chans
    taps = []
    masked = [jnp.where(own_coarse, uc[1 + p, 1:1 + ch, chans:3 * chans].reshape(2 * chans * ch, width), 0)
              for p in range(cd)]
    for a in range(3):
        block = sum(dot_nt(ps[p + a].reshape((ch + 2) * step, width), masked[p]) for p in range(cd))
        taps += tap_sums(block, step, ch, group32)
    for half in range(2):
        total = jnp.zeros((step, width), F32)
        for g in range(4):
            total = jnp.where(group32 == g, taps[4 * half + g], total)
        put(144 + 48 * half, total)
    tail = jnp.where(group32 == 2, taps[8], tail)
    up_total = jnp.zeros((2 * chans, width), F32)
    for p in range(cd):
        for q in range(ch):
            g = jnp.where(own_coarse, ug[p, q], 0)
            up_total = up_total + dot_nt(act[p, q], jnp.concatenate([g] * 8, axis=0))
    up_total = jnp.concatenate([up_total, jnp.zeros((chans, width), F32)], axis=0)
    tail = jnp.where(group16 == 3, up_total, tail)

    def fill_skip(y, _):
        wide = skip[1:depth + 3, y + 1].reshape((depth + 2) * chans, 2 * width).astype(F32)
        for c in range(3):
            part = shifted(wide, c)[:, :width]
            js[:, y, c, 0:chans] = part.astype(BF).reshape(depth + 2, chans, width)

    lax.fori_loop(0, height + 2, fill_skip, None)
    landed(ucopies, recvs)

    def fill_coarse(y, _):
        wide = uc[:, y, chans:3 * chans].reshape((cd + 2) * 2 * chans, width).astype(F32)
        for c in range(3):
            gs[:, y, c] = shifted(wide, c).astype(BF).reshape(cd + 2, 2 * chans, width)

    lax.fori_loop(0, ch + 2, fill_coarse, None)
    spread = (lax.broadcasted_iota(jnp.int32, (width, 2 * width), 1) // 2
              == lax.broadcasted_iota(jnp.int32, (width, 2 * width), 0)).astype(BF)

    def back_row(q, _):
        k = 18 * chans
        pg = conv_row(wcb[...], [gs[p, pl.ds(q, 3)].reshape(k, width) for p in range(cd + 2)], cd)
        for p in range(cd):
            v = pg[p] * 0.125
            hi = v.astype(BF)
            lo = (v - hi.astype(F32)).astype(BF)
            wide = dot(hi, spread) + dot(lo, spread)
            for e in range(2):
                for f in range(2):
                    g = (jg[2 * p + e, 2 * q + f] + wide) * slope[2 * p + e, 2 * q + f + 2]
                    eh[1 + 2 * p + e, 1 + 2 * q + f] = g.astype(BF)

    lax.fori_loop(0, ch, back_row, None)
    ecopies = exchange(eh, rim_src(1, depth, height, 1), eh, rim_dst(1, depth, height), esend, erecv)
    begin(ecopies, sends)

    low = lax.broadcasted_iota(jnp.int32, (width, width), 0)
    lane = lax.broadcasted_iota(jnp.int32, (width, width), 1)
    for c in range(3):
        source = lax.rem(lane + (c - 1) + 2 * width, 2 * width) // 2
        pick = (low == source).astype(BF)
        wide = dot(uc[:, :, 0:chans].reshape((cd + 2) * (ch + 2) * chans, width), pick)
        wide = wide.astype(BF).reshape(cd + 2, ch + 2, chans, width)
        for x in range(depth + 2):
            for y in range(height + 2):
                js[x, y, c, chans:2 * chans] = wide[(x + 1) // 2, (y + 1) // 2]

    def fine_taps(source, step, grads):
        taps = []
        for a in range(3):
            block = sum(dot_nt(source(a + p), grads[p]) for p in range(depth))
            taps += tap_sums(block, step, height, group16)
        total = jnp.zeros((step, width), F32)
        for g in range(8):
            total = jnp.where(group16 == g, taps[g], total)
        return total, taps[8]

    total, last = fine_taps(
        lambda x: js[x].reshape((height + 2) * 6 * chans, width), 6 * chans,
        [cot[p].reshape(height * chans, width) for p in range(depth)])
    put(48, total)
    tail = jnp.where(group16 == 1, last[:48], tail)
    tail = jnp.where(group16 == 2, last[48:], tail)
    total, last = fine_taps(
        lambda x: vs[x + 2, 2:height + 4, :, :, 0:width].reshape((height + 2) * 3 * chans, width), 3 * chans,
        [eh[1 + p, 1:1 + height, :, 0:width].reshape(height * chans, width) for p in range(depth)])
    put(0, total)
    tail = jnp.where(group16 == 0, last, tail)
    put(240, tail)
    used = 288 // 8
    if gr.shape[0] > used:
        gr[used:] = jnp.zeros((gr.shape[0] - used, 8, width), F32)

    per = gr.shape[0] // nx

    def ring(phase, axis, count, src_of, dst):
        me = (ix, iy, iz)[axis]
        out, got = [], []
        for k in range(1, count):
            to = lax.rem(me + k, count)
            frm = lax.rem(me - k + count, count)
            there = tuple(to if i == axis else v for i, v in enumerate((ix, iy, iz)))

            def copy(src, slot, there=there, k=k):
                return pltpu.make_async_remote_copy(
                    src_ref=src, dst_ref=dst(slot), send_sem=asend.at[phase, k - 1],
                    recv_sem=arecv.at[phase, k - 1], device_id=there, device_id_type=MESH)

            out.append(copy(src_of(to), me))
            got.append(copy(src_of(to), frm))
        for c in out:
            c.start()
        return out, got

    def arrived(copies):
        for c in copies[1]:
            c.wait_recv()

    first = ring(0, 0, nx, lambda to: gr.at[pl.ds(to * per, per)], lambda slot: rx.at[slot])
    rx[ix] = gr[pl.ds(ix * per, per)]

    def dec_row(q, _):
        k = 18 * chans
        out = conv_row(wd[...], [js[p, pl.ds(q, 3)].reshape(k, width) for p in range(depth + 2)], depth)
        for p in range(depth):
            dec_out[p, q] = out[p].astype(BF)

    lax.fori_loop(0, height // 2, dec_row, None)

    def summed(ref, count):
        total = ref[0]
        for k in range(1, count):
            total = total + ref[k]
        return total

    arrived(first)
    ry[iy] = summed(rx, nx)
    second = ring(1, 1, ny, lambda to: ry.at[iy], lambda slot: ry.at[slot])
    lax.fori_loop(height // 2, height, dec_row, None)
    landed(ecopies, recvs)

    def fill_enc(y, _):
        wide = eh[:, y].reshape((depth + 2) * chans, 2 * width).astype(F32)
        for c in range(3):
            part = shifted(wide, c)[:, :width]
            es[:, y, c] = part.astype(BF).reshape(depth + 2, chans, width)

    lax.fori_loop(0, height + 2, fill_enc, None)

    def vol_row(q, _):
        k = 9 * chans
        out = conv_row(web[...], [es[p, pl.ds(q, 3)].reshape(k, width) for p in range(depth + 2)], depth)
        for p in range(depth):
            vg_out[p, q] = out[p].astype(BF)

    arrived(second)
    rz[iz] = summed(ry, ny)
    third = ring(2, 2, nz, lambda to: rz.at[iz], lambda slot: rz.at[slot])
    lax.fori_loop(0, height // 2, vol_row, None)
    arrived(third)
    ag[ix] = summed(rz, nz)
    fourth = ring(3, 0, nx, lambda to: ag.at[ix], lambda slot: ag.at[slot])
    lax.fori_loop(height // 2, height, vol_row, None)
    arrived(fourth)
    sum_out[...] = ag[...].reshape(sum_out.shape)

    left(zcopies, zsends)
    for copies in (vcopies, ccopies, lcopies, ucopies, ecopies):
        left(copies, sends)
    for copies in (first, second, third, fourth):
        for c in copies[0]:
            c.wait_send()


def stacked(weight):
    k = 9 * weight.shape[1]
    return jnp.swapaxes(weight.reshape(3, k, weight.shape[2]), 1, 2).reshape(3 * weight.shape[2], k)


def flipped(weight):
    return jnp.transpose(weight[::-1], (0, 2, 1))


def per_device(sizes, volume, enc_weight, coarse_weight, up_weight, dec_weight, cotangent):
    nx, ny, nz = sizes
    chans, d, h, w = volume.shape
    cd, ch = d // 2, h // 2
    per = -(-36 // nx)
    vol = jnp.transpose(volume, (1, 2, 0, 3))
    cot = jnp.transpose(cotangent, (1, 2, 0, 3))
    operands = (
        vol, cot, stacked(enc_weight), stacked(dec_weight), stacked(flipped(dec_weight)),
        stacked(coarse_weight), stacked(flipped(coarse_weight)), stacked(flipped(enc_weight)),
        up_weight.T, up_weight)
    c2 = 2 * chans
    scratch = [
        ((d + 6, h + 6, chans, w), BF),
        ((d + 2, h + 2, chans, w), BF),
        ((d, 2, chans, w), BF),
        ((3, d + 6, 2, 2, chans, w), BF),
        ((d + 6, h + 6, 3, chans, 2 * w), BF),
        ((d + 2, h + 2, 3, chans, 2 * w), BF),
        ((d + 4, h + 4, chans, 2 * w), BF),
        ((d, h + 4, chans, 2 * w), F32),
        ((d, h, chans, 2 * w), F32),
        ((cd, ch, chans, 2 * w), BF),
        ((cd, ch, chans, 2 * w), BF),
        ((cd, ch, chans, w), BF),
        ((cd + 2, ch + 2, 3, chans, w), BF),
        ((cd, ch, c2, w), BF),
        ((cd + 2, ch + 2, 3 * chans, w), BF),
        ((cd + 2, ch + 2, 3, c2, w), BF),
        ((d + 2, h + 2, 3, c2, w), BF),
        ((d + 2, h + 2, chans, 2 * w), BF),
        ((d + 2, h + 2, 3, chans, w), BF),
        ((nx * per, 8, w), F32),
        ((nx, per, 8, w), F32),
        ((ny, per, 8, w), F32),
        ((nz, per, 8, w), F32),
        ((nx, per, 8, w), F32),
    ]
    dma = pltpu.SemaphoreType.DMA
    widest = max(sizes) - 1
    sems = [dma((8,))] * 4 + [dma((2,))] * 2 + [dma((8,))] * 6 + [dma((4, max(widest, 1)))] * 2
    vmem = pl.BlockSpec(memory_space=pltpu.VMEM)
    dec, vg, total = pl.pallas_call(
        functools.partial(kernel, sizes),
        out_shape=(
            jax.ShapeDtypeStruct((d, h, chans, w), BF),
            jax.ShapeDtypeStruct((d, h, chans, w), BF),
            jax.ShapeDtypeStruct((nx * per, 8, w), F32)),
        in_specs=[vmem] * len(operands),
        out_specs=(vmem,) * 3,
        scratch_shapes=[pltpu.VMEM(s, t) for s, t in scratch] + sems,
        compiler_params=pltpu.CompilerParams(
            collective_id=0, has_side_effects=True, vmem_limit_bytes=48 * 1024 * 1024),
    )(*operands)
    g = total.reshape(nx * per * 8, w)
    tail = g[240:288]
    enc = jnp.transpose(g[0:48].reshape(48, 8, 16), (1, 0, 2)).reshape(24, 16, 16)
    enc = jnp.concatenate([enc, tail[:, 0:16].reshape(3, 16, 16)], axis=0)
    decg = jnp.transpose(g[48:144].reshape(96, 8, 16), (1, 0, 2)).reshape(24, 32, 16)
    decl = jnp.concatenate([tail[:, 16:32], tail[:, 32:48]], axis=0).reshape(3, 32, 16)
    decg = jnp.concatenate([decg, decl], axis=0)
    coarse = jnp.transpose(g[144:240].reshape(2, 48, 4, 32), (0, 2, 1, 3)).reshape(24, 16, 32)
    coarse = jnp.concatenate([coarse, tail[:, 64:96].reshape(3, 16, 32)], axis=0)
    upg = tail[0:32, 48:64]
    return (jnp.transpose(dec, (2, 0, 1, 3)), jnp.transpose(vg, (2, 0, 1, 3)), enc, coarse, upg, decg)


def solution(mesh):
    sizes = tuple(mesh.shape[a] for a in AXES)
    spec = P(None, "gx", "gy", "gz")
    return jax.shard_map(
        functools.partial(per_device, sizes),
        mesh=mesh,
        in_specs=(spec, P(), P(), P(), P(), spec),
        out_specs=(spec, spec, P(), P(), P(), P()),
        check_vma=False,
    )
```

```python
import functools

import jax
import jax.numpy as jnp
from jax import lax
from jax.experimental import pallas as pl
from jax.experimental.pallas import tpu as pltpu
from jax.sharding import PartitionSpec as P

AXES = ("gx", "gy", "gz")
BF = jnp.bfloat16
F32 = jnp.float32
MESH = pl.DeviceIdType.MESH
DIRS = tuple((dx, dy) for dx in (-1, 0, 1) for dy in (-1, 0, 1) if (dx, dy) != (0, 0))


def dot(a, b):
    return jnp.dot(a, b, preferred_element_type=F32)


def dot_nt(a, b):
    return lax.dot_general(a, b, (((1,), (1,)), ((), ())), preferred_element_type=F32)


def all_of(*conds):
    total = None
    for c in conds:
        if c is not None:
            total = c if total is None else jnp.logical_and(total, c)
    return total


def span(step, size, halo):
    if step == 0:
        return (0, size), (halo, size)
    if step > 0:
        return (size - halo, halo), (0, halo)
    return (0, halo), (halo + size, halo)


def kernel(sizes, vc, we, wd, wdb, wc, wcb, web, upt, up, dec_out, vg_out, sum_out,
           vct, pk, er, vs, cs, skip, slope, jg, ughi, uglo, ug, ph, ps, act, uh, gh, gs, js, eh, es,
           gr, ar,
           vsend, vrecv, zsend, zrecv, psend, precv, gsend, grecv, usend, urecv, ssend, srecv, esend, erecv,
           asend, arecv):
    nx, ny, nz = sizes
    ix, iy, iz = (lax.axis_index(a) for a in AXES)
    depth, height, _, width = vc.shape
    chans = vc.shape[2] // 2
    cd, ch = depth // 2, height // 2

    def exists(step, index, count):
        return None if step == 0 else (index + step < count if step > 0 else index + step >= 0)

    def at(dx, dy, dz=0):
        return (ix + dx, iy + dy, iz + dz)

    def guarded(cond, f):
        if cond is None:
            f()
        else:
            pl.when(cond)(f)

    sends = [all_of(exists(dx, ix, nx), exists(dy, iy, ny)) for dx, dy in DIRS]
    recvs = [all_of(exists(-dx, ix, nx), exists(-dy, iy, ny)) for dx, dy in DIRS]
    ends = tuple((dx, dy, s) for s in (-1, 1) for dx in (-1, 0, 1) for dy in (-1, 0, 1))
    esends = [all_of(exists(dx, ix, nx), exists(dy, iy, ny), exists(dz, iz, nz)) for dx, dy, dz in ends]
    erecvs = [all_of(exists(-dx, ix, nx), exists(-dy, iy, ny), exists(-dz, iz, nz)) for dx, dy, dz in ends]

    for ref in (vct, er, skip, ph, uh, gh, eh):
        ref[...] = jnp.zeros(ref.shape, ref.dtype)
    barrier = pltpu.get_barrier_semaphore()

    def greet(device):
        pl.semaphore_signal(barrier, inc=1, device_id=device, device_id_type=MESH)

    for k in range(1, nx):
        greet((lax.rem(ix + k, nx), iy, iz))
    for k in range(1, ny):
        greet((ix, lax.rem(iy + k, ny), iz))
    for k in range(1, nz):
        greet((ix, iy, lax.rem(iz + k, nz)))
    for dx, dy, dz in [d + (0,) for d in DIRS] + list(ends):
        if (dx != 0) + (dy != 0) + (dz != 0) > 1:
            guarded(all_of(exists(dx, ix, nx), exists(dy, iy, ny), exists(dz, iz, nz)),
                    lambda dx=dx, dy=dy, dz=dz: greet(at(dx, dy, dz)))

    def both(index, count):
        return (jnp.where(index > 0, 1, 0) + jnp.where(index < count - 1, 1, 0)).astype(jnp.int32)

    bx, by, bz = both(ix, nx), both(iy, ny), both(iz, nz)
    pl.semaphore_wait(barrier, nx + ny + nz - 3 + bx * by + bx * bz + by * bz + bx * by * bz)

    def exchange(src, src_at, dst, dst_at, send_sem, recv_sem):
        copies = []
        for d, (dx, dy) in enumerate(DIRS):
            copies.append(pltpu.make_async_remote_copy(
                src_ref=src.at[src_at(dx, dy)], dst_ref=dst.at[dst_at(dx, dy)],
                send_sem=send_sem.at[d], recv_sem=recv_sem.at[d],
                device_id=at(dx, dy), device_id_type=MESH))
        return copies

    def begin(copies, conds):
        for c, s in zip(copies, conds):
            guarded(s, c.start)

    def landed(copies, conds):
        for c, r in zip(copies, conds):
            guarded(r, c.wait_recv)

    def left(copies, conds):
        for c, s in zip(copies, conds):
            guarded(s, c.wait_send)

    def rim_src(halo, d0, h0, off):
        def f(dx, dy):
            (a, n), _ = span(dx, d0, halo)
            (b, m), _ = span(dy, h0, halo)
            return (pl.ds(a + off, n), pl.ds(b + off, m))
        return f

    def rim_dst(halo, d0, h0):
        def f(dx, dy):
            _, (a, n) = span(dx, d0, halo)
            _, (b, m) = span(dy, h0, halo)
            return (pl.ds(a, n), pl.ds(b, m))
        return f

    vcopies = exchange(vc, rim_src(1, depth, height, 0), vct, rim_dst(1, depth, height), vsend, vrecv)
    begin(vcopies, sends)

    row = lax.broadcasted_iota(jnp.int32, (width, 2 * width), 0)
    lane = lax.broadcasted_iota(jnp.int32, (width, 2 * width), 1)
    total = jnp.zeros((depth * chans, 2 * width), F32)
    for n in range(2):
        for y in range(height):
            base = 64 * n + 8 * y
            pick = ((lane == base + row) & (row < 8)) | ((lane == width + base + row - 120) & (row >= 120))
            total = total + dot(vc[:, y, n * chans:(n + 1) * chans].reshape(depth * chans, width), pick.astype(BF))
    for side in range(2):
        pk[side] = total[:, side * width:(side + 1) * width].astype(BF).reshape(depth, chans, width)
    zcopies = []
    for d, (dx, dy, dz) in enumerate(ends):
        (a, n), (b, m) = span(dx, depth, 1)
        side = 1 if dz > 0 else 0
        zcopies.append(pltpu.make_async_remote_copy(
            src_ref=pk.at[side, pl.ds(a, n)], dst_ref=er.at[side, 1 - dy, pl.ds(b, m)],
            send_sem=zsend.at[d], recv_sem=zrecv.at[d],
            device_id=at(dx, dy, dz), device_id_type=MESH))
    begin(zcopies, esends)
    vct[pl.ds(1, depth), pl.ds(1, height)] = vc[...]
    landed(vcopies, recvs)
    landed(zcopies, erecvs)

    def shifted(wide, c):
        if c == 1:
            return wide
        return pltpu.roll(wide, 1 if c == 0 else wide.shape[1] - 1, 1)

    def fill_inputs(y, _):
        dyi, base = (y + 7) // 8, 8 * lax.rem(y + 7, 8)
        flat = ((depth + 2) * chans, width)
        kind, spot = lane // width, lax.rem(lane, width)
        source = base + 64 * kind + spot
        lo = (row == source - 120) & (spot >= 120)
        hi = (row == source) & (spot < 8)
        got = dot(er[1, dyi].reshape(flat), lo.astype(BF)) + dot(er[0, dyi].reshape(flat), hi.astype(BF))
        for n, ref in enumerate((vs, cs)):
            own = vct[:, y, n * chans:(n + 1) * chans].reshape(flat).astype(F32)
            wide = jnp.concatenate([own, got[:, n * width:(n + 1) * width]], axis=1)
            for c in range(3):
                ref[:, y, c] = shifted(wide, c).astype(BF).reshape(depth + 2, chans, 2 * width)

    lax.fori_loop(0, height + 2, fill_inputs, None)

    fine = lax.broadcasted_iota(jnp.int32, (1, 2 * width), 1)
    coarse = lax.broadcasted_iota(jnp.int32, (1, width), 1)
    low_ok = jnp.where(iz > 0, 1.0, 0.0).astype(F32)
    high_ok = jnp.where(iz < nz - 1, 1.0, 0.0).astype(F32)
    fine_mask = jnp.where(fine < width, 1.0, jnp.where(fine < 3 * width // 2, high_ok, low_ok))
    coarse_mask = jnp.where(coarse < width // 2, 1.0, jnp.where(coarse < 3 * width // 4, high_ok, low_ok))
    own_coarse = coarse < width // 2

    def conv_row(weight, planes, outs):
        m = weight.shape[0] // 3
        ys = [dot(weight, x) for x in planes]
        return [ys[p][:m] + ys[p + 1][m:2 * m] + ys[p + 2][2 * m:] for p in range(outs)]

    def enc_row(q, _):
        k = 9 * chans
        pre = conv_row(we[...], [vs[p, pl.ds(q, 3)].reshape(k, 2 * width) for p in range(depth + 2)], depth)
        for p in range(depth):
            t = pre[p]
            sig = 1.0 / (1.0 + jnp.exp(-t))
            skip[1 + p, 1 + q] = (t * sig * fine_mask).astype(BF)
            slope[p, q] = sig * (1.0 + t * (1.0 - sig)) * fine_mask

    lax.fori_loop(0, height, enc_row, None)

    pool = (lax.broadcasted_iota(jnp.int32, (2 * width, width), 0) // 2
            == lax.broadcasted_iota(jnp.int32, (2 * width, width), 1)).astype(BF)

    for q in range(ch):
        rows_in = skip[1:1 + depth, 1 + 2 * q:3 + 2 * q].reshape(depth * 2 * chans, 2 * width)
        half = dot(rows_in, pool).reshape(cd, 4, chans, width)
        ph[1:1 + cd, 1 + q] = ((half[:, 0] + half[:, 1] + half[:, 2] + half[:, 3]) * 0.125).astype(BF)
    pcopies = exchange(ph, rim_src(1, cd, ch, 1), ph, rim_dst(1, cd, ch), psend, precv)
    begin(pcopies, sends)

    def joined_row(q, _):
        k = 9 * chans
        sums = [jnp.zeros((chans, 2 * width), F32) for _ in range(cd)]
        for e in range(2):
            r = 2 * q + e
            out = conv_row(wdb[...], [cs[p, pl.ds(r, 3)].reshape(k, 2 * width) for p in range(depth + 2)], depth)
            for p in range(depth):
                jg[p, r] = out[p][:chans]
                sums[p // 2] = sums[p // 2] + out[p][chans:]
        for p in range(cd):
            hi = sums[p].astype(BF)
            ughi[p, q] = hi
            uglo[p, q] = (sums[p] - hi.astype(F32)).astype(BF)

    lax.fori_loop(0, ch, joined_row, None)
    flat = (cd * ch * chans, 2 * width)
    grad = dot(ughi[...].reshape(flat), pool) + dot(uglo[...].reshape(flat), pool)
    ug[...] = grad.astype(BF).reshape(ug.shape)

    landed(pcopies, recvs)

    def fill_pooled(q, _):
        wide = ph[:, q].reshape((cd + 2) * chans, width).astype(F32)
        for c in range(3):
            ps[:, q, c] = shifted(wide, c).astype(BF).reshape(cd + 2, chans, width)

    lax.fori_loop(0, ch + 2, fill_pooled, None)
    for q in range(ch):
        k = 9 * chans
        pre = conv_row(wc[...], [ps[p, q:q + 3].reshape(k, width) for p in range(cd + 2)], cd)
        for p in range(cd):
            t = pre[p]
            sig = 1.0 / (1.0 + jnp.exp(-t))
            a = (t * sig * coarse_mask).astype(BF)
            act[p, q] = a
            uh[1 + p, 1 + q] = dot(upt[...], a).astype(BF)
            back = dot(up[...], ug[p, q])
            gh[1 + p, 1 + q] = (back * (sig * (1.0 + t * (1.0 - sig)) * coarse_mask)).astype(BF)

    gcopies = exchange(gh, rim_src(1, cd, ch, 1), gh, rim_dst(1, cd, ch), gsend, grecv)
    begin(gcopies, sends)
    ucopies = exchange(uh, rim_src(1, cd, ch, 1), uh, rim_dst(1, cd, ch), usend, urecv)
    begin(ucopies, sends)
    scopies = exchange(skip, rim_src(1, depth, height, 1), skip, rim_dst(1, depth, height), ssend, srecv)
    begin(scopies, sends)

    group16 = lax.broadcasted_iota(jnp.int32, (1, width), 1) // 16
    group32 = lax.broadcasted_iota(jnp.int32, (1, width), 1) // 32

    def tap_sums(block, step, groups, gid):
        out = []
        for b in range(3):
            total = jnp.zeros((step, width), F32)
            for q in range(groups):
                total = jnp.where(gid == q, block[(q + b) * step:(q + b + 1) * step], total)
            size = width // 2
            while size >= width // groups:
                total = total + pltpu.roll(total, size, 1)
                size //= 2
            out.append(total)
        return out

    def put(first, value):
        part, tile = first // 96, first % 96 // 16
        gr[part, tile:tile + 3] = value.astype(BF).reshape(3, 16, width)

    tail = jnp.zeros((3 * chans, width), F32)
    step = 3 * chans
    taps = []
    masked = [jnp.where(own_coarse, gh[1 + p, 1:1 + ch].reshape(2 * chans * ch, width), 0)
              for p in range(cd)]
    for a in range(3):
        block = sum(dot_nt(ps[p + a].reshape((ch + 2) * step, width), masked[p]) for p in range(cd))
        taps += tap_sums(block, step, ch, group32)
    for half in range(2):
        total = jnp.zeros((step, width), F32)
        for g in range(4):
            total = jnp.where(group32 == g, taps[4 * half + g], total)
        put(144 + 48 * half, total)
    tail = jnp.where(group32 == 2, taps[8], tail)
    up_total = jnp.zeros((2 * chans, width), F32)
    for p in range(cd):
        for q in range(ch):
            g = jnp.where(own_coarse, ug[p, q], 0)
            up_total = up_total + dot_nt(act[p, q], jnp.concatenate([g] * 8, axis=0))
    up_total = jnp.concatenate([up_total, jnp.zeros((chans, width), F32)], axis=0)
    tail = jnp.where(group16 == 3, up_total, tail)

    def fill_skip(first, count, y):
        wide = skip[first:first + count, y].reshape(count * chans, 2 * width).astype(F32)
        for c in range(3):
            part = shifted(wide, c)[:, :width]
            js[first:first + count, y, c, 0:chans] = part.astype(BF).reshape(count, chans, width)

    lax.fori_loop(1, height + 1, lambda y, _: fill_skip(1, depth, y), None)
    landed(gcopies, recvs)

    def fill_coarse(y, _):
        wide = gh[:, y].reshape((cd + 2) * 2 * chans, width).astype(F32)
        for c in range(3):
            gs[:, y, c] = shifted(wide, c).astype(BF).reshape(cd + 2, 2 * chans, width)

    lax.fori_loop(0, ch + 2, fill_coarse, None)
    spread = (lax.broadcasted_iota(jnp.int32, (width, 2 * width), 1) // 2
              == lax.broadcasted_iota(jnp.int32, (width, 2 * width), 0)).astype(BF)

    def back_row(q, _):
        k = 18 * chans
        pg = conv_row(wcb[...], [gs[p, pl.ds(q, 3)].reshape(k, width) for p in range(cd + 2)], cd)
        for p in range(cd):
            v = pg[p] * 0.125
            hi = v.astype(BF)
            lo = (v - hi.astype(F32)).astype(BF)
            wide = dot(hi, spread) + dot(lo, spread)
            for e in range(2):
                for f in range(2):
                    g = (jg[2 * p + e, 2 * q + f] + wide) * slope[2 * p + e, 2 * q + f]
                    eh[1 + 2 * p + e, 1 + 2 * q + f] = g.astype(BF)

    lax.fori_loop(0, ch, back_row, None)
    ecopies = exchange(eh, rim_src(1, depth, height, 1), eh, rim_dst(1, depth, height), esend, erecv)
    begin(ecopies, sends)

    landed(ucopies, recvs)
    low = lax.broadcasted_iota(jnp.int32, (width, width), 0)
    lane = lax.broadcasted_iota(jnp.int32, (width, width), 1)
    for c in range(3):
        source = lax.rem(lane + (c - 1) + 2 * width, 2 * width) // 2
        pick = (low == source).astype(BF)
        wide = dot(uh[...].reshape((cd + 2) * (ch + 2) * chans, width), pick)
        wide = wide.astype(BF).reshape(cd + 2, ch + 2, chans, width)
        for x in range(depth + 2):
            for y in range(height + 2):
                js[x, y, c, chans:2 * chans] = wide[(x + 1) // 2, (y + 1) // 2]
    landed(scopies, recvs)
    for y in (0, height + 1):
        fill_skip(0, depth + 2, y)

    def fill_sides(y, _):
        fill_skip(0, 1, y)
        fill_skip(depth + 1, 1, y)

    lax.fori_loop(1, height + 1, fill_sides, None)

    def fine_taps(source, step, grads):
        taps = []
        for a in range(3):
            block = sum(dot_nt(source(a + p), grads[p]) for p in range(depth))
            taps += tap_sums(block, step, height, group16)
        total = jnp.zeros((step, width), F32)
        for g in range(8):
            total = jnp.where(group16 == g, taps[g], total)
        return total, taps[8]

    total, last = fine_taps(
        lambda x: js[x].reshape((height + 2) * 6 * chans, width), 6 * chans,
        [vc[p, :, chans:2 * chans].reshape(height * chans, width) for p in range(depth)])
    put(48, total[:48])
    put(96, total[48:])
    tail = jnp.where(group16 == 1, last[:48], tail)
    tail = jnp.where(group16 == 2, last[48:], tail)
    total, last = fine_taps(
        lambda x: vs[x, :, :, :, 0:width].reshape((height + 2) * 3 * chans, width), 3 * chans,
        [eh[1 + p, 1:1 + height, :, 0:width].reshape(height * chans, width) for p in range(depth)])
    put(0, total)
    tail = jnp.where(group16 == 0, last, tail)
    put(240, tail)
    used = 96 // 16
    if gr.shape[1] > used:
        gr[:, used:] = jnp.zeros((3, gr.shape[1] - used, 16, width), BF)

    here = (ix, iy, iz)

    def ring(phase):
        out, got = [], []
        for part in range(3):
            axis = (part + phase % 3) % 3
            count, me = sizes[axis], here[axis]
            per = gr.shape[1] // sizes[part]
            for k in range(1, count):
                to = lax.rem(me + k, count)
                frm = lax.rem(me - k + count, count)
                there = tuple(to if i == axis else v for i, v in enumerate(here))
                src = gr.at[part, pl.ds(to * per, per)] if phase == 0 else ar.at[phase, part, me]

                def copy(slot):
                    return pltpu.make_async_remote_copy(
                        src_ref=src, dst_ref=ar.at[phase, part, slot], send_sem=asend.at[phase, part, k - 1],
                        recv_sem=arecv.at[phase, part, k - 1], device_id=there, device_id_type=MESH)

                out.append(copy(me))
                got.append(copy(frm))
        for c in out:
            c.start()
        return out, got

    def advance(copies, phase):
        for c in copies[1]:
            c.wait_recv()
        for part in range(3):
            total = ar[phase, part, 0].astype(F32)
            for k in range(1, sizes[(part + phase) % 3]):
                total = total + ar[phase, part, k].astype(F32)
            ar[phase + 1, part, here[(part + phase + 1) % 3]] = total.astype(BF)
        return ring(phase + 1)

    first = ring(0)
    for part in range(3):
        per = gr.shape[1] // sizes[part]
        ar[0, part, here[part]] = gr[part, pl.ds(here[part] * per, per)]

    def dec_row(q, _):
        k = 18 * chans
        out = conv_row(wd[...], [js[p, pl.ds(q, 3)].reshape(k, width) for p in range(depth + 2)], depth)
        for p in range(depth):
            dec_out[p, q] = out[p].astype(BF)

    lax.fori_loop(0, height // 2, dec_row, None)

    second = advance(first, 0)
    lax.fori_loop(height // 2, height, dec_row, None)
    landed(ecopies, recvs)

    def fill_enc(y, _):
        wide = eh[:, y].reshape((depth + 2) * chans, 2 * width).astype(F32)
        for c in range(3):
            part = shifted(wide, c)[:, :width]
            es[:, y, c] = part.astype(BF).reshape(depth + 2, chans, width)

    lax.fori_loop(0, height + 2, fill_enc, None)

    def vol_row(q, _):
        k = 9 * chans
        out = conv_row(web[...], [es[p, pl.ds(q, 3)].reshape(k, width) for p in range(depth + 2)], depth)
        for p in range(depth):
            vg_out[p, q] = out[p].astype(BF)

    third = advance(second, 1)
    lax.fori_loop(0, height // 2, vol_row, None)
    fourth = advance(third, 2)
    lax.fori_loop(height // 2, height, vol_row, None)
    for c in fourth[1]:
        c.wait_recv()
    for part in range(3):
        sum_out[part] = ar[3, part].astype(F32).reshape(sum_out.shape[1:])

    left(zcopies, esends)
    for copies in (vcopies, pcopies, gcopies, ucopies, scopies, ecopies):
        left(copies, sends)
    for copies in (first, second, third, fourth):
        for c in copies[0]:
            c.wait_send()


def stacked(weight):
    k = 9 * weight.shape[1]
    return jnp.swapaxes(weight.reshape(3, k, weight.shape[2]), 1, 2).reshape(3 * weight.shape[2], k)


def flipped(weight):
    return jnp.transpose(weight[::-1], (0, 2, 1))


def per_device(sizes, volume, enc_weight, coarse_weight, up_weight, dec_weight, cotangent):
    nx, ny, nz = sizes
    chans, d, h, w = volume.shape
    cd, ch = d // 2, h // 2
    tiles = max(-(-6 // n) * n for n in sizes)
    pair = jnp.transpose(jnp.concatenate([volume, cotangent], axis=0), (1, 2, 0, 3))
    operands = (
        pair, stacked(enc_weight), stacked(dec_weight), stacked(flipped(dec_weight)),
        stacked(coarse_weight), stacked(flipped(coarse_weight)), stacked(flipped(enc_weight)),
        up_weight.T, up_weight)
    c2 = 2 * chans
    scratch = [
        ((d + 2, h + 2, c2, w), BF),
        ((2, d, chans, w), BF),
        ((2, 3, d + 2, chans, w), BF),
        ((d + 2, h + 2, 3, chans, 2 * w), BF),
        ((d + 2, h + 2, 3, chans, 2 * w), BF),
        ((d + 2, h + 2, chans, 2 * w), BF),
        ((d, h, chans, 2 * w), F32),
        ((d, h, chans, 2 * w), F32),
        ((cd, ch, chans, 2 * w), BF),
        ((cd, ch, chans, 2 * w), BF),
        ((cd, ch, chans, w), BF),
        ((cd + 2, ch + 2, chans, w), BF),
        ((cd + 2, ch + 2, 3, chans, w), BF),
        ((cd, ch, c2, w), BF),
        ((cd + 2, ch + 2, chans, w), BF),
        ((cd + 2, ch + 2, c2, w), BF),
        ((cd + 2, ch + 2, 3, c2, w), BF),
        ((d + 2, h + 2, 3, c2, w), BF),
        ((d + 2, h + 2, chans, 2 * w), BF),
        ((d + 2, h + 2, 3, chans, w), BF),
        ((3, tiles, 16, w), BF),
        ((4, 3, max(sizes), tiles // max(sizes), 16, w), BF),
    ]
    dma = pltpu.SemaphoreType.DMA
    widest = max(sizes) - 1
    sems = [dma((8,))] * 2 + [dma((18,))] * 2 + [dma((8,))] * 10 + [dma((4, 3, max(widest, 1)))] * 2
    vmem = pl.BlockSpec(memory_space=pltpu.VMEM)
    dec, vg, total = pl.pallas_call(
        functools.partial(kernel, sizes),
        out_shape=(
            jax.ShapeDtypeStruct((d, h, chans, w), BF),
            jax.ShapeDtypeStruct((d, h, chans, w), BF),
            jax.ShapeDtypeStruct((3, tiles, 16, w), F32)),
        in_specs=[vmem] * len(operands),
        out_specs=(vmem,) * 3,
        scratch_shapes=[pltpu.VMEM(s, t) for s, t in scratch] + sems,
        compiler_params=pltpu.CompilerParams(
            collective_id=0, has_side_effects=True, vmem_limit_bytes=48 * 1024 * 1024),
    )(*operands)
    g = total[:, :6].reshape(288, w)
    tail = g[240:288]
    enc = jnp.transpose(g[0:48].reshape(48, 8, 16), (1, 0, 2)).reshape(24, 16, 16)
    enc = jnp.concatenate([enc, tail[:, 0:16].reshape(3, 16, 16)], axis=0)
    decg = jnp.transpose(g[48:144].reshape(96, 8, 16), (1, 0, 2)).reshape(24, 32, 16)
    decl = jnp.concatenate([tail[:, 16:32], tail[:, 32:48]], axis=0).reshape(3, 32, 16)
    decg = jnp.concatenate([decg, decl], axis=0)
    coarse = jnp.transpose(g[144:240].reshape(2, 48, 4, 32), (0, 2, 1, 3)).reshape(24, 16, 32)
    coarse = jnp.concatenate([coarse, tail[:, 64:96].reshape(3, 16, 32)], axis=0)
    upg = tail[0:32, 48:64]
    return (jnp.transpose(dec, (2, 0, 1, 3)), jnp.transpose(vg, (2, 0, 1, 3)), enc, coarse, upg, decg)


def solution(mesh):
    sizes = tuple(mesh.shape[a] for a in AXES)
    spec = P(None, "gx", "gy", "gz")
    return jax.shard_map(
        functools.partial(per_device, sizes),
        mesh=mesh,
        in_specs=(spec, P(), P(), P(), P(), spec),
        out_specs=(spec, spec, P(), P(), P(), P()),
        check_vma=False,
    )
```

```python
import functools

import jax
import jax.numpy as jnp
from jax import lax
from jax.experimental import pallas as pl
from jax.experimental.pallas import tpu as pltpu
from jax.sharding import PartitionSpec as P

AXES = ("gx", "gy", "gz")
BF = jnp.bfloat16
F32 = jnp.float32
MESH = pl.DeviceIdType.MESH
DIRS = tuple((dx, dy) for dx in (-1, 0, 1) for dy in (-1, 0, 1) if (dx, dy) != (0, 0))


def dot(a, b):
    return jnp.dot(a, b, preferred_element_type=F32)


def dot_nt(a, b):
    return lax.dot_general(a, b, (((1,), (1,)), ((), ())), preferred_element_type=F32)


def all_of(*conds):
    total = None
    for c in conds:
        if c is not None:
            total = c if total is None else jnp.logical_and(total, c)
    return total


def span(step, size, halo):
    if step == 0:
        return (0, size), (halo, size)
    if step > 0:
        return (size - halo, halo), (0, halo)
    return (0, halo), (halo + size, halo)


def kernel(sizes, vc, we, wd, wdb, wc, wcb, web, upt, up, dec_out, vg_out, sum_out,
           vct, pk, er, vs, cs, skip, slope, jg, ughi, uglo, ug, ph, ps, act, uh, gh, gs, js, eh, es,
           gr, ar,
           vsend, vrecv, zsend, zrecv, psend, precv, gsend, grecv, usend, urecv, ssend, srecv, esend, erecv,
           asend, arecv):
    nx, ny, nz = sizes
    ix, iy, iz = (lax.axis_index(a) for a in AXES)
    depth, height, _, width = vc.shape
    chans = vc.shape[2] // 2
    cd, ch = depth // 2, height // 2

    def exists(step, index, count):
        return None if step == 0 else (index + step < count if step > 0 else index + step >= 0)

    def at(dx, dy, dz=0):
        return (ix + dx, iy + dy, iz + dz)

    def guarded(cond, f):
        if cond is None:
            f()
        else:
            pl.when(cond)(f)

    sends = [all_of(exists(dx, ix, nx), exists(dy, iy, ny)) for dx, dy in DIRS]
    recvs = [all_of(exists(-dx, ix, nx), exists(-dy, iy, ny)) for dx, dy in DIRS]
    ends = tuple((dx, dy, s) for s in (-1, 1) for dx in (-1, 0, 1) for dy in (-1, 0, 1))
    esends = [all_of(exists(dx, ix, nx), exists(dy, iy, ny), exists(dz, iz, nz)) for dx, dy, dz in ends]
    erecvs = [all_of(exists(-dx, ix, nx), exists(-dy, iy, ny), exists(-dz, iz, nz)) for dx, dy, dz in ends]

    cores = min(2, nx)
    lows, across = nx // cores, ny // 2 if ny > 4 else ny
    highs = ny // across
    core, y_low, x_at, y_high = lax.rem(ix, cores), ix // cores, lax.rem(iy, across), iy // across
    groups = (
        (cores * across, core * across + x_at,
         lambda j: (y_low * cores + j // across, y_high * across + lax.rem(j, across), iz)),
        (highs * lows, y_high * lows + y_low,
         lambda j: (lax.rem(j, lows) * cores + core, (j // lows) * across + x_at, iz)),
        (nz, iz, lambda j: (ix, iy, j)),
    )

    for ref in (vct, er, skip, ph, uh, gh, eh):
        ref[...] = jnp.zeros(ref.shape, ref.dtype)
    vct[1:1 + depth, 1:1 + height] = vc[...]
    barrier = pltpu.get_barrier_semaphore()

    def greet(device):
        pl.semaphore_signal(barrier, inc=1, device_id=device, device_id_type=MESH)

    for count, me, member in groups:
        for k in range(1, count):
            greet(member(lax.rem(me + k, count)))
    for dx, dy, dz in [d + (0,) for d in DIRS] + list(ends):
        if dx != 0 or dy != 0:
            guarded(all_of(exists(dx, ix, nx), exists(dy, iy, ny), exists(dz, iz, nz)),
                    lambda dx=dx, dy=dy, dz=dz: greet(at(dx, dy, dz)))

    def both(index, count):
        return (jnp.where(index > 0, 1, 0) + jnp.where(index < count - 1, 1, 0)).astype(jnp.int32)

    row = lax.broadcasted_iota(jnp.int32, (width, 2 * width), 0)
    lane = lax.broadcasted_iota(jnp.int32, (width, 2 * width), 1)
    total = jnp.zeros((depth * chans, 2 * width), F32)
    for n in range(2):
        for y in range(height):
            base = 64 * n + 8 * y
            pick = ((lane == base + row) & (row < 8)) | ((lane == width + base + row - 120) & (row >= 120))
            total = total + dot(vc[:, y, n * chans:(n + 1) * chans].reshape(depth * chans, width), pick.astype(BF))
    for side in range(2):
        pk[side] = total[:, side * width:(side + 1) * width].astype(BF).reshape(depth, chans, width)
    bx, by, bz = both(ix, nx), both(iy, ny), both(iz, nz)
    near = bx + by + bx * by
    pl.semaphore_wait(barrier, sum(count - 1 for count, _, _ in groups) + near + near * bz)

    def exchange(src, src_at, dst, dst_at, send_sem, recv_sem):
        copies = []
        for d, (dx, dy) in enumerate(DIRS):
            copies.append(pltpu.make_async_remote_copy(
                src_ref=src.at[src_at(dx, dy)], dst_ref=dst.at[dst_at(dx, dy)],
                send_sem=send_sem.at[d], recv_sem=recv_sem.at[d],
                device_id=at(dx, dy), device_id_type=MESH))
        return copies

    def begin(copies, conds):
        for c, s in zip(copies, conds):
            guarded(s, c.start)

    def landed(copies, conds):
        for c, r in zip(copies, conds):
            guarded(r, c.wait_recv)

    def left(copies, conds):
        for c, s in zip(copies, conds):
            guarded(s, c.wait_send)

    def rim_src(halo, d0, h0, off):
        def f(dx, dy):
            (a, n), _ = span(dx, d0, halo)
            (b, m), _ = span(dy, h0, halo)
            return (pl.ds(a + off, n), pl.ds(b + off, m))
        return f

    def rim_dst(halo, d0, h0):
        def f(dx, dy):
            _, (a, n) = span(dx, d0, halo)
            _, (b, m) = span(dy, h0, halo)
            return (pl.ds(a, n), pl.ds(b, m))
        return f

    vcopies = exchange(vc, rim_src(1, depth, height, 0), vct, rim_dst(1, depth, height), vsend, vrecv)
    begin(vcopies, sends)

    zcopies = []
    for d, (dx, dy, dz) in enumerate(ends):
        (a, n), (b, m) = span(dx, depth, 1)
        side = 1 if dz > 0 else 0
        zcopies.append(pltpu.make_async_remote_copy(
            src_ref=pk.at[side, pl.ds(a, n)], dst_ref=er.at[side, 1 - dy, pl.ds(b, m)],
            send_sem=zsend.at[d], recv_sem=zrecv.at[d],
            device_id=at(dx, dy, dz), device_id_type=MESH))
    begin(zcopies, esends)
    landed(vcopies, recvs)
    landed(zcopies, erecvs)

    def shifted(wide, c):
        if c == 1:
            return wide
        return pltpu.roll(wide, 1 if c == 0 else wide.shape[1] - 1, 1)

    def fill_inputs(y, _):
        dyi, base = (y + 7) // 8, 8 * lax.rem(y + 7, 8)
        flat = ((depth + 2) * chans, width)
        kind, spot = lane // width, lax.rem(lane, width)
        source = base + 64 * kind + spot
        lo = (row == source - 120) & (spot >= 120)
        hi = (row == source) & (spot < 8)
        got = dot(er[1, dyi].reshape(flat), lo.astype(BF)) + dot(er[0, dyi].reshape(flat), hi.astype(BF))
        for n, ref in enumerate((vs, cs)):
            own = vct[:, y, n * chans:(n + 1) * chans].reshape(flat).astype(F32)
            wide = jnp.concatenate([own, got[:, n * width:(n + 1) * width]], axis=1)
            for c in range(3):
                ref[:, y, c] = shifted(wide, c).astype(BF).reshape(depth + 2, chans, 2 * width)

    lax.fori_loop(0, height + 2, fill_inputs, None)

    fine = lax.broadcasted_iota(jnp.int32, (1, 2 * width), 1)
    coarse = lax.broadcasted_iota(jnp.int32, (1, width), 1)
    low_ok = jnp.where(iz > 0, 1.0, 0.0).astype(F32)
    high_ok = jnp.where(iz < nz - 1, 1.0, 0.0).astype(F32)
    fine_mask = jnp.where(fine < width, 1.0, jnp.where(fine < 3 * width // 2, high_ok, low_ok))
    coarse_mask = jnp.where(coarse < width // 2, 1.0, jnp.where(coarse < 3 * width // 4, high_ok, low_ok))
    own_coarse = coarse < width // 2

    def conv_row(weight, planes, outs):
        m = weight.shape[0] // 3
        ys = [dot(weight, x) for x in planes]
        return [ys[p][:m] + ys[p + 1][m:2 * m] + ys[p + 2][2 * m:] for p in range(outs)]

    def enc_row(q, _):
        k = 9 * chans
        pre = conv_row(we[...], [vs[p, pl.ds(q, 3)].reshape(k, 2 * width) for p in range(depth + 2)], depth)
        for p in range(depth):
            t = pre[p]
            sig = 1.0 / (1.0 + jnp.exp(-t))
            skip[1 + p, 1 + q] = (t * sig * fine_mask).astype(BF)
            slope[p, q] = sig * (1.0 + t * (1.0 - sig)) * fine_mask

    lax.fori_loop(0, height, enc_row, None)

    pool = (lax.broadcasted_iota(jnp.int32, (2 * width, width), 0) // 2
            == lax.broadcasted_iota(jnp.int32, (2 * width, width), 1)).astype(BF)

    for q in range(ch):
        rows_in = skip[1:1 + depth, 1 + 2 * q:3 + 2 * q].reshape(depth * 2 * chans, 2 * width)
        half = dot(rows_in, pool).reshape(cd, 4, chans, width)
        ph[1:1 + cd, 1 + q] = ((half[:, 0] + half[:, 1] + half[:, 2] + half[:, 3]) * 0.125).astype(BF)
    pcopies = exchange(ph, rim_src(1, cd, ch, 1), ph, rim_dst(1, cd, ch), psend, precv)
    begin(pcopies, sends)
    scopies = exchange(skip, rim_src(1, depth, height, 1), skip, rim_dst(1, depth, height), ssend, srecv)
    begin(scopies, sends)

    def joined_row(q, _):
        k = 9 * chans
        sums = [jnp.zeros((chans, 2 * width), F32) for _ in range(cd)]
        for e in range(2):
            r = 2 * q + e
            out = conv_row(wdb[...], [cs[p, pl.ds(r, 3)].reshape(k, 2 * width) for p in range(depth + 2)], depth)
            for p in range(depth):
                jg[p, r] = out[p][:chans]
                sums[p // 2] = sums[p // 2] + out[p][chans:]
        for p in range(cd):
            hi = sums[p].astype(BF)
            ughi[p, q] = hi
            uglo[p, q] = (sums[p] - hi.astype(F32)).astype(BF)

    lax.fori_loop(0, ch, joined_row, None)
    flat = (cd * ch * chans, 2 * width)
    grad = dot(ughi[...].reshape(flat), pool) + dot(uglo[...].reshape(flat), pool)
    ug[...] = grad.astype(BF).reshape(ug.shape)

    landed(pcopies, recvs)

    def fill_pooled(q, _):
        wide = ph[:, q].reshape((cd + 2) * chans, width).astype(F32)
        for c in range(3):
            ps[:, q, c] = shifted(wide, c).astype(BF).reshape(cd + 2, chans, width)

    lax.fori_loop(0, ch + 2, fill_pooled, None)
    for q in range(ch):
        k = 9 * chans
        pre = conv_row(wc[...], [ps[p, q:q + 3].reshape(k, width) for p in range(cd + 2)], cd)
        for p in range(cd):
            t = pre[p]
            sig = 1.0 / (1.0 + jnp.exp(-t))
            a = (t * sig * coarse_mask).astype(BF)
            act[p, q] = a
            uh[1 + p, 1 + q] = dot(upt[...], a).astype(BF)
            back = dot(up[...], ug[p, q])
            gh[1 + p, 1 + q] = (back * (sig * (1.0 + t * (1.0 - sig)) * coarse_mask)).astype(BF)

    gcopies = exchange(gh, rim_src(1, cd, ch, 1), gh, rim_dst(1, cd, ch), gsend, grecv)
    begin(gcopies, sends)
    ucopies = exchange(uh, rim_src(1, cd, ch, 1), uh, rim_dst(1, cd, ch), usend, urecv)
    begin(ucopies, sends)

    group16 = lax.broadcasted_iota(jnp.int32, (1, width), 1) // 16
    group32 = lax.broadcasted_iota(jnp.int32, (1, width), 1) // 32

    def tap_sums(block, step, groups, gid):
        out = []
        for b in range(3):
            total = jnp.zeros((step, width), F32)
            for q in range(groups):
                total = jnp.where(gid == q, block[(q + b) * step:(q + b + 1) * step], total)
            size = width // 2
            while size >= width // groups:
                total = total + pltpu.roll(total, size, 1)
                size //= 2
            out.append(total)
        return out

    def put(first, value):
        gr[first // 16:first // 16 + 3] = value.astype(BF).reshape(3, 16, width)

    tail = jnp.zeros((3 * chans, width), F32)
    step = 3 * chans
    taps = []
    masked = [jnp.where(own_coarse, gh[1 + p, 1:1 + ch].reshape(2 * chans * ch, width), 0)
              for p in range(cd)]
    for a in range(3):
        block = sum(dot_nt(ps[p + a].reshape((ch + 2) * step, width), masked[p]) for p in range(cd))
        taps += tap_sums(block, step, ch, group32)
    for half in range(2):
        total = jnp.zeros((step, width), F32)
        for g in range(4):
            total = jnp.where(group32 == g, taps[4 * half + g], total)
        put(144 + 48 * half, total)
    tail = jnp.where(group32 == 2, taps[8], tail)
    up_total = jnp.zeros((2 * chans, width), F32)
    for p in range(cd):
        for q in range(ch):
            g = jnp.where(own_coarse, ug[p, q], 0)
            up_total = up_total + dot_nt(act[p, q], jnp.concatenate([g] * 8, axis=0))
    up_total = jnp.concatenate([up_total, jnp.zeros((chans, width), F32)], axis=0)
    tail = jnp.where(group16 == 3, up_total, tail)

    def fill_skip(first, count, y):
        wide = skip[first:first + count, y].reshape(count * chans, 2 * width).astype(F32)
        for c in range(3):
            part = shifted(wide, c)[:, :width]
            js[first:first + count, y, c, 0:chans] = part.astype(BF).reshape(count, chans, width)

    lax.fori_loop(1, height + 1, lambda y, _: fill_skip(1, depth, y), None)
    landed(scopies, recvs)
    for y in (0, height + 1):
        fill_skip(0, depth + 2, y)

    def fill_sides(y, _):
        fill_skip(0, 1, y)
        fill_skip(depth + 1, 1, y)

    lax.fori_loop(1, height + 1, fill_sides, None)

    def fine_taps(source, step, grads):
        taps = []
        for a in range(3):
            block = sum(dot_nt(source(a + p), grads[p]) for p in range(depth))
            taps += tap_sums(block, step, height, group16)
        total = jnp.zeros((step, width), F32)
        for g in range(8):
            total = jnp.where(group16 == g, taps[g], total)
        return total, taps[8]

    def joined_taps(first):
        return fine_taps(
            lambda x: js[x, :, :, first:first + chans].reshape((height + 2) * 3 * chans, width), 3 * chans,
            [vc[p, :, chans:2 * chans].reshape(height * chans, width) for p in range(depth)])

    total, last = joined_taps(0)
    put(48, total)
    tail = jnp.where(group16 == 1, last, tail)
    landed(gcopies, recvs)

    def fill_coarse(y, _):
        wide = gh[:, y].reshape((cd + 2) * 2 * chans, width).astype(F32)
        for c in range(3):
            gs[:, y, c] = shifted(wide, c).astype(BF).reshape(cd + 2, 2 * chans, width)

    lax.fori_loop(0, ch + 2, fill_coarse, None)
    spread = (lax.broadcasted_iota(jnp.int32, (width, 2 * width), 1) // 2
              == lax.broadcasted_iota(jnp.int32, (width, 2 * width), 0)).astype(BF)

    def back_row(q, _):
        k = 18 * chans
        pg = conv_row(wcb[...], [gs[p, pl.ds(q, 3)].reshape(k, width) for p in range(cd + 2)], cd)
        for p in range(cd):
            v = pg[p] * 0.125
            hi = v.astype(BF)
            lo = (v - hi.astype(F32)).astype(BF)
            wide = dot(hi, spread) + dot(lo, spread)
            for e in range(2):
                for f in range(2):
                    g = (jg[2 * p + e, 2 * q + f] + wide) * slope[2 * p + e, 2 * q + f]
                    eh[1 + 2 * p + e, 1 + 2 * q + f] = g.astype(BF)

    lax.fori_loop(0, ch, back_row, None)
    ecopies = exchange(eh, rim_src(1, depth, height, 1), eh, rim_dst(1, depth, height), esend, erecv)
    begin(ecopies, sends)

    landed(ucopies, recvs)
    low = lax.broadcasted_iota(jnp.int32, (width, width), 0)
    lane = lax.broadcasted_iota(jnp.int32, (width, width), 1)
    for c in range(3):
        source = lax.rem(lane + (c - 1) + 2 * width, 2 * width) // 2
        pick = (low == source).astype(BF)
        wide = dot(uh[...].reshape((cd + 2) * (ch + 2) * chans, width), pick)
        wide = wide.astype(BF).reshape(cd + 2, ch + 2, chans, width)
        for x in range(depth + 2):
            for y in range(height + 2):
                js[x, y, c, chans:2 * chans] = wide[(x + 1) // 2, (y + 1) // 2]

    total, last = joined_taps(chans)
    put(96, total)
    tail = jnp.where(group16 == 2, last, tail)
    total, last = fine_taps(
        lambda x: vs[x, :, :, :, 0:width].reshape((height + 2) * 3 * chans, width), 3 * chans,
        [eh[1 + p, 1:1 + height, :, 0:width].reshape(height * chans, width) for p in range(depth)])
    put(0, total)
    tail = jnp.where(group16 == 0, last, tail)
    put(240, tail)
    used = 288 // 16
    if gr.shape[0] > used:
        gr[used:] = jnp.zeros((gr.shape[0] - used, 16, width), BF)

    per = gr.shape[0] // groups[0][0]

    def ring(phase):
        count, me, member = groups[phase % 3]
        out, got = [], []
        for k in range(1, count):
            to = lax.rem(me + k, count)
            frm = lax.rem(me - k + count, count)
            src = gr.at[pl.ds(to * per, per)] if phase == 0 else ar.at[phase, me]

            def copy(slot):
                return pltpu.make_async_remote_copy(
                    src_ref=src, dst_ref=ar.at[phase, slot], send_sem=asend.at[phase, k - 1],
                    recv_sem=arecv.at[phase, k - 1], device_id=member(to), device_id_type=MESH)

            out.append(copy(me))
            got.append(copy(frm))
        for c in out:
            c.start()
        return out, got

    def advance(copies, phase):
        for c in copies[1]:
            c.wait_recv()
        total = ar[phase, 0].astype(F32)
        for k in range(1, groups[phase][0]):
            total = total + ar[phase, k].astype(F32)
        ar[phase + 1, groups[(phase + 1) % 3][1]] = total.astype(BF)
        return ring(phase + 1)

    first = ring(0)
    ar[0, groups[0][1]] = gr[pl.ds(groups[0][1] * per, per)]

    def dec_row(q, _):
        k = 18 * chans
        out = conv_row(wd[...], [js[p, pl.ds(q, 3)].reshape(k, width) for p in range(depth + 2)], depth)
        for p in range(depth):
            dec_out[p, q] = out[p].astype(BF)

    lax.fori_loop(0, height // 2, dec_row, None)

    second = advance(first, 0)
    lax.fori_loop(height // 2, height, dec_row, None)
    landed(ecopies, recvs)

    def fill_enc(y, _):
        wide = eh[:, y].reshape((depth + 2) * chans, 2 * width).astype(F32)
        for c in range(3):
            part = shifted(wide, c)[:, :width]
            es[:, y, c] = part.astype(BF).reshape(depth + 2, chans, width)

    lax.fori_loop(0, height + 2, fill_enc, None)

    def vol_row(q, _):
        k = 9 * chans
        out = conv_row(web[...], [es[p, pl.ds(q, 3)].reshape(k, width) for p in range(depth + 2)], depth)
        for p in range(depth):
            vg_out[p, q] = out[p].astype(BF)

    third = advance(second, 1)
    lax.fori_loop(0, height // 2, vol_row, None)
    fourth = advance(third, 2)
    lax.fori_loop(height // 2, height, vol_row, None)
    for c in fourth[1]:
        c.wait_recv()
    sum_out[...] = ar[3, 0:groups[0][0]].astype(F32).reshape(sum_out.shape)

    left(zcopies, esends)
    for copies in (vcopies, pcopies, gcopies, ucopies, scopies, ecopies):
        left(copies, sends)
    for copies in (first, second, third, fourth):
        for c in copies[0]:
            c.wait_send()


def stacked(weight):
    k = 9 * weight.shape[1]
    return jnp.swapaxes(weight.reshape(3, k, weight.shape[2]), 1, 2).reshape(3 * weight.shape[2], k)


def flipped(weight):
    return jnp.transpose(weight[::-1], (0, 2, 1))


def per_device(sizes, volume, enc_weight, coarse_weight, up_weight, dec_weight, cotangent):
    nx, ny, nz = sizes
    chans, d, h, w = volume.shape
    cd, ch = d // 2, h // 2
    owners = min(2, nx) * (ny // 2 if ny > 4 else ny)
    per = -(-18 // owners)
    pair = jnp.transpose(jnp.concatenate([volume, cotangent], axis=0), (1, 2, 0, 3))
    operands = (
        pair, stacked(enc_weight), stacked(dec_weight), stacked(flipped(dec_weight)),
        stacked(coarse_weight), stacked(flipped(coarse_weight)), stacked(flipped(enc_weight)),
        up_weight.T, up_weight)
    c2 = 2 * chans
    widest = max(owners, nx * ny // owners, nz) - 1
    scratch = [
        ((d + 2, h + 2, c2, w), BF),
        ((2, d, chans, w), BF),
        ((2, 3, d + 2, chans, w), BF),
        ((d + 2, h + 2, 3, chans, 2 * w), BF),
        ((d + 2, h + 2, 3, chans, 2 * w), BF),
        ((d + 2, h + 2, chans, 2 * w), BF),
        ((d, h, chans, 2 * w), F32),
        ((d, h, chans, 2 * w), F32),
        ((cd, ch, chans, 2 * w), BF),
        ((cd, ch, chans, 2 * w), BF),
        ((cd, ch, chans, w), BF),
        ((cd + 2, ch + 2, chans, w), BF),
        ((cd + 2, ch + 2, 3, chans, w), BF),
        ((cd, ch, c2, w), BF),
        ((cd + 2, ch + 2, chans, w), BF),
        ((cd + 2, ch + 2, c2, w), BF),
        ((cd + 2, ch + 2, 3, c2, w), BF),
        ((d + 2, h + 2, 3, c2, w), BF),
        ((d + 2, h + 2, chans, 2 * w), BF),
        ((d + 2, h + 2, 3, chans, w), BF),
        ((owners * per, 16, w), BF),
        ((4, widest + 1, per, 16, w), BF),
    ]
    dma = pltpu.SemaphoreType.DMA
    sems = [dma((8,))] * 2 + [dma((18,))] * 2 + [dma((8,))] * 10 + [dma((4, max(widest, 1)))] * 2
    vmem = pl.BlockSpec(memory_space=pltpu.VMEM)
    dec, vg, total = pl.pallas_call(
        functools.partial(kernel, sizes),
        out_shape=(
            jax.ShapeDtypeStruct((d, h, chans, w), BF),
            jax.ShapeDtypeStruct((d, h, chans, w), BF),
            jax.ShapeDtypeStruct((owners * per, 16, w), F32)),
        in_specs=[vmem] * len(operands),
        out_specs=(vmem,) * 3,
        scratch_shapes=[pltpu.VMEM(s, t) for s, t in scratch] + sems,
        compiler_params=pltpu.CompilerParams(
            collective_id=0, has_side_effects=True, vmem_limit_bytes=48 * 1024 * 1024),
    )(*operands)
    g = total[:18].reshape(288, w)
    tail = g[240:288]
    enc = jnp.transpose(g[0:48].reshape(48, 8, 16), (1, 0, 2)).reshape(24, 16, 16)
    enc = jnp.concatenate([enc, tail[:, 0:16].reshape(3, 16, 16)], axis=0)
    halves = []
    for first, lane in ((48, 16), (96, 32)):
        half = jnp.transpose(g[first:first + 48].reshape(48, 8, 16), (1, 0, 2)).reshape(24, 16, 16)
        halves.append(jnp.concatenate([half, tail[:, lane:lane + 16].reshape(3, 16, 16)], axis=0))
    decg = jnp.concatenate(halves, axis=1)
    coarse = jnp.transpose(g[144:240].reshape(2, 48, 4, 32), (0, 2, 1, 3)).reshape(24, 16, 32)
    coarse = jnp.concatenate([coarse, tail[:, 64:96].reshape(3, 16, 32)], axis=0)
    upg = tail[0:32, 48:64]
    return (jnp.transpose(dec, (2, 0, 1, 3)), jnp.transpose(vg, (2, 0, 1, 3)), enc, coarse, upg, decg)


def solution(mesh):
    sizes = tuple(mesh.shape[a] for a in AXES)
    spec = P(None, "gx", "gy", "gz")
    return jax.shard_map(
        functools.partial(per_device, sizes),
        mesh=mesh,
        in_specs=(spec, P(), P(), P(), P(), spec),
        out_specs=(spec, spec, P(), P(), P(), P()),
        check_vma=False,
    )
```

```python
import functools

import jax
import jax.numpy as jnp
from jax import lax
from jax.experimental import pallas as pl
from jax.experimental.pallas import tpu as pltpu
from jax.sharding import PartitionSpec as P

AXES = ("gx", "gy", "gz")
BF = jnp.bfloat16
F32 = jnp.float32
MESH = pl.DeviceIdType.MESH
DIRS = tuple((dx, dy) for dx in (-1, 0, 1) for dy in (-1, 0, 1) if (dx, dy) != (0, 0))


def dot(a, b):
    return jnp.dot(a, b, preferred_element_type=F32)


def dot_nt(a, b):
    return lax.dot_general(a, b, (((1,), (1,)), ((), ())), preferred_element_type=F32)


def dot_tn(a, b):
    return lax.dot_general(a, b, (((0,), (0,)), ((), ())), preferred_element_type=F32)


def zero_one(shape, rule):
    return rule(lax.broadcasted_iota(jnp.int32, shape, 0), lax.broadcasted_iota(jnp.int32, shape, 1))


def arrange_weights(enc, coarse, upt, dec, we, wd, wdb, wc, wcb, web, up):
    flat = enc[...].reshape(256, 27)
    same_in = zero_one((256, 144), lambda r, l: r // 16 == l % 16)
    same_out = zero_one((256, 144), lambda r, l: r % 16 == l % 16)
    fold_in = zero_one((16, 256), lambda r, l: r == l % 16).astype(BF)
    fold_out = zero_one((16, 256), lambda r, l: r == l // 16).astype(BF)
    for a in range(3):
        ahead = dot(flat, zero_one((27, 144), lambda r, l: r == 9 * a + l // 16).astype(BF))
        we[16 * a:16 * a + 16] = dot(fold_in, jnp.where(same_in, ahead, 0.0).astype(BF)).astype(BF)
        back = dot(flat, zero_one((27, 144), lambda r, l: r == 26 - 9 * a - l // 16).astype(BF))
        web[16 * a:16 * a + 16] = dot(fold_out, jnp.where(same_out, back, 0.0).astype(BF)).astype(BF)
    totals = [0.0] * 4
    for t in range(9):
        wide = zero_one((32, 288), lambda r, l: l == 32 * t + r).astype(BF)
        slim = zero_one((16, 144), lambda r, l: l == 16 * t + r).astype(BF)
        ahead, back = (t, 9 + t, 18 + t), (26 - t, 17 - t, 8 - t)
        totals[0] += dot(jnp.concatenate([dec[k] for k in ahead], axis=0), wide)
        totals[1] += dot_tn(jnp.concatenate([dec[k] for k in back], axis=1), slim)
        totals[2] += dot_tn(jnp.concatenate([coarse[k] for k in ahead], axis=1), slim)
        totals[3] += dot(jnp.concatenate([coarse[k] for k in back], axis=0), wide)
    for ref, total in zip((wd, wdb, wc, wcb), totals):
        ref[...] = total.astype(BF)
    up[...] = dot_tn(upt[...], zero_one((16, 16), lambda r, l: r == l).astype(BF)).astype(BF)


def finish(dec, vg, total, dec_out, vg_out, enc_out, coarse_out, up_out, decg_out,
           enc, coarse, up, decg, sems):
    copies = [pltpu.make_async_copy(a, b, sems.at[k]) for k, (a, b) in enumerate(
        ((dec, dec_out), (vg, vg_out), (enc, enc_out), (coarse, coarse_out), (up, up_out), (decg, decg_out)))]
    copies[0].start()
    copies[1].start()

    def rows(first, count):
        return total[first // 16:(first + count) // 16].reshape(count, 128)

    eye = zero_one((128, 128), lambda r, l: r == l).astype(BF)
    for c in range(3):
        last = rows(240 + 16 * c, 16)
        block = jnp.concatenate([rows(48 + 16 * c, 16), rows(96 + 16 * c, 16)], axis=0)
        turned = dot_nt(eye, block).reshape(8, 16, 32)
        for g in range(8):
            decg[3 * g + c] = turned[g]
        skip_last = dot_nt(zero_one((16, 128), lambda r, l: l == 16 + r).astype(BF), last)
        upper_last = dot_nt(zero_one((16, 128), lambda r, l: l == 32 + r).astype(BF), last)
        decg[24 + c] = jnp.concatenate([skip_last, upper_last], axis=1)
    copies[5].start()
    for c in range(3):
        for half in range(2):
            block = rows(144 + 48 * half + 16 * c, 16)
            for g in range(4):
                pick = zero_one((128, 32), lambda r, l: r == 32 * g + l).astype(BF)
                coarse[3 * (4 * half + g) + c] = dot(block, pick)
        pick = zero_one((128, 32), lambda r, l: r == 64 + l).astype(BF)
        coarse[24 + c] = dot(rows(240 + 16 * c, 16), pick)
    copies[3].start()
    up[...] = dot_nt(zero_one((16, 128), lambda r, l: l == 48 + r).astype(BF), rows(240, 32))
    copies[4].start()
    grow = zero_one((256, 16), lambda r, l: l == r // 16).astype(BF)
    same = zero_one((256, 128), lambda r, l: r % 16 == l % 16)
    flat = jnp.zeros((256, 27), F32)
    for c in range(3):
        wide = jnp.where(same, dot(grow, rows(16 * c, 16)), 0.0).astype(BF)
        flat = flat + dot(wide, zero_one((128, 27), lambda r, l: l == 3 * (r // 16) + c).astype(BF))
        wide = jnp.where(same, dot(grow, rows(240 + 16 * c, 16)), 0.0).astype(BF)
        flat = flat + dot(wide, zero_one((128, 27), lambda r, l: (r < 16) & (l == 24 + c)).astype(BF))
    enc[...] = flat.reshape(16, 16, 27)
    copies[2].start()
    for c in copies:
        c.wait()


def all_of(*conds):
    total = None
    for c in conds:
        if c is not None:
            total = c if total is None else jnp.logical_and(total, c)
    return total


def span(step, size, halo):
    if step == 0:
        return (0, size), (halo, size)
    if step > 0:
        return (size - halo, halo), (0, halo)
    return (0, halo), (halo + size, halo)


def kernel(sizes, vc, enc_in, coarse_in, upt_in, dec_in, dec_out, vg_out, sum_out,
           enc_w, coarse_w, upt, dec_w, we, wd, wdb, wc, wcb, web, up, turn,
           vct, pk, er, vs, cs, skip, slope, jg, ughi, uglo, ug, ph, ps, act, uh, gh, gs, js, eh, es,
           gr, ar,
           vsend, vrecv, zsend, zrecv, psend, precv, gsend, grecv, usend, urecv, ssend, srecv, esend, erecv,
           asend, arecv, wsem):
    nx, ny, nz = sizes
    ix, iy, iz = (lax.axis_index(a) for a in AXES)
    depth, height, _, width = vc.shape
    chans = vc.shape[2] // 2
    cd, ch = depth // 2, height // 2

    def exists(step, index, count):
        return None if step == 0 else (index + step < count if step > 0 else index + step >= 0)

    def at(dx, dy, dz=0):
        return (ix + dx, iy + dy, iz + dz)

    def guarded(cond, f):
        if cond is None:
            f()
        else:
            pl.when(cond)(f)

    sends = [all_of(exists(dx, ix, nx), exists(dy, iy, ny)) for dx, dy in DIRS]
    recvs = [all_of(exists(-dx, ix, nx), exists(-dy, iy, ny)) for dx, dy in DIRS]
    ends = tuple((dx, dy, s) for s in (-1, 1) for dx in (-1, 0, 1) for dy in (-1, 0, 1))
    esends = [all_of(exists(dx, ix, nx), exists(dy, iy, ny), exists(dz, iz, nz)) for dx, dy, dz in ends]
    erecvs = [all_of(exists(-dx, ix, nx), exists(-dy, iy, ny), exists(-dz, iz, nz)) for dx, dy, dz in ends]

    cores = min(2, nx)
    lows, across = nx // cores, ny // 2 if ny > 4 else ny
    highs = ny // across
    core, y_low, x_at, y_high = lax.rem(ix, cores), ix // cores, lax.rem(iy, across), iy // across
    groups = (
        (cores * across, core * across + x_at,
         lambda j: (y_low * cores + j // across, y_high * across + lax.rem(j, across), iz)),
        (highs * lows, y_high * lows + y_low,
         lambda j: (lax.rem(j, lows) * cores + core, (j // lows) * across + x_at, iz)),
        (nz, iz, lambda j: (ix, iy, j)),
    )

    loads = [pltpu.make_async_copy(a, b, wsem.at[k]) for k, (a, b) in enumerate(
        ((enc_in, enc_w), (coarse_in, coarse_w), (upt_in, upt), (dec_in, dec_w)))]
    for c in loads:
        c.start()

    for ref in (vct, er, skip, ph, uh, gh, eh):
        ref[...] = jnp.zeros(ref.shape, ref.dtype)
    vct[1:1 + depth, 1:1 + height] = vc[...]
    barrier = pltpu.get_barrier_semaphore()

    def greet(device):
        pl.semaphore_signal(barrier, inc=1, device_id=device, device_id_type=MESH)

    for count, me, member in groups:
        for k in range(1, count):
            greet(member(lax.rem(me + k, count)))
    for dx, dy, dz in [d + (0,) for d in DIRS] + list(ends):
        if dx != 0 or dy != 0:
            guarded(all_of(exists(dx, ix, nx), exists(dy, iy, ny), exists(dz, iz, nz)),
                    lambda dx=dx, dy=dy, dz=dz: greet(at(dx, dy, dz)))

    def both(index, count):
        return (jnp.where(index > 0, 1, 0) + jnp.where(index < count - 1, 1, 0)).astype(jnp.int32)

    row = lax.broadcasted_iota(jnp.int32, (width, 2 * width), 0)
    lane = lax.broadcasted_iota(jnp.int32, (width, 2 * width), 1)
    total = jnp.zeros((depth * chans, 2 * width), F32)
    for n in range(2):
        for y in range(height):
            base = 64 * n + 8 * y
            pick = ((lane == base + row) & (row < 8)) | ((lane == width + base + row - 120) & (row >= 120))
            total = total + dot(vc[:, y, n * chans:(n + 1) * chans].reshape(depth * chans, width), pick.astype(BF))
    for side in range(2):
        pk[side] = total[:, side * width:(side + 1) * width].astype(BF).reshape(depth, chans, width)
    bx, by, bz = both(ix, nx), both(iy, ny), both(iz, nz)
    near = bx + by + bx * by
    pl.semaphore_wait(barrier, sum(count - 1 for count, _, _ in groups) + near + near * bz)

    def exchange(src, src_at, dst, dst_at, send_sem, recv_sem):
        copies = []
        for d, (dx, dy) in enumerate(DIRS):
            copies.append(pltpu.make_async_remote_copy(
                src_ref=src.at[src_at(dx, dy)], dst_ref=dst.at[dst_at(dx, dy)],
                send_sem=send_sem.at[d], recv_sem=recv_sem.at[d],
                device_id=at(dx, dy), device_id_type=MESH))
        return copies

    def begin(copies, conds):
        for c, s in zip(copies, conds):
            guarded(s, c.start)

    def landed(copies, conds):
        for c, r in zip(copies, conds):
            guarded(r, c.wait_recv)

    def left(copies, conds):
        for c, s in zip(copies, conds):
            guarded(s, c.wait_send)

    def rim_src(halo, d0, h0, off):
        def f(dx, dy):
            (a, n), _ = span(dx, d0, halo)
            (b, m), _ = span(dy, h0, halo)
            return (pl.ds(a + off, n), pl.ds(b + off, m))
        return f

    def rim_dst(halo, d0, h0):
        def f(dx, dy):
            _, (a, n) = span(dx, d0, halo)
            _, (b, m) = span(dy, h0, halo)
            return (pl.ds(a, n), pl.ds(b, m))
        return f

    vcopies = exchange(vc, rim_src(1, depth, height, 0), vct, rim_dst(1, depth, height), vsend, vrecv)
    begin(vcopies, sends)

    zcopies = []
    for d, (dx, dy, dz) in enumerate(ends):
        (a, n), (b, m) = span(dx, depth, 1)
        side = 1 if dz > 0 else 0
        zcopies.append(pltpu.make_async_remote_copy(
            src_ref=pk.at[side, pl.ds(a, n)], dst_ref=er.at[side, 1 - dy, pl.ds(b, m)],
            send_sem=zsend.at[d], recv_sem=zrecv.at[d],
            device_id=at(dx, dy, dz), device_id_type=MESH))
    begin(zcopies, esends)
    for c in loads:
        c.wait()
    arrange_weights(enc_w, coarse_w, upt, dec_w, we, wd, wdb, wc, wcb, web, up)
    landed(vcopies, recvs)
    landed(zcopies, erecvs)

    def shifted(wide, c):
        if c == 1:
            return wide
        return pltpu.roll(wide, 1 if c == 0 else wide.shape[1] - 1, 1)

    def fill_inputs(y, _):
        dyi, base = (y + 7) // 8, 8 * lax.rem(y + 7, 8)
        flat = ((depth + 2) * chans, width)
        kind, spot = lane // width, lax.rem(lane, width)
        source = base + 64 * kind + spot
        lo = (row == source - 120) & (spot >= 120)
        hi = (row == source) & (spot < 8)
        got = dot(er[1, dyi].reshape(flat), lo.astype(BF)) + dot(er[0, dyi].reshape(flat), hi.astype(BF))
        for n, ref in enumerate((vs, cs)):
            own = vct[:, y, n * chans:(n + 1) * chans].reshape(flat).astype(F32)
            wide = jnp.concatenate([own, got[:, n * width:(n + 1) * width]], axis=1)
            for c in range(3):
                ref[:, y, c] = shifted(wide, c).astype(BF).reshape(depth + 2, chans, 2 * width)

    lax.fori_loop(0, height + 2, fill_inputs, None)

    fine = lax.broadcasted_iota(jnp.int32, (1, 2 * width), 1)
    coarse = lax.broadcasted_iota(jnp.int32, (1, width), 1)
    low_ok = jnp.where(iz > 0, 1.0, 0.0).astype(F32)
    high_ok = jnp.where(iz < nz - 1, 1.0, 0.0).astype(F32)
    fine_mask = jnp.where(fine < width, 1.0, jnp.where(fine < 3 * width // 2, high_ok, low_ok))
    coarse_mask = jnp.where(coarse < width // 2, 1.0, jnp.where(coarse < 3 * width // 4, high_ok, low_ok))
    own_coarse = coarse < width // 2

    def conv_row(weight, planes, outs):
        m = weight.shape[0] // 3
        ys = [dot(weight, x) for x in planes]
        return [ys[p][:m] + ys[p + 1][m:2 * m] + ys[p + 2][2 * m:] for p in range(outs)]

    def enc_row(q, _):
        k = 9 * chans
        pre = conv_row(we[...], [vs[p, pl.ds(q, 3)].reshape(k, 2 * width) for p in range(depth + 2)], depth)
        for p in range(depth):
            t = pre[p]
            sig = 1.0 / (1.0 + jnp.exp(-t))
            skip[1 + p, 1 + q] = (t * sig * fine_mask).astype(BF)
            slope[p, q] = sig * (1.0 + t * (1.0 - sig)) * fine_mask

    lax.fori_loop(0, height, enc_row, None)

    pool = (lax.broadcasted_iota(jnp.int32, (2 * width, width), 0) // 2
            == lax.broadcasted_iota(jnp.int32, (2 * width, width), 1)).astype(BF)

    for q in range(ch):
        rows_in = skip[1:1 + depth, 1 + 2 * q:3 + 2 * q].reshape(depth * 2 * chans, 2 * width)
        half = dot(rows_in, pool).reshape(cd, 4, chans, width)
        ph[1:1 + cd, 1 + q] = ((half[:, 0] + half[:, 1] + half[:, 2] + half[:, 3]) * 0.125).astype(BF)
    pcopies = exchange(ph, rim_src(1, cd, ch, 1), ph, rim_dst(1, cd, ch), psend, precv)
    begin(pcopies, sends)
    scopies = exchange(skip, rim_src(1, depth, height, 1), skip, rim_dst(1, depth, height), ssend, srecv)
    begin(scopies, sends)

    def joined_row(q, _):
        k = 9 * chans
        sums = [jnp.zeros((chans, 2 * width), F32) for _ in range(cd)]
        for e in range(2):
            r = 2 * q + e
            out = conv_row(wdb[...], [cs[p, pl.ds(r, 3)].reshape(k, 2 * width) for p in range(depth + 2)], depth)
            for p in range(depth):
                jg[p, r] = out[p][:chans]
                sums[p // 2] = sums[p // 2] + out[p][chans:]
        for p in range(cd):
            hi = sums[p].astype(BF)
            ughi[p, q] = hi
            uglo[p, q] = (sums[p] - hi.astype(F32)).astype(BF)

    lax.fori_loop(0, ch, joined_row, None)
    flat = (cd * ch * chans, 2 * width)
    grad = dot(ughi[...].reshape(flat), pool) + dot(uglo[...].reshape(flat), pool)
    ug[...] = grad.astype(BF).reshape(ug.shape)

    landed(pcopies, recvs)

    def fill_pooled(q, _):
        wide = ph[:, q].reshape((cd + 2) * chans, width).astype(F32)
        for c in range(3):
            ps[:, q, c] = shifted(wide, c).astype(BF).reshape(cd + 2, chans, width)

    lax.fori_loop(0, ch + 2, fill_pooled, None)
    for q in range(ch):
        k = 9 * chans
        pre = conv_row(wc[...], [ps[p, q:q + 3].reshape(k, width) for p in range(cd + 2)], cd)
        for p in range(cd):
            t = pre[p]
            sig = 1.0 / (1.0 + jnp.exp(-t))
            a = (t * sig * coarse_mask).astype(BF)
            act[p, q] = a
            uh[1 + p, 1 + q] = dot(upt[...], a).astype(BF)
            back = dot(up[...], ug[p, q])
            gh[1 + p, 1 + q] = (back * (sig * (1.0 + t * (1.0 - sig)) * coarse_mask)).astype(BF)

    gcopies = exchange(gh, rim_src(1, cd, ch, 1), gh, rim_dst(1, cd, ch), gsend, grecv)
    begin(gcopies, sends)
    ucopies = exchange(uh, rim_src(1, cd, ch, 1), uh, rim_dst(1, cd, ch), usend, urecv)
    begin(ucopies, sends)

    group16 = lax.broadcasted_iota(jnp.int32, (1, width), 1) // 16
    group32 = lax.broadcasted_iota(jnp.int32, (1, width), 1) // 32

    def tap_sums(block, step, groups, gid):
        out = []
        for b in range(3):
            total = jnp.zeros((step, width), F32)
            for q in range(groups):
                total = jnp.where(gid == q, block[(q + b) * step:(q + b + 1) * step], total)
            size = width // 2
            while size >= width // groups:
                total = total + pltpu.roll(total, size, 1)
                size //= 2
            out.append(total)
        return out

    def put(first, value):
        gr[first // 16:first // 16 + 3] = value.astype(BF).reshape(3, 16, width)

    tail = jnp.zeros((3 * chans, width), F32)
    step = 3 * chans
    taps = []
    masked = [jnp.where(own_coarse, gh[1 + p, 1:1 + ch].reshape(2 * chans * ch, width), 0)
              for p in range(cd)]
    for a in range(3):
        block = sum(dot_nt(ps[p + a].reshape((ch + 2) * step, width), masked[p]) for p in range(cd))
        taps += tap_sums(block, step, ch, group32)
    for half in range(2):
        total = jnp.zeros((step, width), F32)
        for g in range(4):
            total = jnp.where(group32 == g, taps[4 * half + g], total)
        put(144 + 48 * half, total)
    tail = jnp.where(group32 == 2, taps[8], tail)
    up_total = jnp.zeros((2 * chans, width), F32)
    for p in range(cd):
        for q in range(ch):
            g = jnp.where(own_coarse, ug[p, q], 0)
            up_total = up_total + dot_nt(act[p, q], jnp.concatenate([g] * 8, axis=0))
    up_total = jnp.concatenate([up_total, jnp.zeros((chans, width), F32)], axis=0)
    tail = jnp.where(group16 == 3, up_total, tail)

    def fill_skip(first, count, y):
        wide = skip[first:first + count, y].reshape(count * chans, 2 * width).astype(F32)
        for c in range(3):
            part = shifted(wide, c)[:, :width]
            js[first:first + count, y, c, 0:chans] = part.astype(BF).reshape(count, chans, width)

    lax.fori_loop(1, height + 1, lambda y, _: fill_skip(1, depth, y), None)
    landed(scopies, recvs)
    for y in (0, height + 1):
        fill_skip(0, depth + 2, y)

    def fill_sides(y, _):
        fill_skip(0, 1, y)
        fill_skip(depth + 1, 1, y)

    lax.fori_loop(1, height + 1, fill_sides, None)

    def fine_taps(source, step, grads):
        taps = []
        for a in range(3):
            block = sum(dot_nt(source(a + p), grads[p]) for p in range(depth))
            taps += tap_sums(block, step, height, group16)
        total = jnp.zeros((step, width), F32)
        for g in range(8):
            total = jnp.where(group16 == g, taps[g], total)
        return total, taps[8]

    def joined_taps(first):
        return fine_taps(
            lambda x: js[x, :, :, first:first + chans].reshape((height + 2) * 3 * chans, width), 3 * chans,
            [vc[p, :, chans:2 * chans].reshape(height * chans, width) for p in range(depth)])

    total, last = joined_taps(0)
    put(48, total)
    tail = jnp.where(group16 == 1, last, tail)
    landed(gcopies, recvs)

    def fill_coarse(y, _):
        wide = gh[:, y].reshape((cd + 2) * 2 * chans, width).astype(F32)
        for c in range(3):
            gs[:, y, c] = shifted(wide, c).astype(BF).reshape(cd + 2, 2 * chans, width)

    lax.fori_loop(0, ch + 2, fill_coarse, None)
    spread = (lax.broadcasted_iota(jnp.int32, (width, 2 * width), 1) // 2
              == lax.broadcasted_iota(jnp.int32, (width, 2 * width), 0)).astype(BF)

    def back_row(q, _):
        k = 18 * chans
        pg = conv_row(wcb[...], [gs[p, pl.ds(q, 3)].reshape(k, width) for p in range(cd + 2)], cd)
        for p in range(cd):
            v = pg[p] * 0.125
            hi = v.astype(BF)
            lo = (v - hi.astype(F32)).astype(BF)
            wide = dot(hi, spread) + dot(lo, spread)
            for e in range(2):
                for f in range(2):
                    g = (jg[2 * p + e, 2 * q + f] + wide) * slope[2 * p + e, 2 * q + f]
                    eh[1 + 2 * p + e, 1 + 2 * q + f] = g.astype(BF)

    lax.fori_loop(0, ch, back_row, None)
    ecopies = exchange(eh, rim_src(1, depth, height, 1), eh, rim_dst(1, depth, height), esend, erecv)
    begin(ecopies, sends)

    landed(ucopies, recvs)
    low = lax.broadcasted_iota(jnp.int32, (width, width), 0)
    lane = lax.broadcasted_iota(jnp.int32, (width, width), 1)
    for c in range(3):
        source = lax.rem(lane + (c - 1) + 2 * width, 2 * width) // 2
        pick = (low == source).astype(BF)
        wide = dot(uh[...].reshape((cd + 2) * (ch + 2) * chans, width), pick)
        wide = wide.astype(BF).reshape(cd + 2, ch + 2, chans, width)
        for x in range(depth + 2):
            for y in range(height + 2):
                js[x, y, c, chans:2 * chans] = wide[(x + 1) // 2, (y + 1) // 2]

    total, last = joined_taps(chans)
    put(96, total)
    tail = jnp.where(group16 == 2, last, tail)
    total, last = fine_taps(
        lambda x: vs[x, :, :, :, 0:width].reshape((height + 2) * 3 * chans, width), 3 * chans,
        [eh[1 + p, 1:1 + height, :, 0:width].reshape(height * chans, width) for p in range(depth)])
    put(0, total)
    tail = jnp.where(group16 == 0, last, tail)
    put(240, tail)
    used = 288 // 16
    if gr.shape[0] > used:
        gr[used:] = jnp.zeros((gr.shape[0] - used, 16, width), BF)

    per = gr.shape[0] // groups[0][0]

    def ring(phase):
        count, me, member = groups[phase % 3]
        out, got = [], []
        for k in range(1, count):
            to = lax.rem(me + k, count)
            frm = lax.rem(me - k + count, count)
            src = gr.at[pl.ds(to * per, per)] if phase == 0 else ar.at[phase, me]

            def copy(slot):
                return pltpu.make_async_remote_copy(
                    src_ref=src, dst_ref=ar.at[phase, slot], send_sem=asend.at[phase, k - 1],
                    recv_sem=arecv.at[phase, k - 1], device_id=member(to), device_id_type=MESH)

            out.append(copy(me))
            got.append(copy(frm))
        for c in out:
            c.start()
        return out, got

    def advance(copies, phase):
        for c in copies[1]:
            c.wait_recv()
        total = ar[phase, 0].astype(F32)
        for k in range(1, groups[phase][0]):
            total = total + ar[phase, k].astype(F32)
        ar[phase + 1, groups[(phase + 1) % 3][1]] = total.astype(BF)
        return ring(phase + 1)

    first = ring(0)
    ar[0, groups[0][1]] = gr[pl.ds(groups[0][1] * per, per)]

    order = zero_one((height * chans, height * chans),
                     lambda r, l: (r // height == l % chans) & (r % height == l // chans)).astype(BF)

    def channels_first(which, ref):
        for p in range(depth):
            moved = dot(order, turn[which, p].reshape(height * chans, width))
            ref[:, p] = moved.reshape(chans, height, width).astype(BF)

    def dec_row(q, _):
        k = 18 * chans
        out = conv_row(wd[...], [js[p, pl.ds(q, 3)].reshape(k, width) for p in range(depth + 2)], depth)
        for p in range(depth):
            turn[0, p, q] = out[p].astype(BF)

    lax.fori_loop(0, height // 2, dec_row, None)

    second = advance(first, 0)
    lax.fori_loop(height // 2, height, dec_row, None)
    channels_first(0, dec_out)
    landed(ecopies, recvs)

    def fill_enc(y, _):
        wide = eh[:, y].reshape((depth + 2) * chans, 2 * width).astype(F32)
        for c in range(3):
            part = shifted(wide, c)[:, :width]
            es[:, y, c] = part.astype(BF).reshape(depth + 2, chans, width)

    lax.fori_loop(0, height + 2, fill_enc, None)

    def vol_row(q, _):
        k = 9 * chans
        out = conv_row(web[...], [es[p, pl.ds(q, 3)].reshape(k, width) for p in range(depth + 2)], depth)
        for p in range(depth):
            turn[1, p, q] = out[p].astype(BF)

    third = advance(second, 1)
    lax.fori_loop(0, height // 2, vol_row, None)
    fourth = advance(third, 2)
    lax.fori_loop(height // 2, height, vol_row, None)
    channels_first(1, vg_out)
    for c in fourth[1]:
        c.wait_recv()
    sum_out[...] = ar[3, 0:groups[0][0]].reshape(sum_out.shape)

    left(zcopies, esends)
    for copies in (vcopies, pcopies, gcopies, ucopies, scopies, ecopies):
        left(copies, sends)
    for copies in (first, second, third, fourth):
        for c in copies[0]:
            c.wait_send()


def per_device(sizes, volume, enc_weight, coarse_weight, up_weight, dec_weight, cotangent):
    nx, ny, nz = sizes
    chans, d, h, w = volume.shape
    cd, ch = d // 2, h // 2
    owners = min(2, nx) * (ny // 2 if ny > 4 else ny)
    per = -(-18 // owners)
    pair = jnp.transpose(jnp.concatenate([volume, cotangent], axis=0), (1, 2, 0, 3))
    operands = (
        pair, jnp.transpose(enc_weight, (1, 2, 0)), coarse_weight, up_weight.T, jnp.transpose(dec_weight, (0, 2, 1)))
    c2 = 2 * chans
    widest = max(owners, nx * ny // owners, nz) - 1
    scratch = [
        ((16, 16, 27), BF),
        ((27, 16, 32), BF),
        ((16, 32), BF),
        ((27, 16, 32), BF),
        ((48, 144), BF),
        ((48, 288), BF),
        ((96, 144), BF),
        ((96, 144), BF),
        ((48, 288), BF),
        ((48, 144), BF),
        ((32, 16), BF),
        ((2, d, h, chans, w), BF),
        ((d + 2, h + 2, c2, w), BF),
        ((2, d, chans, w), BF),
        ((2, 3, d + 2, chans, w), BF),
        ((d + 2, h + 2, 3, chans, 2 * w), BF),
        ((d + 2, h + 2, 3, chans, 2 * w), BF),
        ((d + 2, h + 2, chans, 2 * w), BF),
        ((d, h, chans, 2 * w), F32),
        ((d, h, chans, 2 * w), F32),
        ((cd, ch, chans, 2 * w), BF),
        ((cd, ch, chans, 2 * w), BF),
        ((cd, ch, chans, w), BF),
        ((cd + 2, ch + 2, chans, w), BF),
        ((cd + 2, ch + 2, 3, chans, w), BF),
        ((cd, ch, c2, w), BF),
        ((cd + 2, ch + 2, chans, w), BF),
        ((cd + 2, ch + 2, c2, w), BF),
        ((cd + 2, ch + 2, 3, c2, w), BF),
        ((d + 2, h + 2, 3, c2, w), BF),
        ((d + 2, h + 2, chans, 2 * w), BF),
        ((d + 2, h + 2, 3, chans, w), BF),
        ((owners * per, 16, w), BF),
        ((4, widest + 1, per, 16, w), BF),
    ]
    dma = pltpu.SemaphoreType.DMA
    sems = [dma((8,))] * 2 + [dma((18,))] * 2 + [dma((8,))] * 10 + [dma((4, max(widest, 1)))] * 2 + [dma((4,))]
    hbm = pl.BlockSpec(memory_space=pl.ANY)
    vmem = pl.BlockSpec(memory_space=pltpu.VMEM)
    dec, vg, total = pl.pallas_call(
        functools.partial(kernel, sizes),
        out_shape=(
            jax.ShapeDtypeStruct((chans, d, h, w), BF),
            jax.ShapeDtypeStruct((chans, d, h, w), BF),
            jax.ShapeDtypeStruct((owners * per, 16, w), BF)),
        in_specs=[vmem] + [hbm] * 4,
        out_specs=(vmem,) * 3,
        scratch_shapes=[pltpu.VMEM(s, t) for s, t in scratch] + sems,
        compiler_params=pltpu.CompilerParams(
            collective_id=0, has_side_effects=True, vmem_limit_bytes=48 * 1024 * 1024),
    )(*operands)
    grads = ((16, 16, 27), (27, 16, 32), (16, 32), (27, 16, 32))
    dec, vg, enc, coarse, upg, decg = pl.pallas_call(
        finish,
        out_shape=tuple(jax.ShapeDtypeStruct(x.shape, BF) for x in (dec, vg))
        + tuple(jax.ShapeDtypeStruct(x, F32) for x in grads),
        in_specs=[vmem] * 3,
        out_specs=(hbm,) * 6,
        scratch_shapes=[pltpu.VMEM(x, F32) for x in grads] + [dma((6,))],
        compiler_params=pltpu.CompilerParams(vmem_limit_bytes=8 * 1024 * 1024),
    )(dec, vg, total)
    return (dec, vg, jnp.transpose(enc, (2, 0, 1)), coarse, upg.T, jnp.transpose(decg, (0, 2, 1)))


def solution(mesh):
    sizes = tuple(mesh.shape[a] for a in AXES)
    spec = P(None, "gx", "gy", "gz")
    return jax.shard_map(
        functools.partial(per_device, sizes),
        mesh=mesh,
        in_specs=(spec, P(), P(), P(), P(), spec),
        out_specs=(spec, spec, P(), P(), P(), P()),
        check_vma=False,
    )
```

```python
import functools

import jax
import jax.numpy as jnp
from jax import lax
from jax.experimental import pallas as pl
from jax.experimental.pallas import tpu as pltpu
from jax.sharding import PartitionSpec as P

AXES = ("gx", "gy", "gz")
BF = jnp.bfloat16
F32 = jnp.float32
MESH = pl.DeviceIdType.MESH
DIRS = tuple((dx, dy) for dy in (-1, 1, 0) for dx in (-1, 1, 0) if (dx, dy) != (0, 0))


def dot(a, b):
    return jnp.dot(a, b, preferred_element_type=F32)


def dot_nt(a, b):
    return lax.dot_general(a, b, (((1,), (1,)), ((), ())), preferred_element_type=F32)


def dot_tn(a, b):
    return lax.dot_general(a, b, (((0,), (0,)), ((), ())), preferred_element_type=F32)


def zero_one(shape, rule):
    return rule(lax.broadcasted_iota(jnp.int32, shape, 0), lax.broadcasted_iota(jnp.int32, shape, 1))


def arrange_weights(enc, coarse, upt, dec, we, wd, wdb, wc, wcb, web, up):
    flat = enc[...].reshape(256, 27)
    same_in = zero_one((256, 144), lambda r, l: r // 16 == l % 16)
    same_out = zero_one((256, 144), lambda r, l: r % 16 == l % 16)
    fold_in = zero_one((16, 256), lambda r, l: r == l % 16).astype(BF)
    fold_out = zero_one((16, 256), lambda r, l: r == l // 16).astype(BF)
    for a in range(3):
        ahead = dot(flat, zero_one((27, 144), lambda r, l: r == 9 * a + l // 16).astype(BF))
        we[16 * a:16 * a + 16] = dot(fold_in, jnp.where(same_in, ahead, 0.0).astype(BF)).astype(BF)
        back = dot(flat, zero_one((27, 144), lambda r, l: r == 26 - 9 * a - l // 16).astype(BF))
        web[16 * a:16 * a + 16] = dot(fold_out, jnp.where(same_out, back, 0.0).astype(BF)).astype(BF)
    totals = [0.0] * 4
    for t in range(9):
        wide = zero_one((32, 288), lambda r, l: l == 32 * t + r).astype(BF)
        slim = zero_one((16, 144), lambda r, l: l == 16 * t + r).astype(BF)
        ahead, back = (t, 9 + t, 18 + t), (26 - t, 17 - t, 8 - t)
        totals[0] += dot(jnp.concatenate([dec[k] for k in ahead], axis=0), wide)
        totals[1] += dot_tn(jnp.concatenate([dec[k] for k in back], axis=1), slim)
        totals[2] += dot_tn(jnp.concatenate([coarse[k] for k in ahead], axis=1), slim)
        totals[3] += dot(jnp.concatenate([coarse[k] for k in back], axis=0), wide)
    for ref, total in zip((wd, wdb, wc, wcb), totals):
        ref[...] = total.astype(BF)
    up[...] = dot_tn(upt[...], zero_one((16, 16), lambda r, l: r == l).astype(BF)).astype(BF)


def finish(dec, vg, total, dec_out, vg_out, enc_out, coarse_out, up_out, decg_out,
           enc, coarse, up, decg, sems):
    copies = [pltpu.make_async_copy(a, b, sems.at[k]) for k, (a, b) in enumerate(
        ((dec, dec_out), (vg, vg_out), (enc, enc_out), (coarse, coarse_out), (up, up_out), (decg, decg_out)))]
    copies[0].start()
    copies[1].start()

    def rows(first, count):
        return total[first // 16:(first + count) // 16].reshape(count, 128)

    eye = zero_one((128, 128), lambda r, l: r == l).astype(BF)
    for c in range(3):
        last = rows(240 + 16 * c, 16)
        block = jnp.concatenate([rows(48 + 16 * c, 16), rows(96 + 16 * c, 16)], axis=0)
        turned = dot_nt(eye, block).reshape(8, 16, 32)
        for g in range(8):
            decg[3 * g + c] = turned[g]
        skip_last = dot_nt(zero_one((16, 128), lambda r, l: l == 16 + r).astype(BF), last)
        upper_last = dot_nt(zero_one((16, 128), lambda r, l: l == 32 + r).astype(BF), last)
        decg[24 + c] = jnp.concatenate([skip_last, upper_last], axis=1)
    copies[5].start()
    for c in range(3):
        for half in range(2):
            block = rows(144 + 48 * half + 16 * c, 16)
            for g in range(4):
                pick = zero_one((128, 32), lambda r, l: r == 32 * g + l).astype(BF)
                coarse[3 * (4 * half + g) + c] = dot(block, pick)
        pick = zero_one((128, 32), lambda r, l: r == 64 + l).astype(BF)
        coarse[24 + c] = dot(rows(240 + 16 * c, 16), pick)
    copies[3].start()
    up[...] = dot_nt(zero_one((16, 128), lambda r, l: l == 48 + r).astype(BF), rows(240, 32))
    copies[4].start()
    grow = zero_one((256, 16), lambda r, l: l == r // 16).astype(BF)
    same = zero_one((256, 128), lambda r, l: r % 16 == l % 16)
    flat = jnp.zeros((256, 27), F32)
    for c in range(3):
        wide = jnp.where(same, dot(grow, rows(16 * c, 16)), 0.0).astype(BF)
        flat = flat + dot(wide, zero_one((128, 27), lambda r, l: l == 3 * (r // 16) + c).astype(BF))
        wide = jnp.where(same, dot(grow, rows(240 + 16 * c, 16)), 0.0).astype(BF)
        flat = flat + dot(wide, zero_one((128, 27), lambda r, l: (r < 16) & (l == 24 + c)).astype(BF))
    enc[...] = flat.reshape(16, 16, 27)
    copies[2].start()
    for c in copies:
        c.wait()


def all_of(*conds):
    total = None
    for c in conds:
        if c is not None:
            total = c if total is None else jnp.logical_and(total, c)
    return total


def span(step, size, halo):
    if step == 0:
        return (0, size), (halo, size)
    if step > 0:
        return (size - halo, halo), (0, halo)
    return (0, halo), (halo + size, halo)


def kernel(sizes, vc, enc_in, coarse_in, upt_in, dec_in, dec_out, vg_out, sum_out,
           enc_w, coarse_w, upt, dec_w, we, wd, wdb, wc, wcb, web, up, turn,
           vct, pk, er, vs, cs, skip, slope, jg, ughi, uglo, ug, ph, ps, act, uh, gh, gs, js, eh, es,
           gr, ar,
           vsend, vrecv, zsend, zrecv, psend, precv, gsend, grecv, usend, urecv, ssend, srecv, esend, erecv,
           asend, arecv, wsem):
    nx, ny, nz = sizes
    ix, iy, iz = (lax.axis_index(a) for a in AXES)
    depth, height, _, width = vc.shape
    chans = vc.shape[2] // 2
    cd, ch = depth // 2, height // 2

    def exists(step, index, count):
        return None if step == 0 else (index + step < count if step > 0 else index + step >= 0)

    def at(dx, dy, dz=0):
        return (ix + dx, iy + dy, iz + dz)

    def guarded(cond, f):
        if cond is None:
            f()
        else:
            pl.when(cond)(f)

    sends = [all_of(exists(dx, ix, nx), exists(dy, iy, ny)) for dx, dy in DIRS]
    recvs = [all_of(exists(-dx, ix, nx), exists(-dy, iy, ny)) for dx, dy in DIRS]
    ends = tuple((dx, dy, s) for dy in (-1, 1, 0) for dx in (-1, 1, 0) for s in (-1, 1))
    esends = [all_of(exists(dx, ix, nx), exists(dy, iy, ny), exists(dz, iz, nz)) for dx, dy, dz in ends]
    erecvs = [all_of(exists(-dx, ix, nx), exists(-dy, iy, ny), exists(-dz, iz, nz)) for dx, dy, dz in ends]

    cores = min(2, nx)
    lows, across = nx // cores, ny // 2 if ny > 4 else ny
    highs = ny // across
    core, y_low, x_at, y_high = lax.rem(ix, cores), ix // cores, lax.rem(iy, across), iy // across
    groups = (
        (cores * across, core * across + x_at,
         lambda j: (y_low * cores + j // across, y_high * across + lax.rem(j, across), iz)),
        (highs * lows, y_high * lows + y_low,
         lambda j: (lax.rem(j, lows) * cores + core, (j // lows) * across + x_at, iz)),
        (nz, iz, lambda j: (ix, iy, j)),
    )

    loads = [pltpu.make_async_copy(a, b, wsem.at[k]) for k, (a, b) in enumerate(
        ((enc_in, enc_w), (coarse_in, coarse_w), (upt_in, upt), (dec_in, dec_w)))]
    for c in loads:
        c.start()

    for ref in (vct, er, skip, ph, uh, gh, eh):
        ref[...] = jnp.zeros(ref.shape, ref.dtype)
    vct[1:1 + depth, 1:1 + height] = vc[...]
    barrier = pltpu.get_barrier_semaphore()

    def greet(device):
        pl.semaphore_signal(barrier, inc=1, device_id=device, device_id_type=MESH)

    for count, me, member in groups:
        for k in range(1, count):
            greet(member(lax.rem(me + k, count)))
    for dx, dy, dz in [d + (0,) for d in DIRS] + list(ends):
        if dx != 0 or dy != 0:
            guarded(all_of(exists(dx, ix, nx), exists(dy, iy, ny), exists(dz, iz, nz)),
                    lambda dx=dx, dy=dy, dz=dz: greet(at(dx, dy, dz)))

    def both(index, count):
        return (jnp.where(index > 0, 1, 0) + jnp.where(index < count - 1, 1, 0)).astype(jnp.int32)

    row = lax.broadcasted_iota(jnp.int32, (width, 2 * width), 0)
    lane = lax.broadcasted_iota(jnp.int32, (width, 2 * width), 1)
    total = jnp.zeros((depth * chans, 2 * width), F32)
    for n in range(2):
        for y in range(height):
            base = 64 * n + 8 * y
            pick = ((lane == base + row) & (row < 8)) | ((lane == width + base + row - 120) & (row >= 120))
            total = total + dot(vc[:, y, n * chans:(n + 1) * chans].reshape(depth * chans, width), pick.astype(BF))
    for side in range(2):
        pk[side] = total[:, side * width:(side + 1) * width].astype(BF).reshape(depth, chans, width)
    bx, by, bz = both(ix, nx), both(iy, ny), both(iz, nz)
    near = bx + by + bx * by
    pl.semaphore_wait(barrier, sum(count - 1 for count, _, _ in groups) + near + near * bz)

    def exchange(src, src_at, dst, dst_at, send_sem, recv_sem):
        copies = []
        for d, (dx, dy) in enumerate(DIRS):
            copies.append(pltpu.make_async_remote_copy(
                src_ref=src.at[src_at(dx, dy)], dst_ref=dst.at[dst_at(dx, dy)],
                send_sem=send_sem.at[d], recv_sem=recv_sem.at[d],
                device_id=at(dx, dy), device_id_type=MESH))
        return copies

    def begin(copies, conds):
        for c, s in zip(copies, conds):
            guarded(s, c.start)

    def landed(copies, conds):
        for c, r in zip(copies, conds):
            guarded(r, c.wait_recv)

    def landed_rows(copies, conds, dirs, rim):
        part = [i for i, d in enumerate(dirs) if (d[1] != 0) == rim]
        landed([copies[i] for i in part], [conds[i] for i in part])

    def left(copies, conds):
        for c, s in zip(copies, conds):
            guarded(s, c.wait_send)

    def rim_src(halo, d0, h0, off):
        def f(dx, dy):
            (a, n), _ = span(dx, d0, halo)
            (b, m), _ = span(dy, h0, halo)
            return (pl.ds(a + off, n), pl.ds(b + off, m))
        return f

    def rim_dst(halo, d0, h0):
        def f(dx, dy):
            _, (a, n) = span(dx, d0, halo)
            _, (b, m) = span(dy, h0, halo)
            return (pl.ds(a, n), pl.ds(b, m))
        return f

    vcopies = exchange(vc, rim_src(1, depth, height, 0), vct, rim_dst(1, depth, height), vsend, vrecv)
    begin(vcopies, sends)

    zcopies = []
    for d, (dx, dy, dz) in enumerate(ends):
        (a, n), (b, m) = span(dx, depth, 1)
        side = 1 if dz > 0 else 0
        zcopies.append(pltpu.make_async_remote_copy(
            src_ref=pk.at[side, pl.ds(a, n)], dst_ref=er.at[side, 1 - dy, pl.ds(b, m)],
            send_sem=zsend.at[d], recv_sem=zrecv.at[d],
            device_id=at(dx, dy, dz), device_id_type=MESH))
    begin(zcopies, esends)
    for c in loads:
        c.wait()
    arrange_weights(enc_w, coarse_w, upt, dec_w, we, wd, wdb, wc, wcb, web, up)

    def shifted(wide, c):
        if c == 1:
            return wide
        return pltpu.roll(wide, 1 if c == 0 else wide.shape[1] - 1, 1)

    def fill_inputs(y, _):
        dyi, base = (y + 7) // 8, 8 * lax.rem(y + 7, 8)
        flat = ((depth + 2) * chans, width)
        kind, spot = lane // width, lax.rem(lane, width)
        source = base + 64 * kind + spot
        lo = (row == source - 120) & (spot >= 120)
        hi = (row == source) & (spot < 8)
        got = dot(er[1, dyi].reshape(flat), lo.astype(BF)) + dot(er[0, dyi].reshape(flat), hi.astype(BF))
        for n, ref in enumerate((vs, cs)):
            own = vct[:, y, n * chans:(n + 1) * chans].reshape(flat).astype(F32)
            wide = jnp.concatenate([own, got[:, n * width:(n + 1) * width]], axis=1)
            for c in range(3):
                ref[:, y, c] = shifted(wide, c).astype(BF).reshape(depth + 2, chans, 2 * width)


    fine = lax.broadcasted_iota(jnp.int32, (1, 2 * width), 1)
    coarse = lax.broadcasted_iota(jnp.int32, (1, width), 1)
    low_ok = jnp.where(iz > 0, 1.0, 0.0).astype(F32)
    high_ok = jnp.where(iz < nz - 1, 1.0, 0.0).astype(F32)
    fine_mask = jnp.where(fine < width, 1.0, jnp.where(fine < 3 * width // 2, high_ok, low_ok))
    coarse_mask = jnp.where(coarse < width // 2, 1.0, jnp.where(coarse < 3 * width // 4, high_ok, low_ok))
    own_coarse = coarse < width // 2

    def conv_row(weight, planes, outs):
        m = weight.shape[0] // 3
        ys = [dot(weight, x) for x in planes]
        return [ys[p][:m] + ys[p + 1][m:2 * m] + ys[p + 2][2 * m:] for p in range(outs)]

    def enc_row(q, _):
        k = 9 * chans
        pre = conv_row(we[...], [vs[p, pl.ds(q, 3)].reshape(k, 2 * width) for p in range(depth + 2)], depth)
        for p in range(depth):
            t = pre[p]
            sig = 1.0 / (1.0 + jnp.exp(-t))
            skip[1 + p, 1 + q] = (t * sig * fine_mask).astype(BF)
            slope[p, q] = sig * (1.0 + t * (1.0 - sig)) * fine_mask

    landed_rows(zcopies, erecvs, ends, False)
    landed_rows(vcopies, recvs, DIRS, False)
    lax.fori_loop(1, height + 1, fill_inputs, None)
    lax.fori_loop(1, height - 1, enc_row, None)
    landed_rows(zcopies, erecvs, ends, True)
    landed_rows(vcopies, recvs, DIRS, True)
    for y in (0, height + 1):
        fill_inputs(y, None)
    for q in (0, height - 1):
        enc_row(q, None)

    pool = (lax.broadcasted_iota(jnp.int32, (2 * width, width), 0) // 2
            == lax.broadcasted_iota(jnp.int32, (2 * width, width), 1)).astype(BF)

    for q in range(ch):
        rows_in = skip[1:1 + depth, 1 + 2 * q:3 + 2 * q].reshape(depth * 2 * chans, 2 * width)
        half = dot(rows_in, pool).reshape(cd, 4, chans, width)
        ph[1:1 + cd, 1 + q] = ((half[:, 0] + half[:, 1] + half[:, 2] + half[:, 3]) * 0.125).astype(BF)
    pcopies = exchange(ph, rim_src(1, cd, ch, 1), ph, rim_dst(1, cd, ch), psend, precv)
    begin(pcopies, sends)
    scopies = exchange(skip, rim_src(1, depth, height, 1), skip, rim_dst(1, depth, height), ssend, srecv)
    begin(scopies, sends)

    def joined_row(q, _):
        k = 9 * chans
        sums = [jnp.zeros((chans, 2 * width), F32) for _ in range(cd)]
        for e in range(2):
            r = 2 * q + e
            out = conv_row(wdb[...], [cs[p, pl.ds(r, 3)].reshape(k, 2 * width) for p in range(depth + 2)], depth)
            for p in range(depth):
                jg[p, r] = out[p][:chans]
                sums[p // 2] = sums[p // 2] + out[p][chans:]
        for p in range(cd):
            hi = sums[p].astype(BF)
            ughi[p, q] = hi
            uglo[p, q] = (sums[p] - hi.astype(F32)).astype(BF)

    lax.fori_loop(0, ch, joined_row, None)
    flat = (cd * ch * chans, 2 * width)
    grad = dot(ughi[...].reshape(flat), pool) + dot(uglo[...].reshape(flat), pool)
    ug[...] = grad.astype(BF).reshape(ug.shape)

    def fill_pooled(q, _):
        wide = ph[:, q].reshape((cd + 2) * chans, width).astype(F32)
        for c in range(3):
            ps[:, q, c] = shifted(wide, c).astype(BF).reshape(cd + 2, chans, width)

    landed_rows(pcopies, recvs, DIRS, False)
    lax.fori_loop(1, ch + 1, fill_pooled, None)
    def coarse_row(q):
        k = 9 * chans
        pre = conv_row(wc[...], [ps[p, q:q + 3].reshape(k, width) for p in range(cd + 2)], cd)
        for p in range(cd):
            t = pre[p]
            sig = 1.0 / (1.0 + jnp.exp(-t))
            a = (t * sig * coarse_mask).astype(BF)
            act[p, q] = a
            uh[1 + p, 1 + q] = dot(upt[...], a).astype(BF)
            back = dot(up[...], ug[p, q])
            gh[1 + p, 1 + q] = (back * (sig * (1.0 + t * (1.0 - sig)) * coarse_mask)).astype(BF)

    for q in range(1, ch - 1):
        coarse_row(q)
    landed_rows(pcopies, recvs, DIRS, True)
    for q in (0, ch + 1):
        fill_pooled(q, None)
    for q in (0, ch - 1):
        coarse_row(q)
    gcopies = exchange(gh, rim_src(1, cd, ch, 1), gh, rim_dst(1, cd, ch), gsend, grecv)
    begin(gcopies, sends)
    ucopies = exchange(uh, rim_src(1, cd, ch, 1), uh, rim_dst(1, cd, ch), usend, urecv)
    begin(ucopies, sends)

    group16 = lax.broadcasted_iota(jnp.int32, (1, width), 1) // 16
    group32 = lax.broadcasted_iota(jnp.int32, (1, width), 1) // 32

    def tap_sums(block, step, groups, gid):
        out = []
        for b in range(3):
            total = jnp.zeros((step, width), F32)
            for q in range(groups):
                total = jnp.where(gid == q, block[(q + b) * step:(q + b + 1) * step], total)
            size = width // 2
            while size >= width // groups:
                total = total + pltpu.roll(total, size, 1)
                size //= 2
            out.append(total)
        return out

    def put(first, value):
        gr[first // 16:first // 16 + 3] = value.astype(BF).reshape(3, 16, width)

    tail = jnp.zeros((3 * chans, width), F32)
    step = 3 * chans
    taps = []
    masked = [jnp.where(own_coarse, gh[1 + p, 1:1 + ch].reshape(2 * chans * ch, width), 0)
              for p in range(cd)]
    for a in range(3):
        block = sum(dot_nt(ps[p + a].reshape((ch + 2) * step, width), masked[p]) for p in range(cd))
        taps += tap_sums(block, step, ch, group32)
    for half in range(2):
        total = jnp.zeros((step, width), F32)
        for g in range(4):
            total = jnp.where(group32 == g, taps[4 * half + g], total)
        put(144 + 48 * half, total)
    tail = jnp.where(group32 == 2, taps[8], tail)
    up_total = jnp.zeros((2 * chans, width), F32)
    for p in range(cd):
        for q in range(ch):
            g = jnp.where(own_coarse, ug[p, q], 0)
            up_total = up_total + dot_nt(act[p, q], jnp.concatenate([g] * 8, axis=0))
    up_total = jnp.concatenate([up_total, jnp.zeros((chans, width), F32)], axis=0)
    tail = jnp.where(group16 == 3, up_total, tail)

    def fill_skip(first, count, y):
        wide = skip[first:first + count, y].reshape(count * chans, 2 * width).astype(F32)
        for c in range(3):
            part = shifted(wide, c)[:, :width]
            js[first:first + count, y, c, 0:chans] = part.astype(BF).reshape(count, chans, width)

    lax.fori_loop(1, height + 1, lambda y, _: fill_skip(1, depth, y), None)
    landed(scopies, recvs)
    for y in (0, height + 1):
        fill_skip(0, depth + 2, y)

    def fill_sides(y, _):
        fill_skip(0, 1, y)
        fill_skip(depth + 1, 1, y)

    lax.fori_loop(1, height + 1, fill_sides, None)

    def fine_taps(source, step, grads):
        taps = []
        for a in range(3):
            block = sum(dot_nt(source(a + p), grads[p]) for p in range(depth))
            taps += tap_sums(block, step, height, group16)
        total = jnp.zeros((step, width), F32)
        for g in range(8):
            total = jnp.where(group16 == g, taps[g], total)
        return total, taps[8]

    def joined_taps(first):
        return fine_taps(
            lambda x: js[x, :, :, first:first + chans].reshape((height + 2) * 3 * chans, width), 3 * chans,
            [vc[p, :, chans:2 * chans].reshape(height * chans, width) for p in range(depth)])

    total, last = joined_taps(0)
    put(48, total)
    tail = jnp.where(group16 == 1, last, tail)

    def fill_coarse(y, _):
        wide = gh[:, y].reshape((cd + 2) * 2 * chans, width).astype(F32)
        for c in range(3):
            gs[:, y, c] = shifted(wide, c).astype(BF).reshape(cd + 2, 2 * chans, width)

    landed_rows(gcopies, recvs, DIRS, False)
    lax.fori_loop(1, ch + 1, fill_coarse, None)
    spread = (lax.broadcasted_iota(jnp.int32, (width, 2 * width), 1) // 2
              == lax.broadcasted_iota(jnp.int32, (width, 2 * width), 0)).astype(BF)

    def back_row(q, _):
        k = 18 * chans
        pg = conv_row(wcb[...], [gs[p, pl.ds(q, 3)].reshape(k, width) for p in range(cd + 2)], cd)
        for p in range(cd):
            v = pg[p] * 0.125
            hi = v.astype(BF)
            lo = (v - hi.astype(F32)).astype(BF)
            wide = dot(hi, spread) + dot(lo, spread)
            for e in range(2):
                for f in range(2):
                    g = (jg[2 * p + e, 2 * q + f] + wide) * slope[2 * p + e, 2 * q + f]
                    eh[1 + 2 * p + e, 1 + 2 * q + f] = g.astype(BF)

    lax.fori_loop(1, ch - 1, back_row, None)
    landed_rows(gcopies, recvs, DIRS, True)
    for y in (0, ch + 1):
        fill_coarse(y, None)
    for q in (0, ch - 1):
        back_row(q, None)
    ecopies = exchange(eh, rim_src(1, depth, height, 1), eh, rim_dst(1, depth, height), esend, erecv)
    begin(ecopies, sends)

    landed(ucopies, recvs)
    low = lax.broadcasted_iota(jnp.int32, (width, width), 0)
    lane = lax.broadcasted_iota(jnp.int32, (width, width), 1)
    for c in range(3):
        source = lax.rem(lane + (c - 1) + 2 * width, 2 * width) // 2
        pick = (low == source).astype(BF)
        wide = dot(uh[...].reshape((cd + 2) * (ch + 2) * chans, width), pick)
        wide = wide.astype(BF).reshape(cd + 2, ch + 2, chans, width)
        for x in range(depth + 2):
            for y in range(height + 2):
                js[x, y, c, chans:2 * chans] = wide[(x + 1) // 2, (y + 1) // 2]

    total, last = joined_taps(chans)
    put(96, total)
    tail = jnp.where(group16 == 2, last, tail)
    total, last = fine_taps(
        lambda x: vs[x, :, :, :, 0:width].reshape((height + 2) * 3 * chans, width), 3 * chans,
        [eh[1 + p, 1:1 + height, :, 0:width].reshape(height * chans, width) for p in range(depth)])
    put(0, total)
    tail = jnp.where(group16 == 0, last, tail)
    put(240, tail)
    used = 288 // 16
    if gr.shape[0] > used:
        gr[used:] = jnp.zeros((gr.shape[0] - used, 16, width), BF)

    per = gr.shape[0] // groups[0][0]

    def ring(phase):
        count, me, member = groups[phase % 3]
        out, got = [], []
        for k in sorted(range(1, count), key=lambda k: abs(2 * k - count)):
            to = lax.rem(me + k, count)
            frm = lax.rem(me - k + count, count)
            src = gr.at[pl.ds(to * per, per)] if phase == 0 else ar.at[phase, me]

            def copy(slot):
                return pltpu.make_async_remote_copy(
                    src_ref=src, dst_ref=ar.at[phase, slot], send_sem=asend.at[phase, k - 1],
                    recv_sem=arecv.at[phase, k - 1], device_id=member(to), device_id_type=MESH)

            out.append(copy(me))
            got.append(copy(frm))
        for c in out:
            c.start()
        return out, got

    def advance(copies, phase):
        for c in copies[1]:
            c.wait_recv()
        total = ar[phase, 0].astype(F32)
        for k in range(1, groups[phase][0]):
            total = total + ar[phase, k].astype(F32)
        ar[phase + 1, groups[(phase + 1) % 3][1]] = total.astype(BF)
        return ring(phase + 1)

    first = ring(0)
    ar[0, groups[0][1]] = gr[pl.ds(groups[0][1] * per, per)]

    order = zero_one((height * chans, height * chans),
                     lambda r, l: (r // height == l % chans) & (r % height == l // chans)).astype(BF)

    def channels_first(which, ref):
        for p in range(depth):
            moved = dot(order, turn[which, p].reshape(height * chans, width))
            ref[:, p] = moved.reshape(chans, height, width).astype(BF)

    def dec_row(q, _):
        k = 18 * chans
        out = conv_row(wd[...], [js[p, pl.ds(q, 3)].reshape(k, width) for p in range(depth + 2)], depth)
        for p in range(depth):
            turn[0, p, q] = out[p].astype(BF)

    lax.fori_loop(0, height // 2, dec_row, None)

    second = advance(first, 0)
    lax.fori_loop(height // 2, height, dec_row, None)
    channels_first(0, dec_out)
    landed(ecopies, recvs)

    def fill_enc(y, _):
        wide = eh[:, y].reshape((depth + 2) * chans, 2 * width).astype(F32)
        for c in range(3):
            part = shifted(wide, c)[:, :width]
            es[:, y, c] = part.astype(BF).reshape(depth + 2, chans, width)

    lax.fori_loop(0, height + 2, fill_enc, None)

    def vol_row(q, _):
        k = 9 * chans
        out = conv_row(web[...], [es[p, pl.ds(q, 3)].reshape(k, width) for p in range(depth + 2)], depth)
        for p in range(depth):
            turn[1, p, q] = out[p].astype(BF)

    third = advance(second, 1)
    lax.fori_loop(0, height // 2, vol_row, None)
    fourth = advance(third, 2)
    lax.fori_loop(height // 2, height, vol_row, None)
    channels_first(1, vg_out)
    for c in fourth[1]:
        c.wait_recv()
    sum_out[...] = ar[3, 0:groups[0][0]].reshape(sum_out.shape)

    left(zcopies, esends)
    for copies in (vcopies, pcopies, gcopies, ucopies, scopies, ecopies):
        left(copies, sends)
    for copies in (first, second, third, fourth):
        for c in copies[0]:
            c.wait_send()


def per_device(sizes, volume, enc_weight, coarse_weight, up_weight, dec_weight, cotangent):
    nx, ny, nz = sizes
    chans, d, h, w = volume.shape
    cd, ch = d // 2, h // 2
    owners = min(2, nx) * (ny // 2 if ny > 4 else ny)
    per = -(-18 // owners)
    pair = jnp.transpose(jnp.concatenate([volume, cotangent], axis=0), (1, 2, 0, 3))
    operands = (
        pair, jnp.transpose(enc_weight, (1, 2, 0)), coarse_weight, up_weight.T, jnp.transpose(dec_weight, (0, 2, 1)))
    c2 = 2 * chans
    widest = max(owners, nx * ny // owners, nz) - 1
    scratch = [
        ((16, 16, 27), BF),
        ((27, 16, 32), BF),
        ((16, 32), BF),
        ((27, 16, 32), BF),
        ((48, 144), BF),
        ((48, 288), BF),
        ((96, 144), BF),
        ((96, 144), BF),
        ((48, 288), BF),
        ((48, 144), BF),
        ((32, 16), BF),
        ((2, d, h, chans, w), BF),
        ((d + 2, h + 2, c2, w), BF),
        ((2, d, chans, w), BF),
        ((2, 3, d + 2, chans, w), BF),
        ((d + 2, h + 2, 3, chans, 2 * w), BF),
        ((d + 2, h + 2, 3, chans, 2 * w), BF),
        ((d + 2, h + 2, chans, 2 * w), BF),
        ((d, h, chans, 2 * w), F32),
        ((d, h, chans, 2 * w), F32),
        ((cd, ch, chans, 2 * w), BF),
        ((cd, ch, chans, 2 * w), BF),
        ((cd, ch, chans, w), BF),
        ((cd + 2, ch + 2, chans, w), BF),
        ((cd + 2, ch + 2, 3, chans, w), BF),
        ((cd, ch, c2, w), BF),
        ((cd + 2, ch + 2, chans, w), BF),
        ((cd + 2, ch + 2, c2, w), BF),
        ((cd + 2, ch + 2, 3, c2, w), BF),
        ((d + 2, h + 2, 3, c2, w), BF),
        ((d + 2, h + 2, chans, 2 * w), BF),
        ((d + 2, h + 2, 3, chans, w), BF),
        ((owners * per, 16, w), BF),
        ((4, widest + 1, per, 16, w), BF),
    ]
    dma = pltpu.SemaphoreType.DMA
    sems = [dma((8,))] * 2 + [dma((18,))] * 2 + [dma((8,))] * 10 + [dma((4, max(widest, 1)))] * 2 + [dma((4,))]
    hbm = pl.BlockSpec(memory_space=pl.ANY)
    vmem = pl.BlockSpec(memory_space=pltpu.VMEM)
    dec, vg, total = pl.pallas_call(
        functools.partial(kernel, sizes),
        out_shape=(
            jax.ShapeDtypeStruct((chans, d, h, w), BF),
            jax.ShapeDtypeStruct((chans, d, h, w), BF),
            jax.ShapeDtypeStruct((owners * per, 16, w), BF)),
        in_specs=[vmem] + [hbm] * 4,
        out_specs=(vmem,) * 3,
        scratch_shapes=[pltpu.VMEM(s, t) for s, t in scratch] + sems,
        compiler_params=pltpu.CompilerParams(
            collective_id=0, has_side_effects=True, vmem_limit_bytes=48 * 1024 * 1024),
    )(*operands)
    grads = ((16, 16, 27), (27, 16, 32), (16, 32), (27, 16, 32))
    dec, vg, enc, coarse, upg, decg = pl.pallas_call(
        finish,
        out_shape=tuple(jax.ShapeDtypeStruct(x.shape, BF) for x in (dec, vg))
        + tuple(jax.ShapeDtypeStruct(x, F32) for x in grads),
        in_specs=[vmem] * 3,
        out_specs=(hbm,) * 6,
        scratch_shapes=[pltpu.VMEM(x, F32) for x in grads] + [dma((6,))],
        compiler_params=pltpu.CompilerParams(vmem_limit_bytes=8 * 1024 * 1024),
    )(dec, vg, total)
    return (dec, vg, jnp.transpose(enc, (2, 0, 1)), coarse, upg.T, jnp.transpose(decg, (0, 2, 1)))


def solution(mesh):
    sizes = tuple(mesh.shape[a] for a in AXES)
    spec = P(None, "gx", "gy", "gz")
    return jax.shard_map(
        functools.partial(per_device, sizes),
        mesh=mesh,
        in_specs=(spec, P(), P(), P(), P(), spec),
        out_specs=(spec, spec, P(), P(), P(), P()),
        check_vma=False,
    )
```

```python
import functools

import jax
import jax.numpy as jnp
from jax import lax
from jax.experimental import pallas as pl
from jax.experimental.pallas import tpu as pltpu
from jax.sharding import PartitionSpec as P

AXES = ("gx", "gy", "gz")
BF = jnp.bfloat16
F32 = jnp.float32
MESH = pl.DeviceIdType.MESH
DIRS = tuple((dx, dy) for dy in (-1, 1, 0) for dx in (-1, 1, 0) if (dx, dy) != (0, 0))


def dot(a, b):
    return jnp.dot(a, b, preferred_element_type=F32)


def dot_nt(a, b):
    return lax.dot_general(a, b, (((1,), (1,)), ((), ())), preferred_element_type=F32)


def dot_tn(a, b):
    return lax.dot_general(a, b, (((0,), (0,)), ((), ())), preferred_element_type=F32)


def zero_one(shape, rule):
    return rule(lax.broadcasted_iota(jnp.int32, shape, 0), lax.broadcasted_iota(jnp.int32, shape, 1))


def arrange_weights(enc, coarse, upt, dec, we, wd, wdb, wc, wcb, web, up):
    flat = enc[...].reshape(256, 27)
    same_in = zero_one((256, 144), lambda r, l: r // 16 == l % 16)
    same_out = zero_one((256, 144), lambda r, l: r % 16 == l % 16)
    fold_in = zero_one((16, 256), lambda r, l: r == l % 16).astype(BF)
    fold_out = zero_one((16, 256), lambda r, l: r == l // 16).astype(BF)
    for a in range(3):
        ahead = dot(flat, zero_one((27, 144), lambda r, l: r == 9 * a + l // 16).astype(BF))
        we[16 * a:16 * a + 16] = dot(fold_in, jnp.where(same_in, ahead, 0.0).astype(BF)).astype(BF)
        back = dot(flat, zero_one((27, 144), lambda r, l: r == 26 - 9 * a - l // 16).astype(BF))
        web[16 * a:16 * a + 16] = dot(fold_out, jnp.where(same_out, back, 0.0).astype(BF)).astype(BF)
    totals = [0.0] * 4
    for t in range(9):
        wide = zero_one((32, 288), lambda r, l: l == 32 * t + r).astype(BF)
        slim = zero_one((16, 144), lambda r, l: l == 16 * t + r).astype(BF)
        ahead, back = (t, 9 + t, 18 + t), (26 - t, 17 - t, 8 - t)
        totals[0] += dot(jnp.concatenate([dec[k] for k in ahead], axis=0), wide)
        totals[1] += dot_tn(jnp.concatenate([dec[k] for k in back], axis=1), slim)
        totals[2] += dot_tn(jnp.concatenate([coarse[k] for k in ahead], axis=1), slim)
        totals[3] += dot(jnp.concatenate([coarse[k] for k in back], axis=0), wide)
    for ref, total in zip((wd, wdb, wc, wcb), totals):
        ref[...] = total.astype(BF)
    up[...] = dot_tn(upt[...], zero_one((16, 16), lambda r, l: r == l).astype(BF)).astype(BF)


def finish(split, dec, vg, total, dec_out, vg_out, enc_out, coarse_out, up_out, decg_out,
           enc, coarse, up, decg, sems):
    copies = [pltpu.make_async_copy(a, b, sems.at[k]) for k, (a, b) in enumerate(
        ((dec, dec_out), (vg, vg_out), (enc, enc_out), (coarse, coarse_out), (up, up_out), (decg, decg_out)))]
    copies[0].start()
    copies[1].start()

    def tile(which, k):
        return total[which * split + k]

    eye = zero_one((128, 128), lambda r, l: r == l).astype(BF)
    for c in range(3):
        block = jnp.concatenate([tile(0, 6 + c), tile(1, 3 + c)], axis=0)
        turned = dot_nt(eye, block).reshape(8, 16, 32)
        for g in range(8):
            decg[3 * g + c] = turned[g]
        skip_last = dot_nt(zero_one((16, 128), lambda r, l: l == 16 * c + r).astype(BF), tile(0, 10))
        upper_last = dot_nt(zero_one((16, 128), lambda r, l: l == 48 + 16 * c + r).astype(BF), tile(1, 6))
        decg[24 + c] = jnp.concatenate([skip_last, upper_last], axis=1)
    copies[5].start()
    for c in range(3):
        for half in range(2):
            block = tile(0, 3 * half + c)
            for g in range(4):
                pick = zero_one((128, 32), lambda r, l: r == 32 * g + l).astype(BF)
                coarse[3 * (4 * half + g) + c] = dot(block, pick)
        pick = zero_one((128, 32), lambda r, l: r == 32 * c + l).astype(BF)
        coarse[24 + c] = dot(tile(0, 9), pick)
    copies[3].start()
    up[...] = jnp.concatenate(
        [dot_nt(zero_one((16, 128), lambda r, l: l == 96 + 16 * k + r).astype(BF), tile(0, 9)) for k in range(2)], axis=1)
    copies[4].start()
    grow = zero_one((256, 16), lambda r, l: l == r // 16).astype(BF)
    same = zero_one((256, 128), lambda r, l: r % 16 == l % 16)
    flat = jnp.zeros((256, 27), F32)
    for c in range(3):
        wide = jnp.where(same, dot(grow, tile(1, c)), 0.0).astype(BF)
        flat = flat + dot(wide, zero_one((128, 27), lambda r, l: l == 3 * (r // 16) + c).astype(BF))
        wide = jnp.where(same, dot(grow, tile(1, 6)), 0.0).astype(BF)
        flat = flat + dot(wide, zero_one((128, 27), lambda r, l: (r // 16 == c) & (l == 24 + c)).astype(BF))
    enc[...] = flat.reshape(16, 16, 27)
    copies[2].start()
    for c in copies:
        c.wait()


def all_of(*conds):
    total = None
    for c in conds:
        if c is not None:
            total = c if total is None else jnp.logical_and(total, c)
    return total


def span(step, size, halo):
    if step == 0:
        return (0, size), (halo, size)
    if step > 0:
        return (size - halo, halo), (0, halo)
    return (0, halo), (halo + size, halo)


def kernel(sizes, vc, enc_in, coarse_in, upt_in, dec_in, dec_out, vg_out, sum_out,
           enc_w, coarse_w, upt, dec_w, we, wd, wdb, wc, wcb, web, up, turn,
           vct, pk, er, vs, cs, skip, slope, jg, ughi, uglo, ug, ph, ps, act, uh, gh, gs, js, eh, es,
           gr0, gr1, ar0, ar1,
           vsend, vrecv, zsend, zrecv, psend, precv, gsend, grecv, usend, urecv, ssend, srecv, esend, erecv,
           asend0, arecv0, asend1, arecv1, wsem):
    nx, ny, nz = sizes
    ix, iy, iz = (lax.axis_index(a) for a in AXES)
    depth, height, _, width = vc.shape
    chans = vc.shape[2] // 2
    cd, ch = depth // 2, height // 2

    def exists(step, index, count):
        return None if step == 0 else (index + step < count if step > 0 else index + step >= 0)

    def at(dx, dy, dz=0):
        return (ix + dx, iy + dy, iz + dz)

    def guarded(cond, f):
        if cond is None:
            f()
        else:
            pl.when(cond)(f)

    sends = [all_of(exists(dx, ix, nx), exists(dy, iy, ny)) for dx, dy in DIRS]
    recvs = [all_of(exists(-dx, ix, nx), exists(-dy, iy, ny)) for dx, dy in DIRS]
    ends = tuple((dx, dy, s) for dy in (-1, 1, 0) for dx in (-1, 1, 0) for s in (-1, 1))
    esends = [all_of(exists(dx, ix, nx), exists(dy, iy, ny), exists(dz, iz, nz)) for dx, dy, dz in ends]
    erecvs = [all_of(exists(-dx, ix, nx), exists(-dy, iy, ny), exists(-dz, iz, nz)) for dx, dy, dz in ends]

    cores = min(2, nx)
    lows, across = nx // cores, ny // 2 if ny > 4 else ny
    highs = ny // across
    core, y_low, x_at, y_high = lax.rem(ix, cores), ix // cores, lax.rem(iy, across), iy // across
    groups = (
        (cores * across, core * across + x_at,
         lambda j: (y_low * cores + j // across, y_high * across + lax.rem(j, across), iz)),
        (highs * lows, y_high * lows + y_low,
         lambda j: (lax.rem(j, lows) * cores + core, (j // lows) * across + x_at, iz)),
        (nz, iz, lambda j: (ix, iy, j)),
    )

    loads = [pltpu.make_async_copy(a, b, wsem.at[k]) for k, (a, b) in enumerate(
        ((enc_in, enc_w), (coarse_in, coarse_w), (upt_in, upt), (dec_in, dec_w)))]
    for c in loads:
        c.start()

    for ref in (vct, er, skip, ph, uh, gh, eh):
        ref[...] = jnp.zeros(ref.shape, ref.dtype)
    vct[1:1 + depth, 1:1 + height] = vc[...]
    barrier = pltpu.get_barrier_semaphore()

    def greet(device):
        pl.semaphore_signal(barrier, inc=1, device_id=device, device_id_type=MESH)

    for count, me, member in groups:
        for k in range(1, count):
            greet(member(lax.rem(me + k, count)))
    for dx, dy, dz in [d + (0,) for d in DIRS] + list(ends):
        if dx != 0 or dy != 0:
            guarded(all_of(exists(dx, ix, nx), exists(dy, iy, ny), exists(dz, iz, nz)),
                    lambda dx=dx, dy=dy, dz=dz: greet(at(dx, dy, dz)))

    def both(index, count):
        return (jnp.where(index > 0, 1, 0) + jnp.where(index < count - 1, 1, 0)).astype(jnp.int32)

    row = lax.broadcasted_iota(jnp.int32, (width, 2 * width), 0)
    lane = lax.broadcasted_iota(jnp.int32, (width, 2 * width), 1)
    total = jnp.zeros((depth * chans, 2 * width), F32)
    for n in range(2):
        for y in range(height):
            base = 64 * n + 8 * y
            pick = ((lane == base + row) & (row < 8)) | ((lane == width + base + row - 120) & (row >= 120))
            total = total + dot(vc[:, y, n * chans:(n + 1) * chans].reshape(depth * chans, width), pick.astype(BF))
    for side in range(2):
        pk[side] = total[:, side * width:(side + 1) * width].astype(BF).reshape(depth, chans, width)
    bx, by, bz = both(ix, nx), both(iy, ny), both(iz, nz)
    near = bx + by + bx * by
    pl.semaphore_wait(barrier, sum(count - 1 for count, _, _ in groups) + near + near * bz)

    def exchange(src, src_at, dst, dst_at, send_sem, recv_sem):
        copies = []
        for d, (dx, dy) in enumerate(DIRS):
            copies.append(pltpu.make_async_remote_copy(
                src_ref=src.at[src_at(dx, dy)], dst_ref=dst.at[dst_at(dx, dy)],
                send_sem=send_sem.at[d], recv_sem=recv_sem.at[d],
                device_id=at(dx, dy), device_id_type=MESH))
        return copies

    def begin(copies, conds):
        for c, s in zip(copies, conds):
            guarded(s, c.start)

    def landed(copies, conds):
        for c, r in zip(copies, conds):
            guarded(r, c.wait_recv)

    def landed_rows(copies, conds, dirs, rim):
        part = [i for i, d in enumerate(dirs) if (d[1] != 0) == rim]
        landed([copies[i] for i in part], [conds[i] for i in part])

    def left(copies, conds):
        for c, s in zip(copies, conds):
            guarded(s, c.wait_send)

    def rim_src(halo, d0, h0, off):
        def f(dx, dy):
            (a, n), _ = span(dx, d0, halo)
            (b, m), _ = span(dy, h0, halo)
            return (pl.ds(a + off, n), pl.ds(b + off, m))
        return f

    def rim_dst(halo, d0, h0):
        def f(dx, dy):
            _, (a, n) = span(dx, d0, halo)
            _, (b, m) = span(dy, h0, halo)
            return (pl.ds(a, n), pl.ds(b, m))
        return f

    vcopies = exchange(vc, rim_src(1, depth, height, 0), vct, rim_dst(1, depth, height), vsend, vrecv)
    begin(vcopies, sends)

    zcopies = []
    for d, (dx, dy, dz) in enumerate(ends):
        (a, n), (b, m) = span(dx, depth, 1)
        side = 1 if dz > 0 else 0
        zcopies.append(pltpu.make_async_remote_copy(
            src_ref=pk.at[side, pl.ds(a, n)], dst_ref=er.at[side, 1 - dy, pl.ds(b, m)],
            send_sem=zsend.at[d], recv_sem=zrecv.at[d],
            device_id=at(dx, dy, dz), device_id_type=MESH))
    begin(zcopies, esends)
    for c in loads:
        c.wait()
    arrange_weights(enc_w, coarse_w, upt, dec_w, we, wd, wdb, wc, wcb, web, up)

    def shifted(wide, c):
        if c == 1:
            return wide
        return pltpu.roll(wide, 1 if c == 0 else wide.shape[1] - 1, 1)

    def fill_inputs(y, _):
        dyi, base = (y + 7) // 8, 8 * lax.rem(y + 7, 8)
        flat = ((depth + 2) * chans, width)
        kind, spot = lane // width, lax.rem(lane, width)
        source = base + 64 * kind + spot
        lo = (row == source - 120) & (spot >= 120)
        hi = (row == source) & (spot < 8)
        got = dot(er[1, dyi].reshape(flat), lo.astype(BF)) + dot(er[0, dyi].reshape(flat), hi.astype(BF))
        for n, ref in enumerate((vs, cs)):
            own = vct[:, y, n * chans:(n + 1) * chans].reshape(flat).astype(F32)
            wide = jnp.concatenate([own, got[:, n * width:(n + 1) * width]], axis=1)
            for c in range(3):
                ref[:, y, c] = shifted(wide, c).astype(BF).reshape(depth + 2, chans, 2 * width)


    sets = ((gr0, ar0, asend0, arecv0), (gr1, ar1, asend1, arecv1))

    def ring(which, phase):
        gr, ar, asend, arecv = sets[which]
        count, me, member = groups[phase % 3]
        per = gr.shape[0] // groups[0][0]
        out, got = [], []
        for k in sorted(range(1, count), key=lambda k: abs(2 * k - count)):
            to = lax.rem(me + k, count)
            frm = lax.rem(me - k + count, count)
            src = gr.at[pl.ds(to * per, per)] if phase == 0 else ar.at[phase, me]

            def copy(slot):
                return pltpu.make_async_remote_copy(
                    src_ref=src, dst_ref=ar.at[phase, slot], send_sem=asend.at[phase, k - 1],
                    recv_sem=arecv.at[phase, k - 1], device_id=member(to), device_id_type=MESH)

            out.append(copy(me))
            got.append(copy(frm))
        for c in out:
            c.start()
        if phase == 0:
            ar[0, me] = gr[pl.ds(me * per, per)]
        everything.extend(out)
        return got

    everything = []

    def advance(which, copies, phase):
        ar = sets[which][1]
        for c in copies:
            c.wait_recv()
        total = ar[phase, 0].astype(F32)
        for k in range(1, groups[phase][0]):
            total = total + ar[phase, k].astype(F32)
        ar[phase + 1, groups[(phase + 1) % 3][1]] = total.astype(BF)
        return ring(which, phase + 1)

    fine = lax.broadcasted_iota(jnp.int32, (1, 2 * width), 1)
    coarse = lax.broadcasted_iota(jnp.int32, (1, width), 1)
    low_ok = jnp.where(iz > 0, 1.0, 0.0).astype(F32)
    high_ok = jnp.where(iz < nz - 1, 1.0, 0.0).astype(F32)
    fine_mask = jnp.where(fine < width, 1.0, jnp.where(fine < 3 * width // 2, high_ok, low_ok))
    coarse_mask = jnp.where(coarse < width // 2, 1.0, jnp.where(coarse < 3 * width // 4, high_ok, low_ok))
    own_coarse = coarse < width // 2

    def conv_row(weight, planes, outs):
        m = weight.shape[0] // 3
        ys = [dot(weight, x) for x in planes]
        return [ys[p][:m] + ys[p + 1][m:2 * m] + ys[p + 2][2 * m:] for p in range(outs)]

    def enc_row(q, _):
        k = 9 * chans
        pre = conv_row(we[...], [vs[p, pl.ds(q, 3)].reshape(k, 2 * width) for p in range(depth + 2)], depth)
        for p in range(depth):
            t = pre[p]
            sig = 1.0 / (1.0 + jnp.exp(-t))
            skip[1 + p, 1 + q] = (t * sig * fine_mask).astype(BF)
            slope[p, q] = sig * (1.0 + t * (1.0 - sig)) * fine_mask

    landed_rows(zcopies, erecvs, ends, False)
    landed_rows(vcopies, recvs, DIRS, False)
    lax.fori_loop(1, height + 1, fill_inputs, None)
    lax.fori_loop(1, height - 1, enc_row, None)
    landed_rows(zcopies, erecvs, ends, True)
    landed_rows(vcopies, recvs, DIRS, True)
    for y in (0, height + 1):
        fill_inputs(y, None)
    for q in (0, height - 1):
        enc_row(q, None)

    pool = (lax.broadcasted_iota(jnp.int32, (2 * width, width), 0) // 2
            == lax.broadcasted_iota(jnp.int32, (2 * width, width), 1)).astype(BF)

    for q in range(ch):
        rows_in = skip[1:1 + depth, 1 + 2 * q:3 + 2 * q].reshape(depth * 2 * chans, 2 * width)
        half = dot(rows_in, pool).reshape(cd, 4, chans, width)
        ph[1:1 + cd, 1 + q] = ((half[:, 0] + half[:, 1] + half[:, 2] + half[:, 3]) * 0.125).astype(BF)
    pcopies = exchange(ph, rim_src(1, cd, ch, 1), ph, rim_dst(1, cd, ch), psend, precv)
    begin(pcopies, sends)
    scopies = exchange(skip, rim_src(1, depth, height, 1), skip, rim_dst(1, depth, height), ssend, srecv)
    begin(scopies, sends)

    def joined_row(q, _):
        k = 9 * chans
        sums = [jnp.zeros((chans, 2 * width), F32) for _ in range(cd)]
        for e in range(2):
            r = 2 * q + e
            out = conv_row(wdb[...], [cs[p, pl.ds(r, 3)].reshape(k, 2 * width) for p in range(depth + 2)], depth)
            for p in range(depth):
                jg[p, r] = out[p][:chans]
                sums[p // 2] = sums[p // 2] + out[p][chans:]
        for p in range(cd):
            hi = sums[p].astype(BF)
            ughi[p, q] = hi
            uglo[p, q] = (sums[p] - hi.astype(F32)).astype(BF)

    lax.fori_loop(0, ch, joined_row, None)
    flat = (cd * ch * chans, 2 * width)
    grad = dot(ughi[...].reshape(flat), pool) + dot(uglo[...].reshape(flat), pool)
    ug[...] = grad.astype(BF).reshape(ug.shape)

    def fill_pooled(q, _):
        wide = ph[:, q].reshape((cd + 2) * chans, width).astype(F32)
        for c in range(3):
            ps[:, q, c] = shifted(wide, c).astype(BF).reshape(cd + 2, chans, width)

    landed_rows(pcopies, recvs, DIRS, False)
    lax.fori_loop(1, ch + 1, fill_pooled, None)
    def coarse_row(q):
        k = 9 * chans
        pre = conv_row(wc[...], [ps[p, q:q + 3].reshape(k, width) for p in range(cd + 2)], cd)
        for p in range(cd):
            t = pre[p]
            sig = 1.0 / (1.0 + jnp.exp(-t))
            a = (t * sig * coarse_mask).astype(BF)
            act[p, q] = a
            uh[1 + p, 1 + q] = dot(upt[...], a).astype(BF)
            back = dot(up[...], ug[p, q])
            gh[1 + p, 1 + q] = (back * (sig * (1.0 + t * (1.0 - sig)) * coarse_mask)).astype(BF)

    for q in range(1, ch - 1):
        coarse_row(q)
    landed_rows(pcopies, recvs, DIRS, True)
    for q in (0, ch + 1):
        fill_pooled(q, None)
    for q in (0, ch - 1):
        coarse_row(q)
    gcopies = exchange(gh, rim_src(1, cd, ch, 1), gh, rim_dst(1, cd, ch), gsend, grecv)
    begin(gcopies, sends)
    ucopies = exchange(uh, rim_src(1, cd, ch, 1), uh, rim_dst(1, cd, ch), usend, urecv)
    begin(ucopies, sends)

    group16 = lax.broadcasted_iota(jnp.int32, (1, width), 1) // 16
    group32 = lax.broadcasted_iota(jnp.int32, (1, width), 1) // 32

    def tap_sums(block, step, groups, gid):
        out = []
        for b in range(3):
            total = jnp.zeros((step, width), F32)
            for q in range(groups):
                total = jnp.where(gid == q, block[(q + b) * step:(q + b + 1) * step], total)
            size = width // 2
            while size >= width // groups:
                total = total + pltpu.roll(total, size, 1)
                size //= 2
            out.append(total)
        return out

    def put(ref, first, value):
        tiles = value.shape[0] // 16
        ref[first:first + tiles] = value.astype(BF).reshape(tiles, 16, width)

    def place(total, gid, first, block):
        for k in range(block.shape[0] // 16):
            total = jnp.where(gid == first + k, block[16 * k:16 * k + 16], total)
        return total

    for ref, used in ((gr0, 11), (gr1, 7)):
        if ref.shape[0] > used:
            ref[used:] = jnp.zeros((ref.shape[0] - used, 16, width), BF)
    blank = jnp.zeros((16, width), F32)
    step = 3 * chans
    taps = []
    masked = [jnp.where(own_coarse, gh[1 + p, 1:1 + ch].reshape(2 * chans * ch, width), 0)
              for p in range(cd)]
    for a in range(3):
        block = sum(dot_nt(ps[p + a].reshape((ch + 2) * step, width), masked[p]) for p in range(cd))
        taps += tap_sums(block, step, ch, group32)
    for half in range(2):
        total = jnp.zeros((step, width), F32)
        for g in range(4):
            total = jnp.where(group32 == g, taps[4 * half + g], total)
        put(gr0, 3 * half, total)
    side = place(blank, group32, 0, taps[8])
    up_total = jnp.zeros((2 * chans, width), F32)
    for p in range(cd):
        for q in range(ch):
            g = jnp.where(own_coarse, ug[p, q], 0)
            up_total = up_total + dot_nt(act[p, q], jnp.concatenate([g] * 8, axis=0))
    side = place(side, group16, 6, up_total)
    put(gr0, 9, side)

    def fill_skip(first, count, y):
        wide = skip[first:first + count, y].reshape(count * chans, 2 * width).astype(F32)
        for c in range(3):
            part = shifted(wide, c)[:, :width]
            js[first:first + count, y, c, 0:chans] = part.astype(BF).reshape(count, chans, width)

    lax.fori_loop(1, height + 1, lambda y, _: fill_skip(1, depth, y), None)
    landed(scopies, recvs)
    for y in (0, height + 1):
        fill_skip(0, depth + 2, y)

    def fill_sides(y, _):
        fill_skip(0, 1, y)
        fill_skip(depth + 1, 1, y)

    lax.fori_loop(1, height + 1, fill_sides, None)

    def fine_taps(source, step, grads):
        taps = []
        for a in range(3):
            block = sum(dot_nt(source(a + p), grads[p]) for p in range(depth))
            taps += tap_sums(block, step, height, group16)
        total = jnp.zeros((step, width), F32)
        for g in range(8):
            total = jnp.where(group16 == g, taps[g], total)
        return total, taps[8]

    def joined_taps(first):
        return fine_taps(
            lambda x: js[x, :, :, first:first + chans].reshape((height + 2) * 3 * chans, width), 3 * chans,
            [vc[p, :, chans:2 * chans].reshape(height * chans, width) for p in range(depth)])

    total, last = joined_taps(0)
    put(gr0, 6, total)
    put(gr0, 10, place(blank, group16, 0, last))
    early = ring(0, 0)

    def fill_coarse(y, _):
        wide = gh[:, y].reshape((cd + 2) * 2 * chans, width).astype(F32)
        for c in range(3):
            gs[:, y, c] = shifted(wide, c).astype(BF).reshape(cd + 2, 2 * chans, width)

    landed_rows(gcopies, recvs, DIRS, False)
    lax.fori_loop(1, ch + 1, fill_coarse, None)
    spread = (lax.broadcasted_iota(jnp.int32, (width, 2 * width), 1) // 2
              == lax.broadcasted_iota(jnp.int32, (width, 2 * width), 0)).astype(BF)

    def back_row(q, _):
        k = 18 * chans
        pg = conv_row(wcb[...], [gs[p, pl.ds(q, 3)].reshape(k, width) for p in range(cd + 2)], cd)
        for p in range(cd):
            v = pg[p] * 0.125
            hi = v.astype(BF)
            lo = (v - hi.astype(F32)).astype(BF)
            wide = dot(hi, spread) + dot(lo, spread)
            for e in range(2):
                for f in range(2):
                    g = (jg[2 * p + e, 2 * q + f] + wide) * slope[2 * p + e, 2 * q + f]
                    eh[1 + 2 * p + e, 1 + 2 * q + f] = g.astype(BF)

    lax.fori_loop(1, ch - 1, back_row, None)
    landed_rows(gcopies, recvs, DIRS, True)
    for y in (0, ch + 1):
        fill_coarse(y, None)
    for q in (0, ch - 1):
        back_row(q, None)
    ecopies = exchange(eh, rim_src(1, depth, height, 1), eh, rim_dst(1, depth, height), esend, erecv)
    begin(ecopies, sends)
    early = advance(0, early, 0)

    landed(ucopies, recvs)
    low = lax.broadcasted_iota(jnp.int32, (width, width), 0)
    lane = lax.broadcasted_iota(jnp.int32, (width, width), 1)
    for c in range(3):
        source = lax.rem(lane + (c - 1) + 2 * width, 2 * width) // 2
        pick = (low == source).astype(BF)
        wide = dot(uh[...].reshape((cd + 2) * (ch + 2) * chans, width), pick)
        wide = wide.astype(BF).reshape(cd + 2, ch + 2, chans, width)
        for x in range(depth + 2):
            for y in range(height + 2):
                js[x, y, c, chans:2 * chans] = wide[(x + 1) // 2, (y + 1) // 2]

    total, last = joined_taps(chans)
    put(gr1, 3, total)
    side = place(blank, group16, 3, last)
    total, last = fine_taps(
        lambda x: vs[x, :, :, :, 0:width].reshape((height + 2) * 3 * chans, width), 3 * chans,
        [eh[1 + p, 1:1 + height, :, 0:width].reshape(height * chans, width) for p in range(depth)])
    put(gr1, 0, total)
    put(gr1, 6, place(side, group16, 0, last))

    late = ring(1, 0)

    order = zero_one((height * chans, height * chans),
                     lambda r, l: (r // height == l % chans) & (r % height == l // chans)).astype(BF)

    def channels_first(which, ref):
        for p in range(depth):
            moved = dot(order, turn[which, p].reshape(height * chans, width))
            ref[:, p] = moved.reshape(chans, height, width).astype(BF)

    def dec_row(q, _):
        k = 18 * chans
        out = conv_row(wd[...], [js[p, pl.ds(q, 3)].reshape(k, width) for p in range(depth + 2)], depth)
        for p in range(depth):
            turn[0, p, q] = out[p].astype(BF)

    lax.fori_loop(0, height // 2, dec_row, None)

    late = advance(1, late, 0)
    early = advance(0, early, 1)
    lax.fori_loop(height // 2, height, dec_row, None)
    channels_first(0, dec_out)
    landed(ecopies, recvs)

    def fill_enc(y, _):
        wide = eh[:, y].reshape((depth + 2) * chans, 2 * width).astype(F32)
        for c in range(3):
            part = shifted(wide, c)[:, :width]
            es[:, y, c] = part.astype(BF).reshape(depth + 2, chans, width)

    lax.fori_loop(0, height + 2, fill_enc, None)

    def vol_row(q, _):
        k = 9 * chans
        out = conv_row(web[...], [es[p, pl.ds(q, 3)].reshape(k, width) for p in range(depth + 2)], depth)
        for p in range(depth):
            turn[1, p, q] = out[p].astype(BF)

    late = advance(1, late, 1)
    early = advance(0, early, 2)
    lax.fori_loop(0, height // 2, vol_row, None)
    late = advance(1, late, 2)
    lax.fori_loop(height // 2, height, vol_row, None)
    channels_first(1, vg_out)
    for c in early + late:
        c.wait_recv()
    sum_out[0:gr0.shape[0]] = ar0[3, 0:groups[0][0]].reshape(gr0.shape)
    sum_out[gr0.shape[0]:] = ar1[3, 0:groups[0][0]].reshape(gr1.shape)

    left(zcopies, esends)
    for copies in (vcopies, pcopies, gcopies, ucopies, scopies, ecopies):
        left(copies, sends)
    for c in everything:
        c.wait_send()


def per_device(sizes, volume, enc_weight, coarse_weight, up_weight, dec_weight, cotangent):
    nx, ny, nz = sizes
    chans, d, h, w = volume.shape
    cd, ch = d // 2, h // 2
    owners = min(2, nx) * (ny // 2 if ny > 4 else ny)
    pers = (-(-11 // owners), -(-7 // owners))
    pair = jnp.transpose(jnp.concatenate([volume, cotangent], axis=0), (1, 2, 0, 3))
    operands = (
        pair, jnp.transpose(enc_weight, (1, 2, 0)), coarse_weight, up_weight.T, jnp.transpose(dec_weight, (0, 2, 1)))
    c2 = 2 * chans
    widest = max(owners, nx * ny // owners, nz) - 1
    scratch = [
        ((16, 16, 27), BF),
        ((27, 16, 32), BF),
        ((16, 32), BF),
        ((27, 16, 32), BF),
        ((48, 144), BF),
        ((48, 288), BF),
        ((96, 144), BF),
        ((96, 144), BF),
        ((48, 288), BF),
        ((48, 144), BF),
        ((32, 16), BF),
        ((2, d, h, chans, w), BF),
        ((d + 2, h + 2, c2, w), BF),
        ((2, d, chans, w), BF),
        ((2, 3, d + 2, chans, w), BF),
        ((d + 2, h + 2, 3, chans, 2 * w), BF),
        ((d + 2, h + 2, 3, chans, 2 * w), BF),
        ((d + 2, h + 2, chans, 2 * w), BF),
        ((d, h, chans, 2 * w), F32),
        ((d, h, chans, 2 * w), F32),
        ((cd, ch, chans, 2 * w), BF),
        ((cd, ch, chans, 2 * w), BF),
        ((cd, ch, chans, w), BF),
        ((cd + 2, ch + 2, chans, w), BF),
        ((cd + 2, ch + 2, 3, chans, w), BF),
        ((cd, ch, c2, w), BF),
        ((cd + 2, ch + 2, chans, w), BF),
        ((cd + 2, ch + 2, c2, w), BF),
        ((cd + 2, ch + 2, 3, c2, w), BF),
        ((d + 2, h + 2, 3, c2, w), BF),
        ((d + 2, h + 2, chans, 2 * w), BF),
        ((d + 2, h + 2, 3, chans, w), BF),
        ((owners * pers[0], 16, w), BF),
        ((owners * pers[1], 16, w), BF),
        ((4, widest + 1, pers[0], 16, w), BF),
        ((4, widest + 1, pers[1], 16, w), BF),
    ]
    dma = pltpu.SemaphoreType.DMA
    sems = [dma((8,))] * 2 + [dma((18,))] * 2 + [dma((8,))] * 10 + [dma((4, max(widest, 1)))] * 4 + [dma((4,))]
    hbm = pl.BlockSpec(memory_space=pl.ANY)
    vmem = pl.BlockSpec(memory_space=pltpu.VMEM)
    dec, vg, total = pl.pallas_call(
        functools.partial(kernel, sizes),
        out_shape=(
            jax.ShapeDtypeStruct((chans, d, h, w), BF),
            jax.ShapeDtypeStruct((chans, d, h, w), BF),
            jax.ShapeDtypeStruct((owners * sum(pers), 16, w), BF)),
        in_specs=[vmem] + [hbm] * 4,
        out_specs=(vmem,) * 3,
        scratch_shapes=[pltpu.VMEM(s, t) for s, t in scratch] + sems,
        compiler_params=pltpu.CompilerParams(
            collective_id=0, has_side_effects=True, vmem_limit_bytes=48 * 1024 * 1024),
    )(*operands)
    grads = ((16, 16, 27), (27, 16, 32), (16, 32), (27, 16, 32))
    dec, vg, enc, coarse, upg, decg = pl.pallas_call(
        functools.partial(finish, owners * pers[0]),
        out_shape=tuple(jax.ShapeDtypeStruct(x.shape, BF) for x in (dec, vg))
        + tuple(jax.ShapeDtypeStruct(x, F32) for x in grads),
        in_specs=[vmem] * 3,
        out_specs=(hbm,) * 6,
        scratch_shapes=[pltpu.VMEM(x, F32) for x in grads] + [dma((6,))],
        compiler_params=pltpu.CompilerParams(vmem_limit_bytes=8 * 1024 * 1024),
    )(dec, vg, total)
    return (dec, vg, jnp.transpose(enc, (2, 0, 1)), coarse, upg.T, jnp.transpose(decg, (0, 2, 1)))


def solution(mesh):
    sizes = tuple(mesh.shape[a] for a in AXES)
    spec = P(None, "gx", "gy", "gz")
    return jax.shard_map(
        functools.partial(per_device, sizes),
        mesh=mesh,
        in_specs=(spec, P(), P(), P(), P(), spec),
        out_specs=(spec, spec, P(), P(), P(), P()),
        check_vma=False,
    )
```

```python
import functools

import jax
import jax.numpy as jnp
from jax import lax
from jax.experimental import pallas as pl
from jax.experimental.pallas import tpu as pltpu
from jax.sharding import PartitionSpec as P

AXES = ("gx", "gy", "gz")
BF = jnp.bfloat16
F32 = jnp.float32
MESH = pl.DeviceIdType.MESH
DIRS = tuple((dx, dy) for dy in (-1, 1, 0) for dx in (-1, 1, 0) if (dx, dy) != (0, 0))


def dot(a, b):
    return jnp.dot(a, b, preferred_element_type=F32)


def dot_nt(a, b):
    return lax.dot_general(a, b, (((1,), (1,)), ((), ())), preferred_element_type=F32)


def dot_tn(a, b):
    return lax.dot_general(a, b, (((0,), (0,)), ((), ())), preferred_element_type=F32)


def zero_one(shape, rule):
    return rule(lax.broadcasted_iota(jnp.int32, shape, 0), lax.broadcasted_iota(jnp.int32, shape, 1))


def arrange_weights(enc, coarse, upt, dec, we, wd, wdb, wc, wcb, web, up):
    flat = enc[...].reshape(256, 27)
    same_in = zero_one((256, 144), lambda r, l: r // 16 == l % 16)
    same_out = zero_one((256, 144), lambda r, l: r % 16 == l % 16)
    fold_in = zero_one((16, 256), lambda r, l: r == l % 16).astype(BF)
    fold_out = zero_one((16, 256), lambda r, l: r == l // 16).astype(BF)
    for a in range(3):
        ahead = dot(flat, zero_one((27, 144), lambda r, l: r == 9 * a + l // 16).astype(BF))
        we[16 * a:16 * a + 16] = dot(fold_in, jnp.where(same_in, ahead, 0.0).astype(BF)).astype(BF)
        back = dot(flat, zero_one((27, 144), lambda r, l: r == 26 - 9 * a - l // 16).astype(BF))
        web[16 * a:16 * a + 16] = dot(fold_out, jnp.where(same_out, back, 0.0).astype(BF)).astype(BF)
    totals = [0.0] * 4
    for t in range(9):
        wide = zero_one((32, 288), lambda r, l: l == 32 * t + r).astype(BF)
        slim = zero_one((16, 144), lambda r, l: l == 16 * t + r).astype(BF)
        ahead, back = (t, 9 + t, 18 + t), (26 - t, 17 - t, 8 - t)
        totals[0] += dot(jnp.concatenate([dec[k] for k in ahead], axis=0), wide)
        totals[1] += dot_tn(jnp.concatenate([dec[k] for k in back], axis=1), slim)
        totals[2] += dot_tn(jnp.concatenate([coarse[k] for k in ahead], axis=1), slim)
        totals[3] += dot(jnp.concatenate([coarse[k] for k in back], axis=0), wide)
    for ref, total in zip((wd, wdb, wc, wcb), totals):
        ref[...] = total.astype(BF)
    up[...] = dot_tn(upt[...], zero_one((16, 16), lambda r, l: r == l).astype(BF)).astype(BF)


def finish(split, dec, vg, total, dec_out, vg_out, enc_out, coarse_out, up_out, decg_out,
           enc, coarse, up, decg, sems):
    copies = [pltpu.make_async_copy(a, b, sems.at[k]) for k, (a, b) in enumerate(
        ((dec, dec_out), (vg, vg_out), (enc, enc_out), (coarse, coarse_out), (up, up_out), (decg, decg_out)))]
    copies[0].start()
    copies[1].start()

    def tile(which, k):
        return total[which * split + k]

    eye = zero_one((128, 128), lambda r, l: r == l).astype(BF)
    for c in range(3):
        block = jnp.concatenate([tile(0, 6 + c), tile(1, 3 + c)], axis=0)
        turned = dot_nt(eye, block).reshape(8, 16, 32)
        for g in range(8):
            decg[3 * g + c] = turned[g]
        skip_last = dot_nt(zero_one((16, 128), lambda r, l: l == 16 * c + r).astype(BF), tile(0, 10))
        upper_last = dot_nt(zero_one((16, 128), lambda r, l: l == 48 + 16 * c + r).astype(BF), tile(1, 6))
        decg[24 + c] = jnp.concatenate([skip_last, upper_last], axis=1)
    copies[5].start()
    for c in range(3):
        for half in range(2):
            block = tile(0, 3 * half + c)
            for g in range(4):
                pick = zero_one((128, 32), lambda r, l: r == 32 * g + l).astype(BF)
                coarse[3 * (4 * half + g) + c] = dot(block, pick)
        pick = zero_one((128, 32), lambda r, l: r == 32 * c + l).astype(BF)
        coarse[24 + c] = dot(tile(0, 9), pick)
    copies[3].start()
    up[...] = jnp.concatenate(
        [dot_nt(zero_one((16, 128), lambda r, l: l == 96 + 16 * k + r).astype(BF), tile(0, 9)) for k in range(2)], axis=1)
    copies[4].start()
    grow = zero_one((256, 16), lambda r, l: l == r // 16).astype(BF)
    same = zero_one((256, 128), lambda r, l: r % 16 == l % 16)
    flat = jnp.zeros((256, 27), F32)
    for c in range(3):
        wide = jnp.where(same, dot(grow, tile(1, c)), 0.0).astype(BF)
        flat = flat + dot(wide, zero_one((128, 27), lambda r, l: l == 3 * (r // 16) + c).astype(BF))
        wide = jnp.where(same, dot(grow, tile(1, 6)), 0.0).astype(BF)
        flat = flat + dot(wide, zero_one((128, 27), lambda r, l: (r // 16 == c) & (l == 24 + c)).astype(BF))
    enc[...] = flat.reshape(16, 16, 27)
    copies[2].start()
    for c in copies:
        c.wait()


def all_of(*conds):
    total = None
    for c in conds:
        if c is not None:
            total = c if total is None else jnp.logical_and(total, c)
    return total


def span(step, size, halo):
    if step == 0:
        return (0, size), (halo, size)
    if step > 0:
        return (size - halo, halo), (0, halo)
    return (0, halo), (halo + size, halo)


def kernel(sizes, vc, enc_in, coarse_in, upt_in, dec_in, dec_out, vg_out, sum_out,
           enc_w, coarse_w, upt, dec_w, we, wd, wdb, wc, wcb, web, up, turn,
           vct, pk, er, vs, cs, skip, slope, jg, ughi, uglo, ug, ph, ps, act, uh, gh, gs, js, eh, es,
           gr0, gr1, ar0, ar1,
           vsend, vrecv, zsend, zrecv, psend, precv, gsend, grecv, usend, urecv, ssend, srecv, esend, erecv,
           asend0, arecv0, asend1, arecv1, wsem):
    nx, ny, nz = sizes
    ix, iy, iz = (lax.axis_index(a) for a in AXES)
    depth, height, _, width = vc.shape
    chans = vc.shape[2] // 2
    cd, ch = depth // 2, height // 2

    def exists(step, index, count):
        return None if step == 0 else (index + step < count if step > 0 else index + step >= 0)

    def at(dx, dy, dz=0):
        return (ix + dx, iy + dy, iz + dz)

    def guarded(cond, f):
        if cond is None:
            f()
        else:
            pl.when(cond)(f)

    sends = [all_of(exists(dx, ix, nx), exists(dy, iy, ny)) for dx, dy in DIRS]
    recvs = [all_of(exists(-dx, ix, nx), exists(-dy, iy, ny)) for dx, dy in DIRS]
    ends = tuple((dx, dy, s) for dy in (-1, 1, 0) for dx in (-1, 1, 0) for s in (-1, 1))
    esends = [all_of(exists(dx, ix, nx), exists(dy, iy, ny), exists(dz, iz, nz)) for dx, dy, dz in ends]
    erecvs = [all_of(exists(-dx, ix, nx), exists(-dy, iy, ny), exists(-dz, iz, nz)) for dx, dy, dz in ends]

    cores = min(2, nx)
    lows, across = nx // cores, ny // 2 if ny > 4 else ny
    highs = ny // across
    core, y_low, x_at, y_high = lax.rem(ix, cores), ix // cores, lax.rem(iy, across), iy // across
    groups = (
        (cores * across, core * across + x_at,
         lambda j: (y_low * cores + j // across, y_high * across + lax.rem(j, across), iz)),
        (highs * lows, y_high * lows + y_low,
         lambda j: (lax.rem(j, lows) * cores + core, (j // lows) * across + x_at, iz)),
        (nz, iz, lambda j: (ix, iy, j)),
    )

    barrier = pltpu.get_barrier_semaphore()

    def greet(device):
        pl.semaphore_signal(barrier, inc=1, device_id=device, device_id_type=MESH)

    for dx, dy, dz in list(ends) + [d + (0,) for d in DIRS]:
        if dx != 0 or dy != 0:
            guarded(all_of(exists(dx, ix, nx), exists(dy, iy, ny), exists(dz, iz, nz)),
                    lambda dx=dx, dy=dy, dz=dz: greet(at(dx, dy, dz)))

    for count, me, member in groups:
        for k in range(1, count):
            greet(member(lax.rem(me + k, count)))
    def both(index, count):
        return (jnp.where(index > 0, 1, 0) + jnp.where(index < count - 1, 1, 0)).astype(jnp.int32)

    loads = [pltpu.make_async_copy(a, b, wsem.at[k]) for k, (a, b) in enumerate(
        ((enc_in, enc_w), (coarse_in, coarse_w), (upt_in, upt), (dec_in, dec_w)))]
    for c in loads:
        c.start()

    row = lax.broadcasted_iota(jnp.int32, (width, 2 * width), 0)
    lane = lax.broadcasted_iota(jnp.int32, (width, 2 * width), 1)
    total = jnp.zeros((depth * chans, 2 * width), F32)
    for n in range(2):
        for y in range(height):
            base = 64 * n + 8 * y
            pick = ((lane == base + row) & (row < 8)) | ((lane == width + base + row - 120) & (row >= 120))
            total = total + dot(vc[:, y, n * chans:(n + 1) * chans].reshape(depth * chans, width), pick.astype(BF))
    for side in range(2):
        pk[side] = total[:, side * width:(side + 1) * width].astype(BF).reshape(depth, chans, width)
    bx, by, bz = both(ix, nx), both(iy, ny), both(iz, nz)
    near = bx + by + bx * by
    pl.semaphore_wait(barrier, sum(count - 1 for count, _, _ in groups) + near + near * bz)

    def exchange(src, src_at, dst, dst_at, send_sem, recv_sem):
        copies = []
        for d, (dx, dy) in enumerate(DIRS):
            copies.append(pltpu.make_async_remote_copy(
                src_ref=src.at[src_at(dx, dy)], dst_ref=dst.at[dst_at(dx, dy)],
                send_sem=send_sem.at[d], recv_sem=recv_sem.at[d],
                device_id=at(dx, dy), device_id_type=MESH))
        return copies

    def begin(copies, conds):
        for c, s in zip(copies, conds):
            guarded(s, c.start)

    def landed(copies, conds):
        for c, r in zip(copies, conds):
            guarded(r, c.wait_recv)

    def landed_rows(copies, conds, dirs, rim):
        part = [i for i, d in enumerate(dirs) if (d[1] != 0) == rim]
        landed([copies[i] for i in part], [conds[i] for i in part])

    def left(copies, conds):
        for c, s in zip(copies, conds):
            guarded(s, c.wait_send)

    def rim_src(halo, d0, h0, off):
        def f(dx, dy):
            (a, n), _ = span(dx, d0, halo)
            (b, m), _ = span(dy, h0, halo)
            return (pl.ds(a + off, n), pl.ds(b + off, m))
        return f

    def rim_dst(halo, d0, h0):
        def f(dx, dy):
            _, (a, n) = span(dx, d0, halo)
            _, (b, m) = span(dy, h0, halo)
            return (pl.ds(a, n), pl.ds(b, m))
        return f

    vcopies = exchange(vc, rim_src(1, depth, height, 0), vct, rim_dst(1, depth, height), vsend, vrecv)
    begin(vcopies, sends)

    zcopies = []
    for d, (dx, dy, dz) in enumerate(ends):
        (a, n), (b, m) = span(dx, depth, 1)
        side = 1 if dz > 0 else 0
        zcopies.append(pltpu.make_async_remote_copy(
            src_ref=pk.at[side, pl.ds(a, n)], dst_ref=er.at[side, 1 - dy, pl.ds(b, m)],
            send_sem=zsend.at[d], recv_sem=zrecv.at[d],
            device_id=at(dx, dy, dz), device_id_type=MESH))
    begin(zcopies, esends)
    vct[1:1 + depth, 1:1 + height] = vc[...]

    def clear(ref, d0, h0):
        for d, (dx, dy) in enumerate(DIRS):
            _, (a, n) = span(dx, d0, 1)
            _, (b, m) = span(dy, h0, 1)

            def zero(a=a, n=n, b=b, m=m):
                ref[a:a + n, b:b + m] = jnp.zeros((n, m) + ref.shape[2:], ref.dtype)

            if recvs[d] is not None:
                pl.when(jnp.logical_not(recvs[d]))(zero)

    for ref in (vct, skip, eh):
        clear(ref, depth, height)
    for ref in (ph, uh, gh):
        clear(ref, cd, ch)
    for d, (dx, dy, dz) in enumerate(ends):
        _, (b, m) = span(dx, depth, 1)

        def zero(side=1 if dz > 0 else 0, dyi=1 - dy, b=b, m=m):
            er[side, dyi, b:b + m] = jnp.zeros((m, chans, width), BF)

        pl.when(jnp.logical_not(erecvs[d]))(zero)

    for c in loads:
        c.wait()
    arrange_weights(enc_w, coarse_w, upt, dec_w, we, wd, wdb, wc, wcb, web, up)

    def shifted(wide, c):
        if c == 1:
            return wide
        return pltpu.roll(wide, 1 if c == 0 else wide.shape[1] - 1, 1)

    def fill_inputs(y, _):
        dyi, base = (y + 7) // 8, 8 * lax.rem(y + 7, 8)
        flat = ((depth + 2) * chans, width)
        kind, spot = lane // width, lax.rem(lane, width)
        source = base + 64 * kind + spot
        lo = (row == source - 120) & (spot >= 120)
        hi = (row == source) & (spot < 8)
        got = dot(er[1, dyi].reshape(flat), lo.astype(BF)) + dot(er[0, dyi].reshape(flat), hi.astype(BF))
        for n, ref in enumerate((vs, cs)):
            own = vct[:, y, n * chans:(n + 1) * chans].reshape(flat).astype(F32)
            wide = jnp.concatenate([own, got[:, n * width:(n + 1) * width]], axis=1)
            for c in range(3):
                ref[:, y, c] = shifted(wide, c).astype(BF).reshape(depth + 2, chans, 2 * width)


    sets = ((gr0, ar0, asend0, arecv0), (gr1, ar1, asend1, arecv1))

    def ring(which, phase):
        gr, ar, asend, arecv = sets[which]
        count, me, member = groups[phase % 3]
        per = gr.shape[0] // groups[0][0]
        out, got = [], []
        for k in sorted(range(1, count), key=lambda k: abs(2 * k - count)):
            to = lax.rem(me + k, count)
            frm = lax.rem(me - k + count, count)
            src = gr.at[pl.ds(to * per, per)] if phase == 0 else ar.at[phase, me]

            def copy(slot):
                return pltpu.make_async_remote_copy(
                    src_ref=src, dst_ref=ar.at[phase, slot], send_sem=asend.at[phase, k - 1],
                    recv_sem=arecv.at[phase, k - 1], device_id=member(to), device_id_type=MESH)

            out.append(copy(me))
            got.append(copy(frm))
        for c in out:
            c.start()
        if phase == 0:
            ar[0, me] = gr[pl.ds(me * per, per)]
        everything.extend(out)
        return got

    everything = []

    def advance(which, copies, phase):
        ar = sets[which][1]
        for c in copies:
            c.wait_recv()
        total = ar[phase, 0].astype(F32)
        for k in range(1, groups[phase][0]):
            total = total + ar[phase, k].astype(F32)
        ar[phase + 1, groups[(phase + 1) % 3][1]] = total.astype(BF)
        return ring(which, phase + 1)

    fine = lax.broadcasted_iota(jnp.int32, (1, 2 * width), 1)
    coarse = lax.broadcasted_iota(jnp.int32, (1, width), 1)
    low_ok = jnp.where(iz > 0, 1.0, 0.0).astype(F32)
    high_ok = jnp.where(iz < nz - 1, 1.0, 0.0).astype(F32)
    fine_mask = jnp.where(fine < width, 1.0, jnp.where(fine < 3 * width // 2, high_ok, low_ok))
    coarse_mask = jnp.where(coarse < width // 2, 1.0, jnp.where(coarse < 3 * width // 4, high_ok, low_ok))
    own_coarse = coarse < width // 2

    def conv_row(weight, planes, outs):
        m = weight.shape[0] // 3
        ys = [dot(weight, x) for x in planes]
        return [ys[p][:m] + ys[p + 1][m:2 * m] + ys[p + 2][2 * m:] for p in range(outs)]

    def enc_row(q, _):
        k = 9 * chans
        pre = conv_row(we[...], [vs[p, pl.ds(q, 3)].reshape(k, 2 * width) for p in range(depth + 2)], depth)
        for p in range(depth):
            t = pre[p]
            sig = 1.0 / (1.0 + jnp.exp(-t))
            skip[1 + p, 1 + q] = (t * sig * fine_mask).astype(BF)
            slope[p, q] = sig * (1.0 + t * (1.0 - sig)) * fine_mask

    landed_rows(zcopies, erecvs, ends, False)
    landed_rows(vcopies, recvs, DIRS, False)
    lax.fori_loop(1, height + 1, fill_inputs, None)
    lax.fori_loop(1, height - 1, enc_row, None)
    landed_rows(zcopies, erecvs, ends, True)
    landed_rows(vcopies, recvs, DIRS, True)
    for y in (0, height + 1):
        fill_inputs(y, None)
    for q in (0, height - 1):
        enc_row(q, None)

    pool = (lax.broadcasted_iota(jnp.int32, (2 * width, width), 0) // 2
            == lax.broadcasted_iota(jnp.int32, (2 * width, width), 1)).astype(BF)

    for q in range(ch):
        rows_in = skip[1:1 + depth, 1 + 2 * q:3 + 2 * q].reshape(depth * 2 * chans, 2 * width)
        half = dot(rows_in, pool).reshape(cd, 4, chans, width)
        ph[1:1 + cd, 1 + q] = ((half[:, 0] + half[:, 1] + half[:, 2] + half[:, 3]) * 0.125).astype(BF)
    pcopies = exchange(ph, rim_src(1, cd, ch, 1), ph, rim_dst(1, cd, ch), psend, precv)
    begin(pcopies, sends)
    scopies = exchange(skip, rim_src(1, depth, height, 1), skip, rim_dst(1, depth, height), ssend, srecv)
    begin(scopies, sends)

    def joined_row(q, _):
        k = 9 * chans
        sums = [jnp.zeros((chans, 2 * width), F32) for _ in range(cd)]
        for e in range(2):
            r = 2 * q + e
            out = conv_row(wdb[...], [cs[p, pl.ds(r, 3)].reshape(k, 2 * width) for p in range(depth + 2)], depth)
            for p in range(depth):
                jg[p, r] = out[p][:chans]
                sums[p // 2] = sums[p // 2] + out[p][chans:]
        for p in range(cd):
            hi = sums[p].astype(BF)
            ughi[p, q] = hi
            uglo[p, q] = (sums[p] - hi.astype(F32)).astype(BF)

    lax.fori_loop(0, ch, joined_row, None)
    flat = (cd * ch * chans, 2 * width)
    grad = dot(ughi[...].reshape(flat), pool) + dot(uglo[...].reshape(flat), pool)
    ug[...] = grad.astype(BF).reshape(ug.shape)

    def fill_pooled(q, _):
        wide = ph[:, q].reshape((cd + 2) * chans, width).astype(F32)
        for c in range(3):
            ps[:, q, c] = shifted(wide, c).astype(BF).reshape(cd + 2, chans, width)

    landed_rows(pcopies, recvs, DIRS, False)
    lax.fori_loop(1, ch + 1, fill_pooled, None)
    def coarse_row(q):
        k = 9 * chans
        pre = conv_row(wc[...], [ps[p, q:q + 3].reshape(k, width) for p in range(cd + 2)], cd)
        for p in range(cd):
            t = pre[p]
            sig = 1.0 / (1.0 + jnp.exp(-t))
            a = (t * sig * coarse_mask).astype(BF)
            act[p, q] = a
            uh[1 + p, 1 + q] = dot(upt[...], a).astype(BF)
            back = dot(up[...], ug[p, q])
            gh[1 + p, 1 + q] = (back * (sig * (1.0 + t * (1.0 - sig)) * coarse_mask)).astype(BF)

    for q in range(1, ch - 1):
        coarse_row(q)
    landed_rows(pcopies, recvs, DIRS, True)
    for q in (0, ch + 1):
        fill_pooled(q, None)
    for q in (0, ch - 1):
        coarse_row(q)
    gcopies = exchange(gh, rim_src(1, cd, ch, 1), gh, rim_dst(1, cd, ch), gsend, grecv)
    begin(gcopies, sends)
    ucopies = exchange(uh, rim_src(1, cd, ch, 1), uh, rim_dst(1, cd, ch), usend, urecv)
    begin(ucopies, sends)

    group16 = lax.broadcasted_iota(jnp.int32, (1, width), 1) // 16
    group32 = lax.broadcasted_iota(jnp.int32, (1, width), 1) // 32

    def tap_sums(block, step, groups, gid):
        out = []
        for b in range(3):
            total = jnp.zeros((step, width), F32)
            for q in range(groups):
                total = jnp.where(gid == q, block[(q + b) * step:(q + b + 1) * step], total)
            size = width // 2
            while size >= width // groups:
                total = total + pltpu.roll(total, size, 1)
                size //= 2
            out.append(total)
        return out

    def put(ref, first, value):
        tiles = value.shape[0] // 16
        ref[first:first + tiles] = value.astype(BF).reshape(tiles, 16, width)

    def place(total, gid, first, block):
        for k in range(block.shape[0] // 16):
            total = jnp.where(gid == first + k, block[16 * k:16 * k + 16], total)
        return total

    for ref, used in ((gr0, 11), (gr1, 7)):
        if ref.shape[0] > used:
            ref[used:] = jnp.zeros((ref.shape[0] - used, 16, width), BF)
    blank = jnp.zeros((16, width), F32)
    step = 3 * chans
    taps = []
    masked = [jnp.where(own_coarse, gh[1 + p, 1:1 + ch].reshape(2 * chans * ch, width), 0)
              for p in range(cd)]
    for a in range(3):
        block = sum(dot_nt(ps[p + a].reshape((ch + 2) * step, width), masked[p]) for p in range(cd))
        taps += tap_sums(block, step, ch, group32)
    for half in range(2):
        total = jnp.zeros((step, width), F32)
        for g in range(4):
            total = jnp.where(group32 == g, taps[4 * half + g], total)
        put(gr0, 3 * half, total)
    side = place(blank, group32, 0, taps[8])
    up_total = jnp.zeros((2 * chans, width), F32)
    for p in range(cd):
        for q in range(ch):
            g = jnp.where(own_coarse, ug[p, q], 0)
            up_total = up_total + dot_nt(act[p, q], jnp.concatenate([g] * 8, axis=0))
    side = place(side, group16, 6, up_total)
    put(gr0, 9, side)

    def fill_skip(first, count, y):
        wide = skip[first:first + count, y].reshape(count * chans, 2 * width).astype(F32)
        for c in range(3):
            part = shifted(wide, c)[:, :width]
            js[first:first + count, y, c, 0:chans] = part.astype(BF).reshape(count, chans, width)

    lax.fori_loop(1, height + 1, lambda y, _: fill_skip(1, depth, y), None)
    landed(scopies, recvs)
    for y in (0, height + 1):
        fill_skip(0, depth + 2, y)

    def fill_sides(y, _):
        fill_skip(0, 1, y)
        fill_skip(depth + 1, 1, y)

    lax.fori_loop(1, height + 1, fill_sides, None)

    def fine_taps(source, step, grads):
        taps = []
        for a in range(3):
            block = sum(dot_nt(source(a + p), grads[p]) for p in range(depth))
            taps += tap_sums(block, step, height, group16)
        total = jnp.zeros((step, width), F32)
        for g in range(8):
            total = jnp.where(group16 == g, taps[g], total)
        return total, taps[8]

    def joined_taps(first):
        return fine_taps(
            lambda x: js[x, :, :, first:first + chans].reshape((height + 2) * 3 * chans, width), 3 * chans,
            [vc[p, :, chans:2 * chans].reshape(height * chans, width) for p in range(depth)])

    total, last = joined_taps(0)
    put(gr0, 6, total)
    put(gr0, 10, place(blank, group16, 0, last))
    early = ring(0, 0)

    def fill_coarse(y, _):
        wide = gh[:, y].reshape((cd + 2) * 2 * chans, width).astype(F32)
        for c in range(3):
            gs[:, y, c] = shifted(wide, c).astype(BF).reshape(cd + 2, 2 * chans, width)

    landed_rows(gcopies, recvs, DIRS, False)
    lax.fori_loop(1, ch + 1, fill_coarse, None)
    spread = (lax.broadcasted_iota(jnp.int32, (width, 2 * width), 1) // 2
              == lax.broadcasted_iota(jnp.int32, (width, 2 * width), 0)).astype(BF)

    def back_row(q, _):
        k = 18 * chans
        pg = conv_row(wcb[...], [gs[p, pl.ds(q, 3)].reshape(k, width) for p in range(cd + 2)], cd)
        for p in range(cd):
            v = pg[p] * 0.125
            hi = v.astype(BF)
            lo = (v - hi.astype(F32)).astype(BF)
            wide = dot(hi, spread) + dot(lo, spread)
            for e in range(2):
                for f in range(2):
                    g = (jg[2 * p + e, 2 * q + f] + wide) * slope[2 * p + e, 2 * q + f]
                    eh[1 + 2 * p + e, 1 + 2 * q + f] = g.astype(BF)

    lax.fori_loop(1, ch - 1, back_row, None)
    landed_rows(gcopies, recvs, DIRS, True)
    for y in (0, ch + 1):
        fill_coarse(y, None)
    for q in (0, ch - 1):
        back_row(q, None)
    ecopies = exchange(eh, rim_src(1, depth, height, 1), eh, rim_dst(1, depth, height), esend, erecv)
    begin(ecopies, sends)
    early = advance(0, early, 0)

    landed(ucopies, recvs)
    low = lax.broadcasted_iota(jnp.int32, (width, width), 0)
    lane = lax.broadcasted_iota(jnp.int32, (width, width), 1)
    for c in range(3):
        source = lax.rem(lane + (c - 1) + 2 * width, 2 * width) // 2
        pick = (low == source).astype(BF)
        wide = dot(uh[...].reshape((cd + 2) * (ch + 2) * chans, width), pick)
        wide = wide.astype(BF).reshape(cd + 2, ch + 2, chans, width)
        for x in range(depth + 2):
            for y in range(height + 2):
                js[x, y, c, chans:2 * chans] = wide[(x + 1) // 2, (y + 1) // 2]

    total, last = joined_taps(chans)
    put(gr1, 3, total)
    side = place(blank, group16, 3, last)
    total, last = fine_taps(
        lambda x: vs[x, :, :, :, 0:width].reshape((height + 2) * 3 * chans, width), 3 * chans,
        [eh[1 + p, 1:1 + height, :, 0:width].reshape(height * chans, width) for p in range(depth)])
    put(gr1, 0, total)
    put(gr1, 6, place(side, group16, 0, last))

    late = ring(1, 0)

    order = zero_one((height * chans, height * chans),
                     lambda r, l: (r // height == l % chans) & (r % height == l // chans)).astype(BF)

    def channels_first(which, ref):
        for p in range(depth):
            moved = dot(order, turn[which, p].reshape(height * chans, width))
            ref[:, p] = moved.reshape(chans, height, width).astype(BF)

    def dec_row(q, _):
        k = 18 * chans
        out = conv_row(wd[...], [js[p, pl.ds(q, 3)].reshape(k, width) for p in range(depth + 2)], depth)
        for p in range(depth):
            turn[0, p, q] = out[p].astype(BF)

    lax.fori_loop(0, height // 2, dec_row, None)

    late = advance(1, late, 0)
    early = advance(0, early, 1)
    lax.fori_loop(height // 2, height, dec_row, None)
    channels_first(0, dec_out)
    landed(ecopies, recvs)

    def fill_enc(y, _):
        wide = eh[:, y].reshape((depth + 2) * chans, 2 * width).astype(F32)
        for c in range(3):
            part = shifted(wide, c)[:, :width]
            es[:, y, c] = part.astype(BF).reshape(depth + 2, chans, width)

    lax.fori_loop(0, height + 2, fill_enc, None)

    def vol_row(q, _):
        k = 9 * chans
        out = conv_row(web[...], [es[p, pl.ds(q, 3)].reshape(k, width) for p in range(depth + 2)], depth)
        for p in range(depth):
            turn[1, p, q] = out[p].astype(BF)

    late = advance(1, late, 1)
    early = advance(0, early, 2)
    lax.fori_loop(0, height // 2, vol_row, None)
    late = advance(1, late, 2)
    lax.fori_loop(height // 2, height, vol_row, None)
    channels_first(1, vg_out)
    for c in early + late:
        c.wait_recv()
    sum_out[0:gr0.shape[0]] = ar0[3, 0:groups[0][0]].reshape(gr0.shape)
    sum_out[gr0.shape[0]:] = ar1[3, 0:groups[0][0]].reshape(gr1.shape)

    left(zcopies, esends)
    for copies in (vcopies, pcopies, gcopies, ucopies, scopies, ecopies):
        left(copies, sends)
    for c in everything:
        c.wait_send()


def per_device(sizes, volume, enc_weight, coarse_weight, up_weight, dec_weight, cotangent):
    nx, ny, nz = sizes
    chans, d, h, w = volume.shape
    cd, ch = d // 2, h // 2
    owners = min(2, nx) * (ny // 2 if ny > 4 else ny)
    pers = (-(-11 // owners), -(-7 // owners))
    pair = jnp.transpose(jnp.concatenate([volume, cotangent], axis=0), (1, 2, 0, 3))
    operands = (
        pair, jnp.transpose(enc_weight, (1, 2, 0)), coarse_weight, up_weight.T, jnp.transpose(dec_weight, (0, 2, 1)))
    c2 = 2 * chans
    widest = max(owners, nx * ny // owners, nz) - 1
    scratch = [
        ((16, 16, 27), BF),
        ((27, 16, 32), BF),
        ((16, 32), BF),
        ((27, 16, 32), BF),
        ((48, 144), BF),
        ((48, 288), BF),
        ((96, 144), BF),
        ((96, 144), BF),
        ((48, 288), BF),
        ((48, 144), BF),
        ((32, 16), BF),
        ((2, d, h, chans, w), BF),
        ((d + 2, h + 2, c2, w), BF),
        ((2, d, chans, w), BF),
        ((2, 3, d + 2, chans, w), BF),
        ((d + 2, h + 2, 3, chans, 2 * w), BF),
        ((d + 2, h + 2, 3, chans, 2 * w), BF),
        ((d + 2, h + 2, chans, 2 * w), BF),
        ((d, h, chans, 2 * w), F32),
        ((d, h, chans, 2 * w), F32),
        ((cd, ch, chans, 2 * w), BF),
        ((cd, ch, chans, 2 * w), BF),
        ((cd, ch, chans, w), BF),
        ((cd + 2, ch + 2, chans, w), BF),
        ((cd + 2, ch + 2, 3, chans, w), BF),
        ((cd, ch, c2, w), BF),
        ((cd + 2, ch + 2, chans, w), BF),
        ((cd + 2, ch + 2, c2, w), BF),
        ((cd + 2, ch + 2, 3, c2, w), BF),
        ((d + 2, h + 2, 3, c2, w), BF),
        ((d + 2, h + 2, chans, 2 * w), BF),
        ((d + 2, h + 2, 3, chans, w), BF),
        ((owners * pers[0], 16, w), BF),
        ((owners * pers[1], 16, w), BF),
        ((4, widest + 1, pers[0], 16, w), BF),
        ((4, widest + 1, pers[1], 16, w), BF),
    ]
    dma = pltpu.SemaphoreType.DMA
    sems = [dma((8,))] * 2 + [dma((18,))] * 2 + [dma((8,))] * 10 + [dma((4, max(widest, 1)))] * 4 + [dma((4,))]
    hbm = pl.BlockSpec(memory_space=pl.ANY)
    vmem = pl.BlockSpec(memory_space=pltpu.VMEM)
    dec, vg, total = pl.pallas_call(
        functools.partial(kernel, sizes),
        out_shape=(
            jax.ShapeDtypeStruct((chans, d, h, w), BF),
            jax.ShapeDtypeStruct((chans, d, h, w), BF),
            jax.ShapeDtypeStruct((owners * sum(pers), 16, w), BF)),
        in_specs=[vmem] + [hbm] * 4,
        out_specs=(vmem,) * 3,
        scratch_shapes=[pltpu.VMEM(s, t) for s, t in scratch] + sems,
        compiler_params=pltpu.CompilerParams(
            collective_id=0, has_side_effects=True, vmem_limit_bytes=48 * 1024 * 1024),
    )(*operands)
    grads = ((16, 16, 27), (27, 16, 32), (16, 32), (27, 16, 32))
    dec, vg, enc, coarse, upg, decg = pl.pallas_call(
        functools.partial(finish, owners * pers[0]),
        out_shape=tuple(jax.ShapeDtypeStruct(x.shape, BF) for x in (dec, vg))
        + tuple(jax.ShapeDtypeStruct(x, F32) for x in grads),
        in_specs=[vmem] * 3,
        out_specs=(hbm,) * 6,
        scratch_shapes=[pltpu.VMEM(x, F32) for x in grads] + [dma((6,))],
        compiler_params=pltpu.CompilerParams(vmem_limit_bytes=8 * 1024 * 1024),
    )(dec, vg, total)
    return (dec, vg, jnp.transpose(enc, (2, 0, 1)), coarse, upg.T, jnp.transpose(decg, (0, 2, 1)))


def solution(mesh):
    sizes = tuple(mesh.shape[a] for a in AXES)
    spec = P(None, "gx", "gy", "gz")
    return jax.shard_map(
        functools.partial(per_device, sizes),
        mesh=mesh,
        in_specs=(spec, P(), P(), P(), P(), spec),
        out_specs=(spec, spec, P(), P(), P(), P()),
        check_vma=False,
    )
```

```python
import functools

import jax
import jax.numpy as jnp
from jax import lax
from jax.experimental import pallas as pl
from jax.experimental.pallas import tpu as pltpu
from jax.sharding import PartitionSpec as P

AXES = ("gx", "gy", "gz")
BF = jnp.bfloat16
F32 = jnp.float32
MESH = pl.DeviceIdType.MESH
DIRS = tuple((dx, dy) for dy in (-1, 1, 0) for dx in (-1, 1, 0) if (dx, dy) != (0, 0))


def dot(a, b):
    return jnp.dot(a, b, preferred_element_type=F32)


def dot_nt(a, b):
    return lax.dot_general(a, b, (((1,), (1,)), ((), ())), preferred_element_type=F32)


def dot_tn(a, b):
    return lax.dot_general(a, b, (((0,), (0,)), ((), ())), preferred_element_type=F32)


def zero_one(shape, rule):
    return rule(lax.broadcasted_iota(jnp.int32, shape, 0), lax.broadcasted_iota(jnp.int32, shape, 1))


def arrange_weights(enc, coarse, upt, dec, we, wd, wdb, wc, wcb, web, up):
    flat = enc[...].reshape(256, 27)
    same_in = zero_one((256, 144), lambda r, l: r // 16 == l % 16)
    same_out = zero_one((256, 144), lambda r, l: r % 16 == l % 16)
    fold_in = zero_one((16, 256), lambda r, l: r == l % 16).astype(BF)
    fold_out = zero_one((16, 256), lambda r, l: r == l // 16).astype(BF)
    for a in range(3):
        ahead = dot(flat, zero_one((27, 144), lambda r, l: r == 9 * a + l // 16).astype(BF))
        we[16 * a:16 * a + 16] = dot(fold_in, jnp.where(same_in, ahead, 0.0).astype(BF)).astype(BF)
        back = dot(flat, zero_one((27, 144), lambda r, l: r == 26 - 9 * a - l // 16).astype(BF))
        web[16 * a:16 * a + 16] = dot(fold_out, jnp.where(same_out, back, 0.0).astype(BF)).astype(BF)
    totals = [0.0] * 4
    for t in range(9):
        wide = zero_one((32, 288), lambda r, l: l == 32 * t + r).astype(BF)
        slim = zero_one((16, 144), lambda r, l: l == 16 * t + r).astype(BF)
        ahead, back = (t, 9 + t, 18 + t), (26 - t, 17 - t, 8 - t)
        totals[0] += dot(jnp.concatenate([dec[k] for k in ahead], axis=0), wide)
        totals[1] += dot_tn(jnp.concatenate([dec[k] for k in back], axis=1), slim)
        totals[2] += dot_tn(jnp.concatenate([coarse[k] for k in ahead], axis=1), slim)
        totals[3] += dot(jnp.concatenate([coarse[k] for k in back], axis=0), wide)
    for ref, total in zip((wd, wdb, wc, wcb), totals):
        ref[...] = total.astype(BF)
    up[...] = dot_tn(upt[...], zero_one((16, 16), lambda r, l: r == l).astype(BF)).astype(BF)


def finish(split, dec, vg, total, dec_out, vg_out, enc_out, coarse_out, up_out, decg_out,
           enc, coarse, up, decg, sems):
    copies = [pltpu.make_async_copy(a, b, sems.at[k]) for k, (a, b) in enumerate(
        ((dec, dec_out), (vg, vg_out), (enc, enc_out), (coarse, coarse_out), (up, up_out), (decg, decg_out)))]
    copies[0].start()
    copies[1].start()

    def tile(which, k):
        return total[which * split + k]

    eye = zero_one((128, 128), lambda r, l: r == l).astype(BF)
    for c in range(3):
        block = jnp.concatenate([tile(0, 6 + c), tile(1, 3 + c)], axis=0)
        turned = dot_nt(eye, block).reshape(8, 16, 32)
        for g in range(8):
            decg[3 * g + c] = turned[g]
        skip_last = dot_nt(zero_one((16, 128), lambda r, l: l == 16 * c + r).astype(BF), tile(0, 10))
        upper_last = dot_nt(zero_one((16, 128), lambda r, l: l == 48 + 16 * c + r).astype(BF), tile(1, 6))
        decg[24 + c] = jnp.concatenate([skip_last, upper_last], axis=1)
    copies[5].start()
    for c in range(3):
        for half in range(2):
            block = tile(0, 3 * half + c)
            for g in range(4):
                pick = zero_one((128, 32), lambda r, l: r == 32 * g + l).astype(BF)
                coarse[3 * (4 * half + g) + c] = dot(block, pick)
        pick = zero_one((128, 32), lambda r, l: r == 32 * c + l).astype(BF)
        coarse[24 + c] = dot(tile(0, 9), pick)
    copies[3].start()
    up[...] = jnp.concatenate(
        [dot_nt(zero_one((16, 128), lambda r, l: l == 96 + 16 * k + r).astype(BF), tile(0, 9)) for k in range(2)], axis=1)
    copies[4].start()
    grow = zero_one((256, 16), lambda r, l: l == r // 16).astype(BF)
    same = zero_one((256, 128), lambda r, l: r % 16 == l % 16)
    flat = jnp.zeros((256, 27), F32)
    for c in range(3):
        wide = jnp.where(same, dot(grow, tile(1, c)), 0.0).astype(BF)
        flat = flat + dot(wide, zero_one((128, 27), lambda r, l: l == 3 * (r // 16) + c).astype(BF))
        wide = jnp.where(same, dot(grow, tile(1, 6)), 0.0).astype(BF)
        flat = flat + dot(wide, zero_one((128, 27), lambda r, l: (r // 16 == c) & (l == 24 + c)).astype(BF))
    enc[...] = flat.reshape(16, 16, 27)
    copies[2].start()
    for c in copies:
        c.wait()


def all_of(*conds):
    total = None
    for c in conds:
        if c is not None:
            total = c if total is None else jnp.logical_and(total, c)
    return total


def span(step, size, halo):
    if step == 0:
        return (0, size), (halo, size)
    if step > 0:
        return (size - halo, halo), (0, halo)
    return (0, halo), (halo + size, halo)


def kernel(sizes, vc, enc_in, coarse_in, upt_in, dec_in, dec_out, vg_out, sum_out,
           enc_w, coarse_w, upt, dec_w, we, wd, wdb, wc, wcb, web, up, turn,
           vct, pk, er, vs, cs, skip, slope, jg, ughi, uglo, ug, ph, ps, act, uh, gh, gs, js, eh, es,
           gr0, gr1, ar0, ar1,
           vsend, vrecv, zsend, zrecv, psend, precv, gsend, grecv, usend, urecv, ssend, srecv, esend, erecv,
           asend0, arecv0, asend1, arecv1, wsem):
    nx, ny, nz = sizes
    ix, iy, iz = (lax.axis_index(a) for a in AXES)
    depth, height, _, width = vc.shape
    chans = vc.shape[2] // 2
    cd, ch = depth // 2, height // 2

    def exists(step, index, count):
        return None if step == 0 else (index + step < count if step > 0 else index + step >= 0)

    def at(dx, dy, dz=0):
        return (ix + dx, iy + dy, iz + dz)

    def guarded(cond, f):
        if cond is None:
            f()
        else:
            pl.when(cond)(f)

    sends = [all_of(exists(dx, ix, nx), exists(dy, iy, ny)) for dx, dy in DIRS]
    recvs = [all_of(exists(-dx, ix, nx), exists(-dy, iy, ny)) for dx, dy in DIRS]
    ends = tuple((dx, dy, s) for dy in (-1, 1, 0) for dx in (-1, 1, 0) for s in (-1, 1))
    esends = [all_of(exists(dx, ix, nx), exists(dy, iy, ny), exists(dz, iz, nz)) for dx, dy, dz in ends]
    erecvs = [all_of(exists(-dx, ix, nx), exists(-dy, iy, ny), exists(-dz, iz, nz)) for dx, dy, dz in ends]

    cores = min(2, nx)
    lows, across = nx // cores, ny // 2 if ny > 4 else ny
    highs = ny // across
    core, y_low, x_at, y_high = lax.rem(ix, cores), ix // cores, lax.rem(iy, across), iy // across
    groups = (
        (cores * across, core * across + x_at,
         lambda j: (y_low * cores + j // across, y_high * across + lax.rem(j, across), iz)),
        (highs * lows, y_high * lows + y_low,
         lambda j: (lax.rem(j, lows) * cores + core, (j // lows) * across + x_at, iz)),
        (nz, iz, lambda j: (ix, iy, j)),
    )

    barrier = pltpu.get_barrier_semaphore()

    def greet(device):
        pl.semaphore_signal(barrier, inc=1, device_id=device, device_id_type=MESH)

    for dx, dy, dz in list(ends) + [d + (0,) for d in DIRS]:
        if dx != 0 or dy != 0:
            guarded(all_of(exists(dx, ix, nx), exists(dy, iy, ny), exists(dz, iz, nz)),
                    lambda dx=dx, dy=dy, dz=dz: greet(at(dx, dy, dz)))

    for count, me, member in groups:
        for k in range(1, count):
            greet(member(lax.rem(me + k, count)))
    def both(index, count):
        return (jnp.where(index > 0, 1, 0) + jnp.where(index < count - 1, 1, 0)).astype(jnp.int32)

    loads = [pltpu.make_async_copy(a, b, wsem.at[k]) for k, (a, b) in enumerate(
        ((enc_in, enc_w), (coarse_in, coarse_w), (upt_in, upt), (dec_in, dec_w)))]
    for c in loads:
        c.start()

    row = lax.broadcasted_iota(jnp.int32, (width, 2 * width), 0)
    lane = lax.broadcasted_iota(jnp.int32, (width, 2 * width), 1)
    total = jnp.zeros((depth * chans, 2 * width), F32)
    for n in range(2):
        for y in range(height):
            base = 64 * n + 8 * y
            pick = ((lane == base + row) & (row < 8)) | ((lane == width + base + row - 120) & (row >= 120))
            total = total + dot(vc[:, y, n * chans:(n + 1) * chans].reshape(depth * chans, width), pick.astype(BF))
    for side in range(2):
        pk[side] = total[:, side * width:(side + 1) * width].astype(BF).reshape(depth, chans, width)
    bx, by, bz = both(ix, nx), both(iy, ny), both(iz, nz)
    near = bx + by + bx * by
    pl.semaphore_wait(barrier, sum(count - 1 for count, _, _ in groups) + near + near * bz)

    def exchange(src, src_at, dst, dst_at, send_sem, recv_sem):
        copies = []
        for d, (dx, dy) in enumerate(DIRS):
            copies.append(pltpu.make_async_remote_copy(
                src_ref=src.at[src_at(dx, dy)], dst_ref=dst.at[dst_at(dx, dy)],
                send_sem=send_sem.at[d], recv_sem=recv_sem.at[d],
                device_id=at(dx, dy), device_id_type=MESH))
        return copies

    def begin(copies, conds):
        for c, s in zip(copies, conds):
            guarded(s, c.start)

    def landed(copies, conds):
        for c, r in zip(copies, conds):
            guarded(r, c.wait_recv)

    def landed_rows(copies, conds, dirs, rim):
        part = [i for i, d in enumerate(dirs) if (d[1] != 0) == rim]
        landed([copies[i] for i in part], [conds[i] for i in part])

    def left(copies, conds):
        for c, s in zip(copies, conds):
            guarded(s, c.wait_send)

    def rim_src(halo, d0, h0, off):
        def f(dx, dy):
            (a, n), _ = span(dx, d0, halo)
            (b, m), _ = span(dy, h0, halo)
            return (pl.ds(a + off, n), pl.ds(b + off, m))
        return f

    def rim_dst(halo, d0, h0):
        def f(dx, dy):
            _, (a, n) = span(dx, d0, halo)
            _, (b, m) = span(dy, h0, halo)
            return (pl.ds(a, n), pl.ds(b, m))
        return f

    vcopies = exchange(vc, rim_src(1, depth, height, 0), vct, rim_dst(1, depth, height), vsend, vrecv)
    begin(vcopies, sends)

    zcopies = []
    for d, (dx, dy, dz) in enumerate(ends):
        (a, n), (b, m) = span(dx, depth, 1)
        side = 1 if dz > 0 else 0
        zcopies.append(pltpu.make_async_remote_copy(
            src_ref=pk.at[side, pl.ds(a, n)], dst_ref=er.at[side, 1 - dy, pl.ds(b, m)],
            send_sem=zsend.at[d], recv_sem=zrecv.at[d],
            device_id=at(dx, dy, dz), device_id_type=MESH))
    begin(zcopies, esends)
    vct[1:1 + depth, 1:1 + height] = vc[...]

    def clear(ref, d0, h0):
        for d, (dx, dy) in enumerate(DIRS):
            _, (a, n) = span(dx, d0, 1)
            _, (b, m) = span(dy, h0, 1)

            def zero(a=a, n=n, b=b, m=m):
                ref[a:a + n, b:b + m] = jnp.zeros((n, m) + ref.shape[2:], ref.dtype)

            if recvs[d] is not None:
                pl.when(jnp.logical_not(recvs[d]))(zero)

    for ref in (vct, skip, eh):
        clear(ref, depth, height)
    for ref in (ph, uh, gh):
        clear(ref, cd, ch)
    for d, (dx, dy, dz) in enumerate(ends):
        _, (b, m) = span(dx, depth, 1)

        def zero(side=1 if dz > 0 else 0, dyi=1 - dy, b=b, m=m):
            er[side, dyi, b:b + m] = jnp.zeros((m, chans, width), BF)

        pl.when(jnp.logical_not(erecvs[d]))(zero)

    for c in loads:
        c.wait()
    arrange_weights(enc_w, coarse_w, upt, dec_w, we, wd, wdb, wc, wcb, web, up)

    def shifted(wide, c):
        if c == 1:
            return wide
        return pltpu.roll(wide, 1 if c == 0 else wide.shape[1] - 1, 1)

    def fill_inputs(y, _):
        dyi, base = (y + 7) // 8, 8 * lax.rem(y + 7, 8)
        flat = ((depth + 2) * chans, width)
        kind, spot = lane // width, lax.rem(lane, width)
        source = base + 64 * kind + spot
        lo = (row == source - 120) & (spot >= 120)
        hi = (row == source) & (spot < 8)
        got = dot(er[1, dyi].reshape(flat), lo.astype(BF)) + dot(er[0, dyi].reshape(flat), hi.astype(BF))
        for n, ref in enumerate((vs, cs)):
            own = vct[:, y, n * chans:(n + 1) * chans].reshape(flat).astype(F32)
            wide = jnp.concatenate([own, got[:, n * width:(n + 1) * width]], axis=1)
            for c in range(3):
                ref[:, y, c] = shifted(wide, c).astype(BF).reshape(depth + 2, chans, 2 * width)


    sets = ((gr0, ar0, asend0, arecv0), (gr1, ar1, asend1, arecv1))

    def ring(which, phase):
        gr, ar, asend, arecv = sets[which]
        count, me, member = groups[phase % 3]
        per = gr.shape[0] // groups[0][0]
        out, got = [], []
        for k in sorted(range(1, count), key=lambda k: abs(2 * k - count)):
            to = lax.rem(me + k, count)
            frm = lax.rem(me - k + count, count)
            src = gr.at[pl.ds(to * per, per)] if phase == 0 else ar.at[phase, me]

            def copy(slot):
                return pltpu.make_async_remote_copy(
                    src_ref=src, dst_ref=ar.at[phase, slot], send_sem=asend.at[phase, k - 1],
                    recv_sem=arecv.at[phase, k - 1], device_id=member(to), device_id_type=MESH)

            out.append(copy(me))
            got.append(copy(frm))
        for c in out:
            c.start()
        if phase == 0:
            ar[0, me] = gr[pl.ds(me * per, per)]
        everything.extend(out)
        return got

    everything = []

    def advance(which, copies, phase):
        ar = sets[which][1]
        for c in copies:
            c.wait_recv()
        total = ar[phase, 0].astype(F32)
        for k in range(1, groups[phase][0]):
            total = total + ar[phase, k].astype(F32)
        ar[phase + 1, groups[(phase + 1) % 3][1]] = total.astype(BF)
        return ring(which, phase + 1)

    fine = lax.broadcasted_iota(jnp.int32, (1, 2 * width), 1)
    coarse = lax.broadcasted_iota(jnp.int32, (1, width), 1)
    low_ok = jnp.where(iz > 0, 1.0, 0.0).astype(F32)
    high_ok = jnp.where(iz < nz - 1, 1.0, 0.0).astype(F32)
    fine_mask = jnp.where(fine < width, 1.0, jnp.where(fine < 3 * width // 2, high_ok, low_ok))
    coarse_mask = jnp.where(coarse < width // 2, 1.0, jnp.where(coarse < 3 * width // 4, high_ok, low_ok))
    own_coarse = coarse < width // 2

    def conv_row(weight, planes, outs):
        m = weight.shape[0] // 3
        ys = [dot(weight, x) for x in planes]
        return [ys[p][:m] + ys[p + 1][m:2 * m] + ys[p + 2][2 * m:] for p in range(outs)]

    def enc_row(q, _):
        k = 9 * chans
        pre = conv_row(we[...], [vs[p, pl.ds(q, 3)].reshape(k, 2 * width) for p in range(depth + 2)], depth)
        for p in range(depth):
            t = pre[p]
            sig = 1.0 / (1.0 + jnp.exp(-t))
            skip[1 + p, 1 + q] = (t * sig * fine_mask).astype(BF)
            slope[p, q] = sig * (1.0 + t * (1.0 - sig)) * fine_mask

    landed_rows(zcopies, erecvs, ends, False)
    landed_rows(vcopies, recvs, DIRS, False)
    lax.fori_loop(1, height + 1, fill_inputs, None)
    lax.fori_loop(1, height - 1, enc_row, None)
    landed_rows(zcopies, erecvs, ends, True)
    landed_rows(vcopies, recvs, DIRS, True)
    for y in (0, height + 1):
        fill_inputs(y, None)
    for q in (0, height - 1):
        enc_row(q, None)

    pool = (lax.broadcasted_iota(jnp.int32, (2 * width, width), 0) // 2
            == lax.broadcasted_iota(jnp.int32, (2 * width, width), 1)).astype(BF)

    for q in range(ch):
        rows_in = skip[1:1 + depth, 1 + 2 * q:3 + 2 * q].reshape(depth * 2 * chans, 2 * width)
        half = dot(rows_in, pool).reshape(cd, 4, chans, width)
        ph[1:1 + cd, 1 + q] = ((half[:, 0] + half[:, 1] + half[:, 2] + half[:, 3]) * 0.125).astype(BF)
    pcopies = exchange(ph, rim_src(1, cd, ch, 1), ph, rim_dst(1, cd, ch), psend, precv)
    begin(pcopies, sends)
    scopies = exchange(skip, rim_src(1, depth, height, 1), skip, rim_dst(1, depth, height), ssend, srecv)
    begin(scopies, sends)

    def joined_row(q, _):
        k = 9 * chans
        sums = [jnp.zeros((chans, 2 * width), F32) for _ in range(cd)]
        for e in range(2):
            r = 2 * q + e
            out = conv_row(wdb[...], [cs[p, pl.ds(r, 3)].reshape(k, 2 * width) for p in range(depth + 2)], depth)
            for p in range(depth):
                jg[p, r] = out[p][:chans]
                sums[p // 2] = sums[p // 2] + out[p][chans:]
        for p in range(cd):
            hi = sums[p].astype(BF)
            ughi[p, q] = hi
            uglo[p, q] = (sums[p] - hi.astype(F32)).astype(BF)

    lax.fori_loop(0, ch, joined_row, None)
    flat = (cd * ch * chans, 2 * width)
    grad = dot(ughi[...].reshape(flat), pool) + dot(uglo[...].reshape(flat), pool)
    ug[...] = grad.astype(BF).reshape(ug.shape)

    def fill_pooled(q, _):
        wide = ph[:, q].reshape((cd + 2) * chans, width).astype(F32)
        for c in range(3):
            ps[:, q, c] = shifted(wide, c).astype(BF).reshape(cd + 2, chans, width)

    landed_rows(pcopies, recvs, DIRS, False)
    lax.fori_loop(1, ch + 1, fill_pooled, None)
    def coarse_row(q):
        k = 9 * chans
        pre = conv_row(wc[...], [ps[p, q:q + 3].reshape(k, width) for p in range(cd + 2)], cd)
        for p in range(cd):
            t = pre[p]
            sig = 1.0 / (1.0 + jnp.exp(-t))
            a = (t * sig * coarse_mask).astype(BF)
            act[p, q] = a
            uh[1 + p, 1 + q] = dot(upt[...], a).astype(BF)
            back = dot(up[...], ug[p, q])
            gh[1 + p, 1 + q] = (back * (sig * (1.0 + t * (1.0 - sig)) * coarse_mask)).astype(BF)

    for q in range(1, ch - 1):
        coarse_row(q)
    landed_rows(pcopies, recvs, DIRS, True)
    for q in (0, ch + 1):
        fill_pooled(q, None)
    for q in (0, ch - 1):
        coarse_row(q)
    gcopies = exchange(gh, rim_src(1, cd, ch, 1), gh, rim_dst(1, cd, ch), gsend, grecv)
    begin(gcopies, sends)
    ucopies = exchange(uh, rim_src(1, cd, ch, 1), uh, rim_dst(1, cd, ch), usend, urecv)
    begin(ucopies, sends)

    group16 = lax.broadcasted_iota(jnp.int32, (1, width), 1) // 16
    group32 = lax.broadcasted_iota(jnp.int32, (1, width), 1) // 32

    def tap_sums(block, step, groups, gid):
        out = []
        for b in range(3):
            total = jnp.zeros((step, width), F32)
            for q in range(groups):
                total = jnp.where(gid == q, block[(q + b) * step:(q + b + 1) * step], total)
            size = width // 2
            while size >= width // groups:
                total = total + pltpu.roll(total, size, 1)
                size //= 2
            out.append(total)
        return out

    def put(ref, first, value):
        tiles = value.shape[0] // 16
        ref[first:first + tiles] = value.astype(BF).reshape(tiles, 16, width)

    def place(total, gid, first, block):
        for k in range(block.shape[0] // 16):
            total = jnp.where(gid == first + k, block[16 * k:16 * k + 16], total)
        return total

    for ref, used in ((gr0, 11), (gr1, 7)):
        if ref.shape[0] > used:
            ref[used:] = jnp.zeros((ref.shape[0] - used, 16, width), BF)
    blank = jnp.zeros((16, width), F32)
    step = 3 * chans
    taps = []
    masked = [jnp.where(own_coarse, gh[1 + p, 1:1 + ch].reshape(2 * chans * ch, width), 0)
              for p in range(cd)]
    for a in range(3):
        block = sum(dot_nt(ps[p + a].reshape((ch + 2) * step, width), masked[p]) for p in range(cd))
        taps += tap_sums(block, step, ch, group32)
    for half in range(2):
        total = jnp.zeros((step, width), F32)
        for g in range(4):
            total = jnp.where(group32 == g, taps[4 * half + g], total)
        put(gr0, 3 * half, total)
    side = place(blank, group32, 0, taps[8])
    up_total = jnp.zeros((2 * chans, width), F32)
    for p in range(cd):
        for q in range(ch):
            g = jnp.where(own_coarse, ug[p, q], 0)
            up_total = up_total + dot_nt(act[p, q], jnp.concatenate([g] * 8, axis=0))
    side = place(side, group16, 6, up_total)
    put(gr0, 9, side)

    def fill_skip(first, count, y):
        wide = skip[first:first + count, y].reshape(count * chans, 2 * width).astype(F32)
        for c in range(3):
            part = shifted(wide, c)[:, :width]
            js[first:first + count, y, c, 0:chans] = part.astype(BF).reshape(count, chans, width)

    lax.fori_loop(1, height + 1, lambda y, _: fill_skip(1, depth, y), None)
    landed(scopies, recvs)
    for y in (0, height + 1):
        fill_skip(0, depth + 2, y)

    def fill_sides(y, _):
        fill_skip(0, 1, y)
        fill_skip(depth + 1, 1, y)

    lax.fori_loop(1, height + 1, fill_sides, None)

    def fine_taps(source, step, grads):
        taps = []
        for a in range(3):
            block = sum(dot_nt(source(a + p), grads[p]) for p in range(depth))
            taps += tap_sums(block, step, height, group16)
        total = jnp.zeros((step, width), F32)
        for g in range(8):
            total = jnp.where(group16 == g, taps[g], total)
        return total, taps[8]

    def joined_taps(first):
        return fine_taps(
            lambda x: js[x, :, :, first:first + chans].reshape((height + 2) * 3 * chans, width), 3 * chans,
            [vc[p, :, chans:2 * chans].reshape(height * chans, width) for p in range(depth)])

    total, last = joined_taps(0)
    put(gr0, 6, total)
    put(gr0, 10, place(blank, group16, 0, last))
    early = ring(0, 0)

    def fill_coarse(y, _):
        wide = gh[:, y].reshape((cd + 2) * 2 * chans, width).astype(F32)
        for c in range(3):
            gs[:, y, c] = shifted(wide, c).astype(BF).reshape(cd + 2, 2 * chans, width)

    landed_rows(gcopies, recvs, DIRS, False)
    lax.fori_loop(1, ch + 1, fill_coarse, None)
    spread = (lax.broadcasted_iota(jnp.int32, (width, 2 * width), 1) // 2
              == lax.broadcasted_iota(jnp.int32, (width, 2 * width), 0)).astype(BF)

    def back_row(q, _):
        k = 18 * chans
        pg = conv_row(wcb[...], [gs[p, pl.ds(q, 3)].reshape(k, width) for p in range(cd + 2)], cd)
        for p in range(cd):
            v = pg[p] * 0.125
            hi = v.astype(BF)
            lo = (v - hi.astype(F32)).astype(BF)
            wide = dot(hi, spread) + dot(lo, spread)
            for e in range(2):
                for f in range(2):
                    g = (jg[2 * p + e, 2 * q + f] + wide) * slope[2 * p + e, 2 * q + f]
                    eh[1 + 2 * p + e, 1 + 2 * q + f] = g.astype(BF)

    lax.fori_loop(1, ch - 1, back_row, None)
    landed_rows(gcopies, recvs, DIRS, True)
    for y in (0, ch + 1):
        fill_coarse(y, None)
    for q in (0, ch - 1):
        back_row(q, None)
    ecopies = exchange(eh, rim_src(1, depth, height, 1), eh, rim_dst(1, depth, height), esend, erecv)
    begin(ecopies, sends)

    landed(ucopies, recvs)
    low = lax.broadcasted_iota(jnp.int32, (width, width), 0)
    lane = lax.broadcasted_iota(jnp.int32, (width, width), 1)
    for c in range(3):
        source = lax.rem(lane + (c - 1) + 2 * width, 2 * width) // 2
        pick = (low == source).astype(BF)
        wide = dot(uh[...].reshape((cd + 2) * (ch + 2) * chans, width), pick)
        wide = wide.astype(BF).reshape(cd + 2, ch + 2, chans, width)
        for x in range(depth + 2):
            for y in range(height + 2):
                js[x, y, c, chans:2 * chans] = wide[(x + 1) // 2, (y + 1) // 2]

    total, last = joined_taps(chans)
    put(gr1, 3, total)
    side = place(blank, group16, 3, last)
    total, last = fine_taps(
        lambda x: vs[x, :, :, :, 0:width].reshape((height + 2) * 3 * chans, width), 3 * chans,
        [eh[1 + p, 1:1 + height, :, 0:width].reshape(height * chans, width) for p in range(depth)])
    put(gr1, 0, total)
    put(gr1, 6, place(side, group16, 0, last))

    late = ring(1, 0)
    early = advance(0, early, 0)

    order = zero_one((height * chans, height * chans),
                     lambda r, l: (r // height == l % chans) & (r % height == l // chans)).astype(BF)

    def channels_first(which, ref):
        for p in range(depth):
            moved = dot(order, turn[which, p].reshape(height * chans, width))
            ref[:, p] = moved.reshape(chans, height, width).astype(BF)

    def dec_row(q, _):
        k = 18 * chans
        out = conv_row(wd[...], [js[p, pl.ds(q, 3)].reshape(k, width) for p in range(depth + 2)], depth)
        for p in range(depth):
            turn[0, p, q] = out[p].astype(BF)

    lax.fori_loop(0, height // 2, dec_row, None)

    late = advance(1, late, 0)
    early = advance(0, early, 1)
    lax.fori_loop(height // 2, height, dec_row, None)
    channels_first(0, dec_out)
    landed(ecopies, recvs)

    def fill_enc(y, _):
        wide = eh[:, y].reshape((depth + 2) * chans, 2 * width).astype(F32)
        for c in range(3):
            part = shifted(wide, c)[:, :width]
            es[:, y, c] = part.astype(BF).reshape(depth + 2, chans, width)

    lax.fori_loop(0, height + 2, fill_enc, None)

    def vol_row(q, _):
        k = 9 * chans
        out = conv_row(web[...], [es[p, pl.ds(q, 3)].reshape(k, width) for p in range(depth + 2)], depth)
        for p in range(depth):
            turn[1, p, q] = out[p].astype(BF)

    late = advance(1, late, 1)
    early = advance(0, early, 2)
    lax.fori_loop(0, height // 2, vol_row, None)
    late = advance(1, late, 2)
    lax.fori_loop(height // 2, height, vol_row, None)
    channels_first(1, vg_out)
    for c in early + late:
        c.wait_recv()
    sum_out[0:gr0.shape[0]] = ar0[3, 0:groups[0][0]].reshape(gr0.shape)
    sum_out[gr0.shape[0]:] = ar1[3, 0:groups[0][0]].reshape(gr1.shape)

    left(zcopies, esends)
    for copies in (vcopies, pcopies, gcopies, ucopies, scopies, ecopies):
        left(copies, sends)
    for c in everything:
        c.wait_send()


def per_device(sizes, volume, enc_weight, coarse_weight, up_weight, dec_weight, cotangent):
    nx, ny, nz = sizes
    chans, d, h, w = volume.shape
    cd, ch = d // 2, h // 2
    owners = min(2, nx) * (ny // 2 if ny > 4 else ny)
    pers = (-(-11 // owners), -(-7 // owners))
    pair = jnp.transpose(jnp.concatenate([volume, cotangent], axis=0), (1, 2, 0, 3))
    operands = (
        pair, jnp.transpose(enc_weight, (1, 2, 0)), coarse_weight, up_weight.T, jnp.transpose(dec_weight, (0, 2, 1)))
    c2 = 2 * chans
    widest = max(owners, nx * ny // owners, nz) - 1
    scratch = [
        ((16, 16, 27), BF),
        ((27, 16, 32), BF),
        ((16, 32), BF),
        ((27, 16, 32), BF),
        ((48, 144), BF),
        ((48, 288), BF),
        ((96, 144), BF),
        ((96, 144), BF),
        ((48, 288), BF),
        ((48, 144), BF),
        ((32, 16), BF),
        ((2, d, h, chans, w), BF),
        ((d + 2, h + 2, c2, w), BF),
        ((2, d, chans, w), BF),
        ((2, 3, d + 2, chans, w), BF),
        ((d + 2, h + 2, 3, chans, 2 * w), BF),
        ((d + 2, h + 2, 3, chans, 2 * w), BF),
        ((d + 2, h + 2, chans, 2 * w), BF),
        ((d, h, chans, 2 * w), F32),
        ((d, h, chans, 2 * w), F32),
        ((cd, ch, chans, 2 * w), BF),
        ((cd, ch, chans, 2 * w), BF),
        ((cd, ch, chans, w), BF),
        ((cd + 2, ch + 2, chans, w), BF),
        ((cd + 2, ch + 2, 3, chans, w), BF),
        ((cd, ch, c2, w), BF),
        ((cd + 2, ch + 2, chans, w), BF),
        ((cd + 2, ch + 2, c2, w), BF),
        ((cd + 2, ch + 2, 3, c2, w), BF),
        ((d + 2, h + 2, 3, c2, w), BF),
        ((d + 2, h + 2, chans, 2 * w), BF),
        ((d + 2, h + 2, 3, chans, w), BF),
        ((owners * pers[0], 16, w), BF),
        ((owners * pers[1], 16, w), BF),
        ((4, widest + 1, pers[0], 16, w), BF),
        ((4, widest + 1, pers[1], 16, w), BF),
    ]
    dma = pltpu.SemaphoreType.DMA
    sems = [dma((8,))] * 2 + [dma((18,))] * 2 + [dma((8,))] * 10 + [dma((4, max(widest, 1)))] * 4 + [dma((4,))]
    hbm = pl.BlockSpec(memory_space=pl.ANY)
    vmem = pl.BlockSpec(memory_space=pltpu.VMEM)
    dec, vg, total = pl.pallas_call(
        functools.partial(kernel, sizes),
        out_shape=(
            jax.ShapeDtypeStruct((chans, d, h, w), BF),
            jax.ShapeDtypeStruct((chans, d, h, w), BF),
            jax.ShapeDtypeStruct((owners * sum(pers), 16, w), BF)),
        in_specs=[vmem] + [hbm] * 4,
        out_specs=(vmem,) * 3,
        scratch_shapes=[pltpu.VMEM(s, t) for s, t in scratch] + sems,
        compiler_params=pltpu.CompilerParams(
            collective_id=0, has_side_effects=True, vmem_limit_bytes=48 * 1024 * 1024),
    )(*operands)
    grads = ((16, 16, 27), (27, 16, 32), (16, 32), (27, 16, 32))
    dec, vg, enc, coarse, upg, decg = pl.pallas_call(
        functools.partial(finish, owners * pers[0]),
        out_shape=tuple(jax.ShapeDtypeStruct(x.shape, BF) for x in (dec, vg))
        + tuple(jax.ShapeDtypeStruct(x, F32) for x in grads),
        in_specs=[vmem] * 3,
        out_specs=(hbm,) * 6,
        scratch_shapes=[pltpu.VMEM(x, F32) for x in grads] + [dma((6,))],
        compiler_params=pltpu.CompilerParams(vmem_limit_bytes=8 * 1024 * 1024),
    )(dec, vg, total)
    return (dec, vg, jnp.transpose(enc, (2, 0, 1)), coarse, upg.T, jnp.transpose(decg, (0, 2, 1)))


def solution(mesh):
    sizes = tuple(mesh.shape[a] for a in AXES)
    spec = P(None, "gx", "gy", "gz")
    return jax.shard_map(
        functools.partial(per_device, sizes),
        mesh=mesh,
        in_specs=(spec, P(), P(), P(), P(), spec),
        out_specs=(spec, spec, P(), P(), P(), P()),
        check_vma=False,
    )
```

```python
import functools

import jax
import jax.numpy as jnp
from jax import lax
from jax.experimental import pallas as pl
from jax.experimental.pallas import tpu as pltpu
from jax.sharding import PartitionSpec as P

AXES = ("gx", "gy", "gz")
BF = jnp.bfloat16
F32 = jnp.float32
MESH = pl.DeviceIdType.MESH
DIRS = tuple((dx, dy) for dy in (-1, 1, 0) for dx in (-1, 1, 0) if (dx, dy) != (0, 0))


def dot(a, b):
    return jnp.dot(a, b, preferred_element_type=F32)


def dot_nt(a, b):
    return lax.dot_general(a, b, (((1,), (1,)), ((), ())), preferred_element_type=F32)


def dot_tn(a, b):
    return lax.dot_general(a, b, (((0,), (0,)), ((), ())), preferred_element_type=F32)


def zero_one(shape, rule):
    return rule(lax.broadcasted_iota(jnp.int32, shape, 0), lax.broadcasted_iota(jnp.int32, shape, 1))


def arrange_weights(enc, coarse, upt, dec, we, wd, wdb, wc, wcb, web, up):
    flat = enc[...].reshape(256, 27)
    same_in = zero_one((256, 144), lambda r, l: r // 16 == l % 16)
    same_out = zero_one((256, 144), lambda r, l: r % 16 == l % 16)
    fold_in = zero_one((16, 256), lambda r, l: r == l % 16).astype(BF)
    fold_out = zero_one((16, 256), lambda r, l: r == l // 16).astype(BF)
    for a in range(3):
        ahead = dot(flat, zero_one((27, 144), lambda r, l: r == 9 * a + l // 16).astype(BF))
        we[16 * a:16 * a + 16] = dot(fold_in, jnp.where(same_in, ahead, 0.0).astype(BF)).astype(BF)
        back = dot(flat, zero_one((27, 144), lambda r, l: r == 26 - 9 * a - l // 16).astype(BF))
        web[16 * a:16 * a + 16] = dot(fold_out, jnp.where(same_out, back, 0.0).astype(BF)).astype(BF)
    totals = [0.0] * 4
    for t in range(9):
        wide = zero_one((32, 288), lambda r, l: l == 32 * t + r).astype(BF)
        slim = zero_one((16, 144), lambda r, l: l == 16 * t + r).astype(BF)
        ahead, back = (t, 9 + t, 18 + t), (26 - t, 17 - t, 8 - t)
        totals[0] += dot(jnp.concatenate([dec[k] for k in ahead], axis=0), wide)
        totals[1] += dot_tn(jnp.concatenate([dec[k] for k in back], axis=1), slim)
        totals[2] += dot_tn(jnp.concatenate([coarse[k] for k in ahead], axis=1), slim)
        totals[3] += dot(jnp.concatenate([coarse[k] for k in back], axis=0), wide)
    for ref, total in zip((wd, wdb, wc, wcb), totals):
        ref[...] = total.astype(BF)
    up[...] = dot_tn(upt[...], zero_one((16, 16), lambda r, l: r == l).astype(BF)).astype(BF)


def finish(split, dec, vg, total, dec_out, vg_out, enc_out, coarse_out, up_out, decg_out,
           enc, coarse, up, decg, sems):
    copies = [pltpu.make_async_copy(a, b, sems.at[k]) for k, (a, b) in enumerate(
        ((dec, dec_out), (vg, vg_out), (enc, enc_out), (coarse, coarse_out), (up, up_out), (decg, decg_out)))]
    copies[0].start()
    copies[1].start()

    def tile(which, k):
        return total[which * split + k]

    eye = zero_one((128, 128), lambda r, l: r == l).astype(BF)
    for c in range(3):
        block = jnp.concatenate([tile(0, 6 + c), tile(1, 3 + c)], axis=0)
        turned = dot_nt(eye, block).reshape(8, 16, 32)
        for g in range(8):
            decg[3 * g + c] = turned[g]
        skip_last = dot_nt(zero_one((16, 128), lambda r, l: l == 16 * c + r).astype(BF), tile(0, 10))
        upper_last = dot_nt(zero_one((16, 128), lambda r, l: l == 48 + 16 * c + r).astype(BF), tile(1, 6))
        decg[24 + c] = jnp.concatenate([skip_last, upper_last], axis=1)
    copies[5].start()
    for c in range(3):
        for half in range(2):
            block = tile(0, 3 * half + c)
            for g in range(4):
                pick = zero_one((128, 32), lambda r, l: r == 32 * g + l).astype(BF)
                coarse[3 * (4 * half + g) + c] = dot(block, pick)
        pick = zero_one((128, 32), lambda r, l: r == 32 * c + l).astype(BF)
        coarse[24 + c] = dot(tile(0, 9), pick)
    copies[3].start()
    up[...] = jnp.concatenate(
        [dot_nt(zero_one((16, 128), lambda r, l: l == 96 + 16 * k + r).astype(BF), tile(0, 9)) for k in range(2)], axis=1)
    copies[4].start()
    grow = zero_one((256, 16), lambda r, l: l == r // 16).astype(BF)
    same = zero_one((256, 128), lambda r, l: r % 16 == l % 16)
    flat = jnp.zeros((256, 27), F32)
    for c in range(3):
        wide = jnp.where(same, dot(grow, tile(1, c)), 0.0).astype(BF)
        flat = flat + dot(wide, zero_one((128, 27), lambda r, l: l == 3 * (r // 16) + c).astype(BF))
        wide = jnp.where(same, dot(grow, tile(1, 6)), 0.0).astype(BF)
        flat = flat + dot(wide, zero_one((128, 27), lambda r, l: (r // 16 == c) & (l == 24 + c)).astype(BF))
    enc[...] = flat.reshape(16, 16, 27)
    copies[2].start()
    for c in copies:
        c.wait()


def all_of(*conds):
    total = None
    for c in conds:
        if c is not None:
            total = c if total is None else jnp.logical_and(total, c)
    return total


def span(step, size, halo):
    if step == 0:
        return (0, size), (halo, size)
    if step > 0:
        return (size - halo, halo), (0, halo)
    return (0, halo), (halo + size, halo)


def kernel(sizes, vc, enc_in, coarse_in, upt_in, dec_in, dec_out, vg_out, sum_out,
           enc_w, coarse_w, upt, dec_w, we, wd, wdb, wc, wcb, web, up, turn,
           vct, pk, er, vs, cs, skip, slope, jg, ughi, uglo, ug, ph, ps, act, uh, gh, gs, js, eh, es,
           gr0, gr1, ar0, ar1,
           vsend, vrecv, zsend, zrecv, psend, precv, gsend, grecv, usend, urecv, ssend, srecv, esend, erecv,
           asend0, arecv0, asend1, arecv1, wsem):
    nx, ny, nz = sizes
    ix, iy, iz = (lax.axis_index(a) for a in AXES)
    depth, height, _, width = vc.shape
    chans = vc.shape[2] // 2
    cd, ch = depth // 2, height // 2

    def exists(step, index, count):
        return None if step == 0 else (index + step < count if step > 0 else index + step >= 0)

    def at(dx, dy, dz=0):
        return (ix + dx, iy + dy, iz + dz)

    def guarded(cond, f):
        if cond is None:
            f()
        else:
            pl.when(cond)(f)

    sends = [all_of(exists(dx, ix, nx), exists(dy, iy, ny)) for dx, dy in DIRS]
    recvs = [all_of(exists(-dx, ix, nx), exists(-dy, iy, ny)) for dx, dy in DIRS]
    ends = tuple((dx, dy, s) for dy in (-1, 1, 0) for dx in (-1, 1, 0) for s in (-1, 1))
    esends = [all_of(exists(dx, ix, nx), exists(dy, iy, ny), exists(dz, iz, nz)) for dx, dy, dz in ends]
    erecvs = [all_of(exists(-dx, ix, nx), exists(-dy, iy, ny), exists(-dz, iz, nz)) for dx, dy, dz in ends]

    cores = min(2, nx)
    lows, across = nx // cores, ny // 2 if ny > 4 else ny
    highs = ny // across
    core, y_low, x_at, y_high = lax.rem(ix, cores), ix // cores, lax.rem(iy, across), iy // across
    groups = (
        (cores * across, core * across + x_at,
         lambda j: (y_low * cores + j // across, y_high * across + lax.rem(j, across), iz)),
        (highs * lows, y_high * lows + y_low,
         lambda j: (lax.rem(j, lows) * cores + core, (j // lows) * across + x_at, iz)),
        (nz, iz, lambda j: (ix, iy, j)),
    )

    barrier = pltpu.get_barrier_semaphore()

    def greet(device):
        pl.semaphore_signal(barrier, inc=1, device_id=device, device_id_type=MESH)

    for dx, dy, dz in list(ends) + [d + (0,) for d in DIRS]:
        if dx != 0 or dy != 0:
            guarded(all_of(exists(dx, ix, nx), exists(dy, iy, ny), exists(dz, iz, nz)),
                    lambda dx=dx, dy=dy, dz=dz: greet(at(dx, dy, dz)))

    for count, me, member in groups:
        for k in range(1, count):
            greet(member(lax.rem(me + k, count)))
    def both(index, count):
        return (jnp.where(index > 0, 1, 0) + jnp.where(index < count - 1, 1, 0)).astype(jnp.int32)

    loads = [pltpu.make_async_copy(a, b, wsem.at[k]) for k, (a, b) in enumerate(
        ((enc_in, enc_w), (coarse_in, coarse_w), (upt_in, upt), (dec_in, dec_w)))]
    for c in loads:
        c.start()

    row = lax.broadcasted_iota(jnp.int32, (width, 2 * width), 0)
    lane = lax.broadcasted_iota(jnp.int32, (width, 2 * width), 1)
    total = jnp.zeros((depth * chans, 2 * width), F32)
    for n in range(2):
        for y in range(height):
            base = 64 * n + 8 * y
            pick = ((lane == base + row) & (row < 8)) | ((lane == width + base + row - 120) & (row >= 120))
            total = total + dot(vc[:, y, n * chans:(n + 1) * chans].reshape(depth * chans, width), pick.astype(BF))
    for side in range(2):
        pk[side] = total[:, side * width:(side + 1) * width].astype(BF).reshape(depth, chans, width)
    bx, by, bz = both(ix, nx), both(iy, ny), both(iz, nz)
    near = bx + by + bx * by
    pl.semaphore_wait(barrier, sum(count - 1 for count, _, _ in groups) + near + near * bz)

    def exchange(src, src_at, dst, dst_at, send_sem, recv_sem):
        copies = []
        for d, (dx, dy) in enumerate(DIRS):
            copies.append(pltpu.make_async_remote_copy(
                src_ref=src.at[src_at(dx, dy)], dst_ref=dst.at[dst_at(dx, dy)],
                send_sem=send_sem.at[d], recv_sem=recv_sem.at[d],
                device_id=at(dx, dy), device_id_type=MESH))
        return copies

    def begin(copies, conds):
        for c, s in zip(copies, conds):
            guarded(s, c.start)

    def landed(copies, conds):
        for c, r in zip(copies, conds):
            guarded(r, c.wait_recv)

    def landed_rows(copies, conds, dirs, rim):
        part = [i for i, d in enumerate(dirs) if (d[1] != 0) == rim]
        landed([copies[i] for i in part], [conds[i] for i in part])

    def left(copies, conds):
        for c, s in zip(copies, conds):
            guarded(s, c.wait_send)

    def rim_src(halo, d0, h0, off):
        def f(dx, dy):
            (a, n), _ = span(dx, d0, halo)
            (b, m), _ = span(dy, h0, halo)
            return (pl.ds(a + off, n), pl.ds(b + off, m))
        return f

    def rim_dst(halo, d0, h0):
        def f(dx, dy):
            _, (a, n) = span(dx, d0, halo)
            _, (b, m) = span(dy, h0, halo)
            return (pl.ds(a, n), pl.ds(b, m))
        return f

    vcopies = exchange(vc, rim_src(1, depth, height, 0), vct, rim_dst(1, depth, height), vsend, vrecv)
    begin(vcopies, sends)

    zcopies = []
    for d, (dx, dy, dz) in enumerate(ends):
        (a, n), (b, m) = span(dx, depth, 1)
        side = 1 if dz > 0 else 0
        zcopies.append(pltpu.make_async_remote_copy(
            src_ref=pk.at[side, pl.ds(a, n)], dst_ref=er.at[side, 1 - dy, pl.ds(b, m)],
            send_sem=zsend.at[d], recv_sem=zrecv.at[d],
            device_id=at(dx, dy, dz), device_id_type=MESH))
    begin(zcopies, esends)
    vct[1:1 + depth, 1:1 + height] = vc[...]

    def clear(ref, d0, h0):
        for d, (dx, dy) in enumerate(DIRS):
            _, (a, n) = span(dx, d0, 1)
            _, (b, m) = span(dy, h0, 1)

            def zero(a=a, n=n, b=b, m=m):
                ref[a:a + n, b:b + m] = jnp.zeros((n, m) + ref.shape[2:], ref.dtype)

            if recvs[d] is not None:
                pl.when(jnp.logical_not(recvs[d]))(zero)

    for ref in (vct, skip, eh):
        clear(ref, depth, height)
    for ref in (ph, uh, gh):
        clear(ref, cd, ch)
    for d, (dx, dy, dz) in enumerate(ends):
        _, (b, m) = span(dx, depth, 1)

        def zero(side=1 if dz > 0 else 0, dyi=1 - dy, b=b, m=m):
            er[side, dyi, b:b + m] = jnp.zeros((m, chans, width), BF)

        pl.when(jnp.logical_not(erecvs[d]))(zero)

    for c in loads:
        c.wait()
    arrange_weights(enc_w, coarse_w, upt, dec_w, we, wd, wdb, wc, wcb, web, up)

    def shifted(wide, c):
        if c == 1:
            return wide
        return pltpu.roll(wide, 1 if c == 0 else wide.shape[1] - 1, 1)

    def fill_inputs(y, _):
        dyi, base = (y + 7) // 8, 8 * lax.rem(y + 7, 8)
        flat = ((depth + 2) * chans, width)
        kind, spot = lane // width, lax.rem(lane, width)
        source = base + 64 * kind + spot
        lo = (row == source - 120) & (spot >= 120)
        hi = (row == source) & (spot < 8)
        got = dot(er[1, dyi].reshape(flat), lo.astype(BF)) + dot(er[0, dyi].reshape(flat), hi.astype(BF))
        for n, ref in enumerate((vs, cs)):
            own = vct[:, y, n * chans:(n + 1) * chans].reshape(flat).astype(F32)
            wide = jnp.concatenate([own, got[:, n * width:(n + 1) * width]], axis=1)
            for c in range(3):
                ref[:, y, c] = shifted(wide, c).astype(BF).reshape(depth + 2, chans, 2 * width)


    sets = ((gr0, ar0, asend0, arecv0), (gr1, ar1, asend1, arecv1))

    def ring(which, phase):
        gr, ar, asend, arecv = sets[which]
        count, me, member = groups[phase % 3]
        per = gr.shape[0] // groups[0][0]
        out, got = [], []
        for k in sorted(range(1, count), key=lambda k: abs(2 * k - count)):
            to = lax.rem(me + k, count)
            frm = lax.rem(me - k + count, count)
            src = gr.at[pl.ds(to * per, per)] if phase == 0 else ar.at[phase, me]

            def copy(slot):
                return pltpu.make_async_remote_copy(
                    src_ref=src, dst_ref=ar.at[phase, slot], send_sem=asend.at[phase, k - 1],
                    recv_sem=arecv.at[phase, k - 1], device_id=member(to), device_id_type=MESH)

            out.append(copy(me))
            got.append(copy(frm))
        for c in out:
            c.start()
        if phase == 0:
            ar[0, me] = gr[pl.ds(me * per, per)]
        everything.extend(out)
        return got

    everything = []

    def advance(which, copies, phase):
        ar = sets[which][1]
        for c in copies:
            c.wait_recv()
        total = ar[phase, 0].astype(F32)
        for k in range(1, groups[phase][0]):
            total = total + ar[phase, k].astype(F32)
        ar[phase + 1, groups[(phase + 1) % 3][1]] = total.astype(BF)
        return ring(which, phase + 1)

    fine = lax.broadcasted_iota(jnp.int32, (1, 2 * width), 1)
    coarse = lax.broadcasted_iota(jnp.int32, (1, width), 1)
    low_ok = jnp.where(iz > 0, 1.0, 0.0).astype(F32)
    high_ok = jnp.where(iz < nz - 1, 1.0, 0.0).astype(F32)
    fine_mask = jnp.where(fine < width, 1.0, jnp.where(fine < 3 * width // 2, high_ok, low_ok))
    coarse_mask = jnp.where(coarse < width // 2, 1.0, jnp.where(coarse < 3 * width // 4, high_ok, low_ok))
    own_coarse = coarse < width // 2

    def conv_row(weight, planes, outs):
        m = weight.shape[0] // 3
        ys = [dot(weight, x) for x in planes]
        return [ys[p][:m] + ys[p + 1][m:2 * m] + ys[p + 2][2 * m:] for p in range(outs)]

    def enc_row(q, _):
        k = 9 * chans
        pre = conv_row(we[...], [vs[p, pl.ds(q, 3)].reshape(k, 2 * width) for p in range(depth + 2)], depth)
        for p in range(depth):
            t = pre[p]
            sig = 1.0 / (1.0 + jnp.exp(-t))
            skip[1 + p, 1 + q] = (t * sig * fine_mask).astype(BF)
            slope[p, q] = sig * (1.0 + t * (1.0 - sig)) * fine_mask

    landed_rows(zcopies, erecvs, ends, False)
    landed_rows(vcopies, recvs, DIRS, False)
    lax.fori_loop(1, height + 1, fill_inputs, None)
    lax.fori_loop(1, height - 1, enc_row, None)
    landed_rows(zcopies, erecvs, ends, True)
    landed_rows(vcopies, recvs, DIRS, True)
    for y in (0, height + 1):
        fill_inputs(y, None)
    for q in (0, height - 1):
        enc_row(q, None)

    pool = (lax.broadcasted_iota(jnp.int32, (2 * width, width), 0) // 2
            == lax.broadcasted_iota(jnp.int32, (2 * width, width), 1)).astype(BF)

    for q in range(ch):
        rows_in = skip[1:1 + depth, 1 + 2 * q:3 + 2 * q].reshape(depth * 2 * chans, 2 * width)
        half = dot(rows_in, pool).reshape(cd, 4, chans, width)
        ph[1:1 + cd, 1 + q] = ((half[:, 0] + half[:, 1] + half[:, 2] + half[:, 3]) * 0.125).astype(BF)
    pcopies = exchange(ph, rim_src(1, cd, ch, 1), ph, rim_dst(1, cd, ch), psend, precv)
    begin(pcopies, sends)
    scopies = exchange(skip, rim_src(1, depth, height, 1), skip, rim_dst(1, depth, height), ssend, srecv)
    begin(scopies, sends)

    def joined_row(q, _):
        k = 9 * chans
        sums = [jnp.zeros((chans, 2 * width), F32) for _ in range(cd)]
        for e in range(2):
            r = 2 * q + e
            out = conv_row(wdb[...], [cs[p, pl.ds(r, 3)].reshape(k, 2 * width) for p in range(depth + 2)], depth)
            for p in range(depth):
                jg[p, r] = out[p][:chans]
                sums[p // 2] = sums[p // 2] + out[p][chans:]
        for p in range(cd):
            hi = sums[p].astype(BF)
            ughi[p, q] = hi
            uglo[p, q] = (sums[p] - hi.astype(F32)).astype(BF)

    lax.fori_loop(0, ch, joined_row, None)
    flat = (cd * ch * chans, 2 * width)
    grad = dot(ughi[...].reshape(flat), pool) + dot(uglo[...].reshape(flat), pool)
    ug[...] = grad.astype(BF).reshape(ug.shape)

    def fill_pooled(q, _):
        wide = ph[:, q].reshape((cd + 2) * chans, width).astype(F32)
        for c in range(3):
            ps[:, q, c] = shifted(wide, c).astype(BF).reshape(cd + 2, chans, width)

    landed_rows(pcopies, recvs, DIRS, False)
    lax.fori_loop(1, ch + 1, fill_pooled, None)
    def coarse_row(q):
        k = 9 * chans
        pre = conv_row(wc[...], [ps[p, q:q + 3].reshape(k, width) for p in range(cd + 2)], cd)
        for p in range(cd):
            t = pre[p]
            sig = 1.0 / (1.0 + jnp.exp(-t))
            a = (t * sig * coarse_mask).astype(BF)
            act[p, q] = a
            uh[1 + p, 1 + q] = dot(upt[...], a).astype(BF)
            back = dot(up[...], ug[p, q])
            gh[1 + p, 1 + q] = (back * (sig * (1.0 + t * (1.0 - sig)) * coarse_mask)).astype(BF)

    for q in range(1, ch - 1):
        coarse_row(q)
    landed_rows(pcopies, recvs, DIRS, True)
    for q in (0, ch + 1):
        fill_pooled(q, None)
    for q in (0, ch - 1):
        coarse_row(q)
    gcopies = exchange(gh, rim_src(1, cd, ch, 1), gh, rim_dst(1, cd, ch), gsend, grecv)
    begin(gcopies, sends)
    ucopies = exchange(uh, rim_src(1, cd, ch, 1), uh, rim_dst(1, cd, ch), usend, urecv)
    begin(ucopies, sends)

    group16 = lax.broadcasted_iota(jnp.int32, (1, width), 1) // 16
    group32 = lax.broadcasted_iota(jnp.int32, (1, width), 1) // 32

    def tap_sums(block, step, groups, gid):
        out = []
        for b in range(3):
            total = jnp.zeros((step, width), F32)
            for q in range(groups):
                total = jnp.where(gid == q, block[(q + b) * step:(q + b + 1) * step], total)
            size = width // 2
            while size >= width // groups:
                total = total + pltpu.roll(total, size, 1)
                size //= 2
            out.append(total)
        return out

    def put(ref, first, value):
        tiles = value.shape[0] // 16
        ref[first:first + tiles] = value.astype(BF).reshape(tiles, 16, width)

    def place(total, gid, first, block):
        for k in range(block.shape[0] // 16):
            total = jnp.where(gid == first + k, block[16 * k:16 * k + 16], total)
        return total

    for ref, used in ((gr0, 11), (gr1, 7)):
        if ref.shape[0] > used:
            ref[used:] = jnp.zeros((ref.shape[0] - used, 16, width), BF)
    blank = jnp.zeros((16, width), F32)
    step = 3 * chans
    taps = []
    masked = [jnp.where(own_coarse, gh[1 + p, 1:1 + ch].reshape(2 * chans * ch, width), 0)
              for p in range(cd)]
    for a in range(3):
        block = sum(dot_nt(ps[p + a].reshape((ch + 2) * step, width), masked[p]) for p in range(cd))
        taps += tap_sums(block, step, ch, group32)
    for half in range(2):
        total = jnp.zeros((step, width), F32)
        for g in range(4):
            total = jnp.where(group32 == g, taps[4 * half + g], total)
        put(gr0, 3 * half, total)
    side = place(blank, group32, 0, taps[8])
    up_total = jnp.zeros((2 * chans, width), F32)
    for p in range(cd):
        for q in range(ch):
            g = jnp.where(own_coarse, ug[p, q], 0)
            up_total = up_total + dot_nt(act[p, q], jnp.concatenate([g] * 8, axis=0))
    side = place(side, group16, 6, up_total)
    put(gr0, 9, side)

    def fill_skip(first, count, y):
        wide = skip[first:first + count, y].reshape(count * chans, 2 * width).astype(F32)
        for c in range(3):
            part = shifted(wide, c)[:, :width]
            js[first:first + count, y, c, 0:chans] = part.astype(BF).reshape(count, chans, width)

    lax.fori_loop(1, height + 1, lambda y, _: fill_skip(1, depth, y), None)
    landed(scopies, recvs)
    for y in (0, height + 1):
        fill_skip(0, depth + 2, y)

    def fill_sides(y, _):
        fill_skip(0, 1, y)
        fill_skip(depth + 1, 1, y)

    lax.fori_loop(1, height + 1, fill_sides, None)

    def fine_taps(source, step, grads):
        taps = []
        for a in range(3):
            block = sum(dot_nt(source(a + p), grads[p]) for p in range(depth))
            taps += tap_sums(block, step, height, group16)
        total = jnp.zeros((step, width), F32)
        for g in range(8):
            total = jnp.where(group16 == g, taps[g], total)
        return total, taps[8]

    def joined_taps(first):
        return fine_taps(
            lambda x: js[x, :, :, first:first + chans].reshape((height + 2) * 3 * chans, width), 3 * chans,
            [vc[p, :, chans:2 * chans].reshape(height * chans, width) for p in range(depth)])

    total, last = joined_taps(0)
    put(gr0, 6, total)
    put(gr0, 10, place(blank, group16, 0, last))
    early = ring(0, 0)

    def fill_coarse(y, _):
        wide = gh[:, y].reshape((cd + 2) * 2 * chans, width).astype(F32)
        for c in range(3):
            gs[:, y, c] = shifted(wide, c).astype(BF).reshape(cd + 2, 2 * chans, width)

    landed_rows(gcopies, recvs, DIRS, False)
    lax.fori_loop(1, ch + 1, fill_coarse, None)
    spread = (lax.broadcasted_iota(jnp.int32, (width, 2 * width), 1) // 2
              == lax.broadcasted_iota(jnp.int32, (width, 2 * width), 0)).astype(BF)

    def back_row(q, _):
        k = 18 * chans
        pg = conv_row(wcb[...], [gs[p, pl.ds(q, 3)].reshape(k, width) for p in range(cd + 2)], cd)
        for p in range(cd):
            v = pg[p] * 0.125
            hi = v.astype(BF)
            lo = (v - hi.astype(F32)).astype(BF)
            wide = dot(hi, spread) + dot(lo, spread)
            for e in range(2):
                for f in range(2):
                    g = (jg[2 * p + e, 2 * q + f] + wide) * slope[2 * p + e, 2 * q + f]
                    eh[1 + 2 * p + e, 1 + 2 * q + f] = g.astype(BF)

    lax.fori_loop(1, ch - 1, back_row, None)
    landed_rows(gcopies, recvs, DIRS, True)
    for y in (0, ch + 1):
        fill_coarse(y, None)
    for q in (0, ch - 1):
        back_row(q, None)
    ecopies = exchange(eh, rim_src(1, depth, height, 1), eh, rim_dst(1, depth, height), esend, erecv)

    landed(ucopies, recvs)
    low = lax.broadcasted_iota(jnp.int32, (width, width), 0)
    lane = lax.broadcasted_iota(jnp.int32, (width, width), 1)
    for c in range(3):
        source = lax.rem(lane + (c - 1) + 2 * width, 2 * width) // 2
        pick = (low == source).astype(BF)
        wide = dot(uh[...].reshape((cd + 2) * (ch + 2) * chans, width), pick)
        wide = wide.astype(BF).reshape(cd + 2, ch + 2, chans, width)
        for x in range(depth + 2):
            for y in range(height + 2):
                js[x, y, c, chans:2 * chans] = wide[(x + 1) // 2, (y + 1) // 2]

    total, last = joined_taps(chans)
    put(gr1, 3, total)
    side = place(blank, group16, 3, last)
    total, last = fine_taps(
        lambda x: vs[x, :, :, :, 0:width].reshape((height + 2) * 3 * chans, width), 3 * chans,
        [eh[1 + p, 1:1 + height, :, 0:width].reshape(height * chans, width) for p in range(depth)])
    put(gr1, 0, total)
    put(gr1, 6, place(side, group16, 0, last))

    late = ring(1, 0)
    begin(ecopies, sends)
    early = advance(0, early, 0)

    order = zero_one((height * chans, height * chans),
                     lambda r, l: (r // height == l % chans) & (r % height == l // chans)).astype(BF)

    def channels_first(which, ref):
        for p in range(depth):
            moved = dot(order, turn[which, p].reshape(height * chans, width))
            ref[:, p] = moved.reshape(chans, height, width).astype(BF)

    def dec_row(q, _):
        k = 18 * chans
        out = conv_row(wd[...], [js[p, pl.ds(q, 3)].reshape(k, width) for p in range(depth + 2)], depth)
        for p in range(depth):
            turn[0, p, q] = out[p].astype(BF)

    lax.fori_loop(0, height // 2, dec_row, None)

    late = advance(1, late, 0)
    early = advance(0, early, 1)
    lax.fori_loop(height // 2, height, dec_row, None)
    channels_first(0, dec_out)
    landed(ecopies, recvs)

    def fill_enc(y, _):
        wide = eh[:, y].reshape((depth + 2) * chans, 2 * width).astype(F32)
        for c in range(3):
            part = shifted(wide, c)[:, :width]
            es[:, y, c] = part.astype(BF).reshape(depth + 2, chans, width)

    lax.fori_loop(0, height + 2, fill_enc, None)

    def vol_row(q, _):
        k = 9 * chans
        out = conv_row(web[...], [es[p, pl.ds(q, 3)].reshape(k, width) for p in range(depth + 2)], depth)
        for p in range(depth):
            turn[1, p, q] = out[p].astype(BF)

    late = advance(1, late, 1)
    early = advance(0, early, 2)
    lax.fori_loop(0, height // 2, vol_row, None)
    late = advance(1, late, 2)
    lax.fori_loop(height // 2, height, vol_row, None)
    channels_first(1, vg_out)
    for c in early + late:
        c.wait_recv()
    sum_out[0:gr0.shape[0]] = ar0[3, 0:groups[0][0]].reshape(gr0.shape)
    sum_out[gr0.shape[0]:] = ar1[3, 0:groups[0][0]].reshape(gr1.shape)

    left(zcopies, esends)
    for copies in (vcopies, pcopies, gcopies, ucopies, scopies, ecopies):
        left(copies, sends)
    for c in everything:
        c.wait_send()


def per_device(sizes, volume, enc_weight, coarse_weight, up_weight, dec_weight, cotangent):
    nx, ny, nz = sizes
    chans, d, h, w = volume.shape
    cd, ch = d // 2, h // 2
    owners = min(2, nx) * (ny // 2 if ny > 4 else ny)
    pers = (-(-11 // owners), -(-7 // owners))
    pair = jnp.transpose(jnp.concatenate([volume, cotangent], axis=0), (1, 2, 0, 3))
    operands = (
        pair, jnp.transpose(enc_weight, (1, 2, 0)), coarse_weight, up_weight.T, jnp.transpose(dec_weight, (0, 2, 1)))
    c2 = 2 * chans
    widest = max(owners, nx * ny // owners, nz) - 1
    scratch = [
        ((16, 16, 27), BF),
        ((27, 16, 32), BF),
        ((16, 32), BF),
        ((27, 16, 32), BF),
        ((48, 144), BF),
        ((48, 288), BF),
        ((96, 144), BF),
        ((96, 144), BF),
        ((48, 288), BF),
        ((48, 144), BF),
        ((32, 16), BF),
        ((2, d, h, chans, w), BF),
        ((d + 2, h + 2, c2, w), BF),
        ((2, d, chans, w), BF),
        ((2, 3, d + 2, chans, w), BF),
        ((d + 2, h + 2, 3, chans, 2 * w), BF),
        ((d + 2, h + 2, 3, chans, 2 * w), BF),
        ((d + 2, h + 2, chans, 2 * w), BF),
        ((d, h, chans, 2 * w), F32),
        ((d, h, chans, 2 * w), F32),
        ((cd, ch, chans, 2 * w), BF),
        ((cd, ch, chans, 2 * w), BF),
        ((cd, ch, chans, w), BF),
        ((cd + 2, ch + 2, chans, w), BF),
        ((cd + 2, ch + 2, 3, chans, w), BF),
        ((cd, ch, c2, w), BF),
        ((cd + 2, ch + 2, chans, w), BF),
        ((cd + 2, ch + 2, c2, w), BF),
        ((cd + 2, ch + 2, 3, c2, w), BF),
        ((d + 2, h + 2, 3, c2, w), BF),
        ((d + 2, h + 2, chans, 2 * w), BF),
        ((d + 2, h + 2, 3, chans, w), BF),
        ((owners * pers[0], 16, w), BF),
        ((owners * pers[1], 16, w), BF),
        ((4, widest + 1, pers[0], 16, w), BF),
        ((4, widest + 1, pers[1], 16, w), BF),
    ]
    dma = pltpu.SemaphoreType.DMA
    sems = [dma((8,))] * 2 + [dma((18,))] * 2 + [dma((8,))] * 10 + [dma((4, max(widest, 1)))] * 4 + [dma((4,))]
    hbm = pl.BlockSpec(memory_space=pl.ANY)
    vmem = pl.BlockSpec(memory_space=pltpu.VMEM)
    dec, vg, total = pl.pallas_call(
        functools.partial(kernel, sizes),
        out_shape=(
            jax.ShapeDtypeStruct((chans, d, h, w), BF),
            jax.ShapeDtypeStruct((chans, d, h, w), BF),
            jax.ShapeDtypeStruct((owners * sum(pers), 16, w), BF)),
        in_specs=[vmem] + [hbm] * 4,
        out_specs=(vmem,) * 3,
        scratch_shapes=[pltpu.VMEM(s, t) for s, t in scratch] + sems,
        compiler_params=pltpu.CompilerParams(
            collective_id=0, has_side_effects=True, vmem_limit_bytes=48 * 1024 * 1024),
    )(*operands)
    grads = ((16, 16, 27), (27, 16, 32), (16, 32), (27, 16, 32))
    dec, vg, enc, coarse, upg, decg = pl.pallas_call(
        functools.partial(finish, owners * pers[0]),
        out_shape=tuple(jax.ShapeDtypeStruct(x.shape, BF) for x in (dec, vg))
        + tuple(jax.ShapeDtypeStruct(x, F32) for x in grads),
        in_specs=[vmem] * 3,
        out_specs=(hbm,) * 6,
        scratch_shapes=[pltpu.VMEM(x, F32) for x in grads] + [dma((6,))],
        compiler_params=pltpu.CompilerParams(vmem_limit_bytes=8 * 1024 * 1024),
    )(dec, vg, total)
    return (dec, vg, jnp.transpose(enc, (2, 0, 1)), coarse, upg.T, jnp.transpose(decg, (0, 2, 1)))


def solution(mesh):
    sizes = tuple(mesh.shape[a] for a in AXES)
    spec = P(None, "gx", "gy", "gz")
    return jax.shard_map(
        functools.partial(per_device, sizes),
        mesh=mesh,
        in_specs=(spec, P(), P(), P(), P(), spec),
        out_specs=(spec, spec, P(), P(), P(), P()),
        check_vma=False,
    )
```
